256 devices in a mesh: branch: 16 (over z, core), tile: 16 (over x, y).
Axes of the slice: x: 4, y: 4, z: 8, core: 2. Of those that a mesh axis runs over, the one named last changes fastest.
Arguments:
- features: bfloat16 [16, 16, 1, 4096, 128], P('branch', 'tile'), may hold values from -6 to 6
- merge_local: bfloat16 [256, 128], replicated, may hold values from -0.375 to 0.375
- conv_local: bfloat16 [3, 3, 128, 128], replicated, may hold values from -0.1875 to 0.1875
- merge_global: bfloat16 [256, 128], replicated, may hold values from -0.375 to 0.375
- conv_global: bfloat16 [3, 3, 128, 128], replicated, may hold values from -0.1875 to 0.1875
- crop_offsets: int32 [15, 16, 1, 2], replicated, may hold values from 0 to 248, as said below
- crop_sizes: int32 [15, 16, 1, 2], replicated, may hold values from 8 to 16
- owners: int32 [15, 16, 1], replicated, may hold values from 0 to 15
Outputs:
- refined: bfloat16 [16, 16, 1, 4096, 128], P('branch', 'tile')
The draws below stay inside these ranges and needn't reach their ends.
Inputs may be any that keep to these rules, and one draw needn't show every extreme that they name: `crop_offsets`: y0 + h <= 16 and x0 + w <= 256, with (h, w) the same tile's crop_sizes.
All inputs are finite; a program needn't handle non-finite values.
Results may differ from the reference program's by a relative error of at most 0.005.
Values may be sent and summed in bfloat16 or wider, within the bound.
A program may use at most 64 MiB of HBM per device.

```python
import math
import jax
import jax.numpy as jnp
import numpy as np
from jax import lax

C = 128
S = 64
BAND_H = 16
GW = 256
IMG = 1
WIN = 16
CELLS = 4096
N_BRANCH = 16
N_TILE = 16


def crop_layout(key):
    shape = (N_BRANCH - 1, N_TILE, IMG)
    key_rows, key_cols, key_top, key_left = jax.random.split(key, 4)
    height = jax.random.randint(key_rows, shape, WIN // 2, WIN + 1, dtype=jnp.int32)
    breadth = jax.random.randint(key_cols, shape, WIN // 2, WIN + 1, dtype=jnp.int32)
    height = height.at[0, 0, 0].set(WIN)
    breadth = breadth.at[0, 0, 0].set(WIN // 2)
    top = jax.random.randint(key_top, shape, 0, BAND_H - height + 1, dtype=jnp.int32)
    left = jax.random.randint(key_left, shape, 0, GW - breadth + 1, dtype=jnp.int32)
    top = top.at[0, 0, 0].set(0)
    left = left.at[0, 0, 0].set(GW - WIN // 2)
    return (jnp.stack([top, left], axis=-1), jnp.stack([height, breadth], axis=-1))


def draw_crop_offsets(key, part):
    return crop_layout(key)[0]


def draw_crop_sizes(key, part):
    return crop_layout(key)[1]


def with_ends(values, own_key, smallest, high):
    longest = values.shape.index(max(values.shape))
    spots = []
    for shift in (0, 1):
        where = [jax.random.randint(jax.random.fold_in(own_key, axis), (), 0, length) for axis, length in enumerate(values.shape)]
        where[longest] = (where[longest] + shift) % values.shape[longest]
        spots.append(tuple(where))
    return values.at[spots[0]].set(smallest).at[spots[1]].set(high)


def block_levels(stream_key, shape, shards, low, largest):
    gain = 1.0
    for dim, shards_of in shards:
        heights = jax.random.uniform(jax.random.fold_in(jax.random.fold_in(stream_key, 6), dim), (shards_of,), jnp.float32, low / len(shards), largest / len(shards))
        gain = gain * jnp.repeat(jnp.exp(heights), shape[dim] // shards_of).reshape((-1,) + (1,) * (len(shape) - 1 - dim))
    return gain


def rank_table(count, lean):
    portions = [(1 << 20) // math.isqrt(standing ** lean) + 1 for standing in range(1, count + 1)]
    spread = 1 + sum(portions) // (1 << 30)
    return np.cumsum(np.array([max(1, weight // spread) for weight in portions]))


def ranked_ids(own_key, shape, number_of, skew):
    listing = rank_table(number_of, skew)
    ticket = jax.random.randint(jax.random.fold_in(own_key, 1), shape, 0, int(listing[number_of - 1]))
    standing = jnp.searchsorted(jnp.asarray(listing, jnp.int32), ticket, side="right")
    return jax.random.permutation(jax.random.fold_in(own_key, 2), number_of)[standing].astype(jnp.int32)


def normal_values(key, dims, scale, limit, shards=(), held_as=jnp.bfloat16):
    loudness = block_levels(key, dims, shards, -0.22, 0.18) if shards else 1.0
    drawn = jax.random.normal(key, dims, jnp.float32) * scale * loudness
    return jnp.minimum(jnp.maximum(drawn, -limit), limit).astype(held_as)


def setup_inputs(seed: int = 0) -> dict:
    keys = jax.random.split(jax.random.key(seed), 9)
    return {
        "features": normal_values(keys[0], (N_BRANCH, N_TILE, IMG, CELLS, C), 1.0, 6.0, ((0, 16), (1, 16))),
        "merge_local": normal_values(keys[1], (2 * C, C), (2 * C) ** -0.5, 0.375),
        "conv_local": normal_values(keys[2], (3, 3, C, C), (9 * C) ** -0.5, 0.1875),
        "merge_global": normal_values(keys[3], (2 * C, C), (2 * C) ** -0.5, 0.375),
        "conv_global": normal_values(keys[4], (3, 3, C, C), (9 * C) ** -0.5, 0.1875),
        "crop_offsets": draw_crop_offsets(jax.random.fold_in(keys[8], 71), 0),
        "crop_sizes": draw_crop_sizes(jax.random.fold_in(keys[8], 71), 0),
        "owners": with_ends(ranked_ids(keys[7], (N_BRANCH - 1, N_TILE, IMG), N_TILE, 2), jax.random.fold_in(keys[7], 3), 0, N_TILE - 1).astype(jnp.int32),
    }


def nearest_map(size_now, extent):
    targets = jnp.arange(WIN, dtype=jnp.int32)[:, None]
    sources = jnp.arange(extent, dtype=jnp.int32)[None, :]
    return ((sources * size_now) // extent == targets).astype(jnp.float32)


def pool_window(cells, row_size, col_size):
    row_map = nearest_map(row_size, S)
    col_map = nearest_map(col_size, S)
    colsum = jnp.einsum('vj,ijc->ivc', col_map, cells.astype(jnp.float32), precision=lax.Precision.HIGHEST)
    rowsum = jnp.einsum('ui,ivc->uvc', row_map, colsum, precision=lax.Precision.HIGHEST)
    counts = jnp.sum(row_map, axis=1)[:, None] * jnp.sum(col_map, axis=1)[None, :]
    return (rowsum / jnp.maximum(counts, 1.0)[:, :, None]).astype(jnp.bfloat16)


def crop_window(padded_band, top, left, row_size, col_size):
    root = jnp.zeros((), jnp.int32)
    sliced = lax.dynamic_slice(padded_band, (top, left, root), (WIN, WIN, padded_band.shape[2]))
    reach = jnp.arange(WIN, dtype=jnp.int32)
    inside = (reach < row_size)[:, None] & (reach < col_size)[None, :]
    return jnp.where(inside[:, :, None], sliced, jnp.zeros_like(sliced))


def upsample(crop_cells, row_size, col_size):
    row_map = nearest_map(row_size, S)
    col_map = nearest_map(col_size, S)
    rows_done = jnp.einsum('ui,uvc->ivc', row_map, crop_cells.astype(jnp.float32), precision=lax.Precision.HIGHEST)
    return jnp.einsum('vj,ivc->ijc', col_map, rows_done, precision=lax.Precision.HIGHEST).astype(jnp.bfloat16)


def convolve(padded, kernel):
    span_rows = padded.shape[1] - 2
    span_cols = padded.shape[2] - 2
    summed = jnp.zeros((padded.shape[0] * span_rows * span_cols, kernel.shape[3]), jnp.float32)
    for row_step in range(3):
        for col_step in range(3):
            sliced = padded[:, row_step:row_step + span_rows, col_step:col_step + span_cols].reshape(-1, padded.shape[3])
            summed = summed + jnp.dot(sliced, kernel[row_step, col_step], preferred_element_type=jnp.float32)
    return summed


def reference(features, merge_local, conv_local, merge_global, conv_global, crop_offsets, crop_sizes, owners):
    nlocal = N_BRANCH - 1
    bands = features[N_BRANCH - 1].reshape(N_TILE, IMG, BAND_H, GW, C)
    padded_bands = jnp.pad(bands, ((0, 0), (0, 0), (0, WIN), (0, WIN), (0, 0)))
    tile_cells = features[:nlocal].reshape(nlocal * N_TILE * IMG, S, S, C)
    corners = crop_offsets.reshape(-1, 2).astype(jnp.int32)
    extents = crop_sizes.reshape(-1, 2).astype(jnp.int32)
    owner_ids = owners.reshape(-1).astype(jnp.int32)
    image_ids = jnp.tile(jnp.arange(IMG, dtype=jnp.int32), nlocal * N_TILE)

    def visit(totals, record):
        cells, corner, extent_pair, owner_id, image_id = record
        window = pool_window(cells, extent_pair[0], extent_pair[1])
        root = jnp.zeros((), jnp.int32)
        anchor = (owner_id, image_id, corner[0], corner[1], root)
        current = lax.dynamic_slice(totals, anchor, (1, 1, WIN, WIN, C))
        totals = lax.dynamic_update_slice(totals, current + window.astype(jnp.float32)[None, None], anchor)
        band_here = padded_bands[owner_id, image_id]
        crop_cells = crop_window(band_here, corner[0], corner[1], extent_pair[0], extent_pair[1])
        upsampled = upsample(crop_cells, extent_pair[0], extent_pair[1])
        joined = jnp.concatenate([cells, upsampled], axis=-1).reshape(S * S, 2 * C)
        merging = jax.nn.relu(jnp.dot(joined, merge_local, preferred_element_type=jnp.float32)).astype(jnp.bfloat16)
        padded = jnp.pad(merging.reshape(1, S, S, C), ((0, 0), (1, 1), (1, 1), (0, 0)))
        return totals, convolve(padded, conv_local).astype(jnp.bfloat16)

    start_totals = jnp.zeros((N_TILE, IMG, BAND_H + WIN, GW + WIN, C), jnp.float32)
    totals, local_out = lax.scan(visit, start_totals, (tile_cells, corners, extents, owner_ids, image_ids))
    pooled = totals[:, :, :BAND_H, :GW].astype(jnp.bfloat16)
    global_parts = []
    for image_index in range(IMG):
        grid_cells = bands[:, image_index].reshape(N_TILE * BAND_H, GW, C)
        pooled_grid = pooled[:, image_index].reshape(N_TILE * BAND_H, GW, C)
        joined = jnp.concatenate([grid_cells, pooled_grid], axis=-1).reshape(-1, 2 * C)
        merging = jax.nn.relu(jnp.dot(joined, merge_global, preferred_element_type=jnp.float32)).astype(jnp.bfloat16)
        padded = jnp.pad(merging.reshape(1, N_TILE * BAND_H, GW, C), ((0, 0), (1, 1), (1, 1), (0, 0)))
        result = convolve(padded, conv_global).astype(jnp.bfloat16)
        global_parts.append(result.reshape(N_TILE, CELLS, C))
    global_out = jnp.stack(global_parts, axis=1)
    local_out = local_out.reshape(nlocal, N_TILE, IMG, CELLS, C)
    return jnp.concatenate([local_out, global_out[None]], axis=0)
```

```python
import functools

import jax
import jax.numpy as jnp
from jax import lax
from jax.experimental import pallas as pl
from jax.experimental.pallas import tpu as pltpu
from jax.sharding import PartitionSpec as P

MESH = pl.DeviceIdType.MESH
BF = jnp.bfloat16
F32 = jnp.float32
C = 128
S = 64
GW = 256
CELLS = 4096
HALF = 8
GROUPS = 2
GROUP = HALF // GROUPS
HOP = 3
GATHER1 = 5
GATHER2 = 12
REDUCE = 8


def band_row(q):
    return jnp.where(q < HALF, q, 3 * HALF - 1 - q)


def iota(shape, dim):
    return lax.broadcasted_iota(jnp.int32, shape, dim)


def kernel(
    n, nz, x_ref, ml_ref, cl_ref, mg_ref, cg_ref, off_ref, size_ref, own_ref, out_ref,
    win, wall, band, smat, pmat, canv, canv_in, rs1, rs1_in, rs2, rs2_in, root_b, halo, halo_out,
    crop, cu, zbuf, wlo, whi,
    bc_s, bc_s2, bc_r, a1_s, a1_r, a2_s, a2_r, cv_s, cv_r, rb_r, r1_s, r1_r, r2_s, r2_r, h_s, h_r,
):
    tiles = n * n
    ops = 2 * tiles
    br = lax.axis_index("branch")
    t = lax.axis_index("tile")
    z, c = br // 2, br % 2
    xx, yy = t // n, t % n
    up = c == 1
    f0 = jnp.where(up, xx, yy)
    g0 = jnp.where(up, yy, xx)
    pos = jnp.where(up, (z + 1) % nz, nz - 1 - z)
    z_next = jnp.where(up, (z + 1) % nz, (z + nz - 1) % nz)
    z_prev = jnp.where(up, (z + nz - 1) % nz, (z + 1) % nz)
    nxt = (2 * z_next + c, t)
    prv = (2 * z_prev + c, t)
    last = 2 * nz - 1
    is_root = br == last
    is_entry = br == last - 1
    half = 1 - c

    def tile_of(f, g):
        return jnp.where(up, f * n + g, g * n + f)

    def rc(src, dst, ss, rs, dev):
        return pltpu.make_async_remote_copy(
            src_ref=src, dst_ref=dst, send_sem=ss, recv_sem=rs, device_id=dev, device_id_type=MESH
        )

    barrier = pltpu.get_barrier_semaphore()

    def greet(dev):
        pl.semaphore_signal(barrier, inc=1, device_id=dev, device_id_type=MESH)

    greet(nxt)
    greet(prv)
    greet((2 * z + 1 - c, t))
    count = 3
    for core in (0, 1):
        for d in range(1, n):
            greet((2 * z + core, ((xx + d) % n) * n + yy))
            greet((2 * z + core, xx * n + (yy + d) % n))
            count += 2
    above = jnp.logical_and(is_root, t > 0)
    below = jnp.logical_and(is_root, t < tiles - 1)

    @pl.when(above)
    def _():
        greet((last, jnp.maximum(t - 1, 0)))

    @pl.when(below)
    def _():
        greet((last, jnp.minimum(t + 1, tiles - 1)))

    extra = jnp.where(above, 1, 0) + jnp.where(below, 1, 0)
    pl.semaphore_wait(barrier, count + extra)

    def x_row(r):
        return x_ref.at[pl.ds(pl.multiple_of(r * GW, GW), GW)]

    def root_up(k):
        return rc(x_row(k), band.at[k], bc_s.at[k], bc_r.at[k], nxt)

    def root_side(k):
        return rc(x_row(2 * HALF - 1 - k), band.at[k], bc_s2.at[k], bc_r.at[k], (last - 1, t))

    @pl.when(is_root)
    def _():
        for k in range(HALF):
            root_up(k).start()
            root_side(k).start()
        band[...] = x_ref[0 : HALF * GW].reshape(HALF, GW, C)

    slot = jnp.minimum(br, last - 1)
    top = off_ref[slot, t, 0, 0]
    hh = size_ref[slot, t, 0, 0]
    ww = size_ref[slot, t, 0, 1]

    sub = iota((256, 1), 0)
    sub_row = band_row(sub // 16) - top
    sub_col = sub % 16
    lane64 = iota((1, 128), 1)
    inside = lane64 < S
    row_hits = jnp.where(jnp.logical_and(inside, ((lane64 * hh) >> 6) == sub_row), 1.0, 0.0)
    col_hits = jnp.where(jnp.logical_and(inside, ((lane64 * ww) >> 6) == sub_col), 1.0, 0.0)
    counts = jnp.sum(row_hits, axis=1, keepdims=True) * jnp.sum(col_hits, axis=1, keepdims=True)
    wide = 1024
    lane = iota((1, wide), 1)
    cols = jnp.where((((lane % S) * ww) >> 6) == sub_col, 1.0, 0.0)

    def pool_step(step, acc):
        rows_at = ((step * (wide // S) + lane // S) * hh) >> 6
        lhs = jnp.where(rows_at == sub_row, cols, 0.0).astype(BF)
        rhs = x_ref[pl.ds(pl.multiple_of(step * wide, wide), wide)]
        return acc + jnp.dot(lhs, rhs, preferred_element_type=F32)

    pooled_win = lax.fori_loop(0, CELLS // wide, pool_step, jnp.zeros((256, C), F32))
    win[...] = (pooled_win / jnp.maximum(counts, 1.0)).astype(BF).reshape(16, 16, C)

    def gather1(d, core):
        if core == 1:
            peer = ((xx + d) % n) * n + yy
            dst = wall.at[yy, xx, c]
            src = win.at[0:HALF]
            sem = a1_r.at[xx, c]
        else:
            peer = xx * n + (yy + d) % n
            dst = wall.at[xx, yy, c]
            src = win.at[HALF : 2 * HALF]
            sem = a1_r.at[yy, c]
        return rc(src, dst, a1_s.at[core, d], sem, (2 * z + core, peer))

    for d in range(n):
        for core in (0, 1):
            if d:
                gather1(d, core).start()
            else:

                @pl.when(c != core)
                def _(d=d, core=core):
                    gather1(d, core).start()

    @pl.when(up)
    def _():
        wall[yy, xx, 1] = win[0:HALF]

    @pl.when(jnp.logical_not(up))
    def _():
        wall[xx, yy, 0] = win[HALF : 2 * HALF]

    diag = iota((16, GW), 1) - iota((16, GW), 0)
    lanes_op = iota((1, ops * 16), 1) // 16

    def select_step(i, at):
        f, rest = i // (2 * n), i % (2 * n)
        g, s = rest // 2, rest % 2
        tile = tile_of(f, g)
        b = 2 * z + s
        bb = jnp.minimum(b, last - 1)
        mine = jnp.logical_and(own_ref[bb, tile, 0] == t, b < last)
        left = jnp.where(mine, off_ref[bb, tile, 0, 1], -1024)
        smat[pl.ds(pl.multiple_of(i * 16, 16), 16)] = jnp.where(diag == left, 1.0, 0.0).astype(BF)
        return jnp.where(lanes_op == (g * n + f) * 2 + s, left, at)

    lefts = lax.fori_loop(0, ops, select_step, jnp.zeros((1, ops * 16), jnp.int32))
    lefts = lefts + iota((1, ops * 16), 1) % 16
    pmat[...] = jnp.where(iota((GW, 1), 0) == lefts, 1.0, 0.0).astype(BF)

    def conv_weights(k_ref):
        zero = jnp.zeros((C, C), BF)
        for sft in range(3):
            for r in range(2):
                rows = slice((r * 3 + sft) * C, (r * 3 + sft + 1) * C)
                for o in range(2):
                    columns = slice(o * C, (o + 1) * C)
                    tap = r - o
                    wlo[rows, columns] = k_ref[tap, sft] if tap >= 0 else zero
                    tap = r + 2 - o
                    whi[rows, columns] = k_ref[tap, sft] if tap <= 2 else zero

    def bcast_copy(k):
        return rc(band.at[k], band.at[k], bc_s.at[k], bc_r.at[k], nxt)

    def rs1_copy(grp, d):
        f = (f0 + d) % n
        return rc(
            rs1.at[grp, f], rs1_in.at[grp, f0], r1_s.at[grp, d], r1_r.at[grp, f0],
            (br, tile_of(f, g0)),
        )

    def rs1_wait(grp, d):
        f = (f0 + d) % n
        rc(
            rs1.at[grp, f], rs1_in.at[grp, f], r1_s.at[grp, d], r1_r.at[grp, f], (br, t)
        ).wait_recv()

    def rs2_copy(grp, d, s):
        g = (g0 + d) % n
        return rc(
            rs2.at[grp, g, s], rs2_in.at[half, g0, grp], r2_s.at[grp, d, s],
            r2_r.at[half, g0, grp], (2 * z + s, tile_of(f0, g)),
        )

    def gather2(d):
        g = (g0 + d) % n
        return rc(wall.at[g0], wall.at[g0], a2_s.at[d], a2_r.at[g0], (br, tile_of(f0, g)))

    def canvas_copy(k):
        return rc(canv.at[k], canv_in.at[k], cv_s.at[k], cv_r.at[k], prv)

    def entry_copy(k):
        return rc(canv.at[k], root_b.at[k], cv_s.at[k], rb_r.at[k], (last, t))

    def on_band(k):
        @pl.when(jnp.logical_not(is_root))
        def _():
            bcast_copy(k).wait_recv()

            @pl.when(pos < nz - 1)
            def _():
                bcast_copy(k).start()

        strips = jnp.dot(smat[...], band[k], preferred_element_type=F32).astype(BF)
        grp, kk = k // GROUP, k % GROUP
        rs1[grp, :, :, :, kk] = strips.reshape(n, n, 2, 16, C)

        @pl.when(kk == GROUP - 1)
        def _():
            for d in range(1, n):
                rs1_copy(grp, d).start()

    def on_rs1(grp):
        total = rs1[grp, f0]
        for d in range(1, n):
            rs1_wait(grp, d)
            total = total + rs1_in[grp, (f0 + d) % n]
        rs2[grp] = total
        for d in range(n):
            for s in (0, 1):
                if d:
                    rs2_copy(grp, d, s).start()
                else:

                    @pl.when(c != s)
                    def _(d=d, s=s):
                        rs2_copy(grp, d, s).start()

        rs2_in[half, g0, grp] = rs2[grp, g0, c]

    def on_gather1():
        for d in range(n):
            f = (f0 + d) % n
            for s in (0, 1):

                def wait(f=f, s=s):
                    rc(
                        win.at[0:HALF], wall.at[g0, f, s], a1_s.at[0, 0], a1_r.at[f, s], (br, t)
                    ).wait_recv()

                if d:
                    wait()
                else:
                    pl.when(c != s)(wait)
        for d in range(1, n):
            gather2(d).start()

    def on_gather2():
        for d in range(1, n):
            g = (g0 + d) % n
            rc(wall.at[g], wall.at[g], a2_s.at[d], a2_r.at[g], (br, t)).wait_recv()

    def on_canvas(k):
        w = wall[:, :, :, pl.ds(k, 1)].reshape(ops * 16, C)
        part = jnp.dot(pmat[...], w, preferred_element_type=F32)
        canv[k] = part.astype(BF)

        @pl.when(pos < nz - 1)
        def _():
            canvas_copy(k).wait_recv()
            canv[k] = (part + canv_in[k].astype(F32)).astype(BF)

        @pl.when(pos > 0)
        def _():
            canvas_copy(k).start()

        @pl.when(is_entry)
        def _():
            entry_copy(k).start()

    def event(cond, fun, *args):
        pl.when(cond)(lambda: fun(*args))

    def tick(tau, carry):
        k = tau - pos * HOP
        event(jnp.logical_and(k >= 0, k < HALF), on_band, jnp.clip(k, 0, HALF - 1))
        event(tau == GATHER1, on_gather1)
        event(tau == GATHER2, on_gather2)
        k = tau - (GATHER2 + (nz - 1 - pos) * HOP)
        event(jnp.logical_and(k >= 0, k < HALF), on_canvas, jnp.clip(k, 0, HALF - 1))
        for grp in range(GROUPS):
            event(tau == pos * HOP + grp * GROUP + GROUP - 1 + REDUCE, on_rs1, grp)
        return carry

    span = max(GATHER2, REDUCE) + (nz - 1) * HOP + HALF
    lax.fori_loop(0, span, tick, 0)

    def put(rows, lanes, value, width):
        m = value.reshape(-1, width, C)
        at = iota((1, width, 1), 1)
        before = jnp.where(at == 0, 0.0, pltpu.roll(m, 1, 1))
        after = jnp.where(at == width - 1, 0.0, pltpu.roll(m, width - 1, 1))
        for sft, v in enumerate((before, m, after)):
            zbuf[rows, lanes + sft * C : lanes + (sft + 1) * C] = v.reshape(-1, C).astype(BF)

    def conv_block(first, hi_first):
        lo = zbuf[pl.ds(first, 256)]
        hi = zbuf[pl.ds(hi_first, 256)]
        res = jnp.dot(lo, wlo[...], preferred_element_type=F32)
        res = res + jnp.dot(hi, whi[...], preferred_element_type=F32)
        return res.astype(BF)

    @pl.when(jnp.logical_not(is_root))
    def _():
        conv_weights(cl_ref)
        for hf in (0, 1):
            for g in range(n):
                for grp in range(GROUPS):

                    def wait(hf=hf, g=g, grp=grp):
                        rc(
                            rs2.at[grp, g, 0], rs2_in.at[hf, g, grp], r2_s.at[grp, 0, 0],
                            r2_r.at[hf, g, grp], (br, t),
                        ).wait_recv()

                    pl.when(jnp.logical_or(half != hf, g0 != g))(wait)
            total = rs2_in[hf, 0]
            for g in range(1, n):
                total = total + rs2_in[hf, g]
            crop[hf * HALF * 16 : (hf + 1) * HALF * 16] = total.reshape(HALF * 16, C)
        s1024 = iota((1024, 1), 0)
        target = band_row(s1024 // S) * 16 + (((s1024 % S) * ww) >> 6)
        lhs = jnp.where(iota((1, 256), 1) == target, 1.0, 0.0).astype(BF)
        cu[...] = jnp.dot(lhs, crop[...], preferred_element_type=F32).astype(BF).reshape(16, S, C)
        zbuf[0:S, 0 : 3 * C] = jnp.zeros((S, 3 * C), BF)
        zbuf[S // 2 * S : (S // 2 + 1) * S, 3 * C :] = jnp.zeros((S, 3 * C), BF)
        weight = ml_ref[...]

        def merge_block(b, carry):
            ups = []
            for i in range(8):
                r = (((b * 8 + i) * hh) >> 6) + top
                ups.append(cu[jnp.clip(r, 0, 15)])
            first = pl.multiple_of(b * 8 * S, 8 * S)
            both = jnp.concatenate(
                [x_ref[pl.ds(first, 8 * S)], jnp.concatenate(ups, axis=0)], axis=1
            )
            m = jnp.maximum(jnp.dot(both, weight, preferred_element_type=F32), 0.0)
            for i in range(8):
                pair = b * 4 + (i + 1) // 2
                rows = pl.ds(pl.multiple_of(pair * S, S), S)
                put(rows, 3 * C * ((i + 1) % 2), m[i * S : (i + 1) * S], S)
            return carry

        lax.fori_loop(0, S // 8, merge_block, 0)

        def conv_step(b, carry):
            first = pl.multiple_of(b * 256, 256)
            res = conv_block(first, pl.multiple_of(b * 256 + S, S))
            for i in range(4):
                for o in range(2):
                    at = pl.ds(pl.multiple_of(b * 512 + (2 * i + o) * S, S), S)
                    out_ref[at] = res[i * S : (i + 1) * S, o * C : (o + 1) * C]
            return carry

        lax.fori_loop(0, S // 8, conv_step, 0)

    def halo_copy(to_below):
        if to_below:
            peer = jnp.minimum(t + 1, tiles - 1)
            return rc(halo_out.at[1], halo.at[0], h_s.at[1], h_r.at[0], (last, peer))
        peer = jnp.maximum(t - 1, 0)
        return rc(halo_out.at[0], halo.at[1], h_s.at[0], h_r.at[1], (last, peer))

    def halo_wait(side):
        rc(halo_out.at[side], halo.at[side], h_s.at[side], h_r.at[side], (last, t)).wait_recv()

    @pl.when(is_root)
    def _():
        conv_weights(cg_ref)
        weight = mg_ref[...]

        def merge_row(r, pooled):
            both = jnp.concatenate([x_ref[r * GW : (r + 1) * GW], pooled], axis=1)
            m = jnp.maximum(jnp.dot(both, weight, preferred_element_type=F32), 0.0)
            pair = (r + 1) // 2
            put(slice(pair * GW, (pair + 1) * GW), 3 * C * ((r + 1) % 2), m, GW)
            return m

        def wait_entry(k):
            rc(canv.at[k], root_b.at[k], cv_s.at[k], rb_r.at[k], (last, t)).wait_recv()

        for k in range(HALF):
            m = merge_row(k, canv[k])
            if k == 0:
                halo_out[0] = m.astype(BF)
                pl.when(above)(lambda: halo_copy(False).start())
            wait_entry(k)
            m = merge_row(15 - k, root_b[k])
            if k == 0:
                halo_out[1] = m.astype(BF)
                pl.when(below)(lambda: halo_copy(True).start())

        zero = jnp.zeros((GW, 3 * C), BF)
        zbuf[0:GW, 0 : 3 * C] = zero
        zbuf[8 * GW : 9 * GW, 3 * C :] = zero

        @pl.when(above)
        def _():
            halo_wait(0)
            put(slice(0, GW), 0, halo[0].astype(F32), GW)

        @pl.when(below)
        def _():
            halo_wait(1)
            put(slice(8 * GW, 9 * GW), 3 * C, halo[1].astype(F32), GW)

        for q in range(8):
            res = conv_block(q * GW, (q + 1) * GW)
            for o in range(2):
                out_ref[(2 * q + o) * GW : (2 * q + o + 1) * GW] = res[:, o * C : (o + 1) * C]

    @pl.when(is_root)
    def _():
        for k in range(HALF):
            root_up(k).wait_send()
            root_side(k).wait_send()

    @pl.when(jnp.logical_and(jnp.logical_not(is_root), pos < nz - 1))
    def _():
        for k in range(HALF):
            bcast_copy(k).wait_send()

    for d in range(n):
        for core in (0, 1):

            def wait(d=d, core=core):
                gather1(d, core).wait_send()
                for grp in range(GROUPS):
                    rs2_copy(grp, d, core).wait_send()

            if d:
                wait()
            else:
                pl.when(c != core)(wait)
    for d in range(1, n):
        gather2(d).wait_send()
        for grp in range(GROUPS):
            rs1_copy(grp, d).wait_send()

    @pl.when(pos > 0)
    def _():
        for k in range(HALF):
            canvas_copy(k).wait_send()

    @pl.when(is_entry)
    def _():
        for k in range(HALF):
            entry_copy(k).wait_send()

    @pl.when(is_root)
    def _():
        for hf in (0, 1):
            for g in range(n):
                for grp in range(GROUPS):

                    def wait(hf=hf, g=g, grp=grp):
                        rc(
                            rs2.at[grp, g, 0], rs2_in.at[hf, g, grp], r2_s.at[grp, 0, 0],
                            r2_r.at[hf, g, grp], (br, t),
                        ).wait_recv()

                    pl.when(jnp.logical_or(half != hf, g0 != g))(wait)
        pl.when(above)(lambda: halo_copy(False).wait_send())
        pl.when(below)(lambda: halo_copy(True).wait_send())


def run(n, nz, features, merge_local, conv_local, merge_global, conv_global, offsets, sizes, owners):
    vm = functools.partial(pl.BlockSpec, memory_space=pltpu.VMEM)
    sm = functools.partial(pl.BlockSpec, memory_space=pltpu.SMEM)
    ops = 2 * n * n
    dma = pltpu.SemaphoreType.DMA
    out = pl.pallas_call(
        functools.partial(kernel, n, nz),
        out_shape=jax.ShapeDtypeStruct((CELLS, C), BF),
        in_specs=[vm()] * 5 + [sm()] * 3,
        out_specs=vm(),
        scratch_shapes=[
            pltpu.VMEM((16, 16, C), BF),
            pltpu.VMEM((n, n, 2, HALF, 16, C), BF),
            pltpu.VMEM((HALF, GW, C), BF),
            pltpu.VMEM((ops * 16, GW), BF),
            pltpu.VMEM((GW, ops * 16), BF),
            pltpu.VMEM((HALF, GW, C), BF),
            pltpu.VMEM((HALF, GW, C), BF),
            pltpu.VMEM((GROUPS, n, n, 2, GROUP, 16, C), BF),
            pltpu.VMEM((GROUPS, n, n, 2, GROUP, 16, C), BF),
            pltpu.VMEM((GROUPS, n, 2, GROUP, 16, C), BF),
            pltpu.VMEM((2, n, GROUPS, GROUP, 16, C), BF),
            pltpu.VMEM((HALF, GW, C), BF),
            pltpu.VMEM((2, GW, C), BF),
            pltpu.VMEM((2, GW, C), BF),
            pltpu.VMEM((256, C), BF),
            pltpu.VMEM((16, S, C), BF),
            pltpu.VMEM((9 * GW, 6 * C), BF),
            pltpu.VMEM((6 * C, 2 * C), BF),
            pltpu.VMEM((6 * C, 2 * C), BF),
            dma((HALF,)),
            dma((HALF,)),
            dma((HALF,)),
            dma((2, n)),
            dma((n, 2)),
            dma((n,)),
            dma((n,)),
            dma((HALF,)),
            dma((HALF,)),
            dma((HALF,)),
            dma((GROUPS, n)),
            dma((GROUPS, n)),
            dma((GROUPS, n, 2)),
            dma((2, n, GROUPS)),
            dma((2,)),
            dma((2,)),
        ],
        compiler_params=pltpu.CompilerParams(
            collective_id=0, has_side_effects=True, vmem_limit_bytes=48 * 1024 * 1024
        ),
        name="glue",
    )(
        features.reshape(CELLS, C), merge_local, conv_local, merge_global, conv_global,
        offsets, sizes, owners,
    )
    return out.reshape(features.shape)


def solution(mesh):
    nz = mesh.shape["branch"] // 2
    n = 1
    while n * n < mesh.shape["tile"]:
        n += 1
    in_specs = (P("branch", "tile", None, None, None), P(), P(), P(), P(), P(), P(), P())
    out_specs = P("branch", "tile", None, None, None)
    return jax.shard_map(
        functools.partial(run, n, nz),
        mesh=mesh,
        in_specs=in_specs,
        out_specs=out_specs,
        check_vma=False,
    )
```

```python
import functools

import jax
import jax.numpy as jnp
from jax import lax
from jax.experimental import pallas as pl
from jax.experimental.pallas import tpu as pltpu
from jax.sharding import PartitionSpec as P

MESH = pl.DeviceIdType.MESH
BF = jnp.bfloat16
F32 = jnp.float32
C = 128
S = 64
GW = 256
WIN = 16
CELLS = 4096
ROWS = 16
SLOTS = 15


def iota(shape, dim):
    return lax.broadcasted_iota(jnp.int32, shape, dim)


def kernel(
    n, x_hbm, ml_hbm, cl_hbm, mg_hbm, cg_hbm, off_hbm, size_hbm, own_hbm, out_ref,
    x_ref, ml_ref, mg_ref, conv_ref, off_ref, size_ref, own_ref,
    win, wall, grow, smat, pmat, rs1, rs1_in, rs2, rs2_in, rs3, crop, rows, mine, cu, zbuf, wlo, whi,
    in_s, gr_s, gr_r, zw_s, zw_r, a1_s, a1_r, a2_s, a2_r, r1_s, r1_r, r2_s, r2_r, zc_s, zc_r, m_s, m_r,
):
    tiles = n * n
    br = lax.axis_index("branch")
    t = lax.axis_index("tile")
    up = br % 2 == 1
    xx, yy = t // n, t % n
    f0 = jnp.where(up, xx, yy)
    g0 = jnp.where(up, yy, xx)
    last = ROWS - 1
    is_root = br == last
    is_local = br < last

    def tile_of(f, g):
        return jnp.where(up, f * n + g, g * n + f)

    def rc(src, dst, ss, rs, dev):
        return pltpu.make_async_remote_copy(
            src_ref=src, dst_ref=dst, send_sem=ss, recv_sem=rs, device_id=dev, device_id_type=MESH
        )

    barrier = pltpu.get_barrier_semaphore()

    def greet(b, tile):
        pl.semaphore_signal(barrier, inc=1, device_id=(b, tile), device_id_type=MESH)

    for d in range(1, ROWS):
        greet((br + d) % ROWS, t)
    for d in range(1, n):
        greet(br, ((xx + d) % n) * n + yy)
        greet(br, xx * n + (yy + d) % n)
    before = jnp.maximum(t - 1, 0)
    after = jnp.minimum(t + 1, tiles - 1)
    has_before, has_after = t > 0, t < tiles - 1
    is_first = br == 0
    first_up = jnp.logical_and(is_first, has_before)
    root_up = jnp.logical_and(is_root, has_before)
    root_down = jnp.logical_and(is_root, has_after)

    @pl.when(first_up)
    def _():
        greet(last, before)

    @pl.when(root_up)
    def _():
        greet(last, before)

    @pl.when(root_down)
    def _():
        greet(0, after)
        greet(last, after)

    def fetch(i, src, dst):
        return pltpu.make_async_copy(src, dst, in_s.at[i])

    fetches = [
        fetch(0, size_hbm, size_ref),
        fetch(1, off_hbm, off_ref),
        fetch(2, own_hbm, own_ref),
        fetch(3, x_hbm, x_ref),
        fetch(4, mg_hbm, mg_ref),
        fetch(5, ml_hbm, ml_ref),
    ]
    for f in fetches:
        f.start()
    pl.when(is_root)(lambda: fetch(6, cg_hbm, conv_ref).start())
    pl.when(is_local)(lambda: fetch(6, cl_hbm, conv_ref).start())
    for f in fetches[:4]:
        f.wait()

    slot = jnp.minimum(br, last - 1)
    top = off_ref[slot, 0, t]
    hh = size_ref[slot, 0, t]
    ww = size_ref[slot, 1, t]

    @pl.when(is_local)
    def _():
        sub = iota((256, 1), 0)
        sub_row = sub // WIN - top
        sub_col = sub % WIN
        lane64 = iota((1, 128), 1)
        inside = lane64 < S
        row_hits = jnp.where(jnp.logical_and(inside, ((lane64 * hh) >> 6) == sub_row), 1.0, 0.0)
        col_hits = jnp.where(jnp.logical_and(inside, ((lane64 * ww) >> 6) == sub_col), 1.0, 0.0)
        counts = jnp.sum(row_hits, axis=1, keepdims=True) * jnp.sum(col_hits, axis=1, keepdims=True)
        wide = 1024
        lane = iota((1, wide), 1)
        cols = jnp.where((((lane % S) * ww) >> 6) == sub_col, 1.0, 0.0)

        def pool_step(step, acc):
            rows_at = ((step * (wide // S) + lane // S) * hh) >> 6
            lhs = jnp.where(rows_at == sub_row, cols, 0.0).astype(BF)
            rhs = x_ref[pl.ds(pl.multiple_of(step * wide, wide), wide)]
            return acc + jnp.dot(lhs, rhs, preferred_element_type=F32)

        total = lax.fori_loop(0, CELLS // wide, pool_step, jnp.zeros((256, C), F32))
        win[...] = (total / jnp.maximum(counts, 1.0)).astype(BF).reshape(ROWS, WIN, C)

    count = ROWS - 1 + 2 * (n - 1)
    extra = jnp.where(first_up, 1, 0) + jnp.where(root_up, 1, 0) + jnp.where(root_down, 2, 0)
    pl.semaphore_wait(barrier, count + extra)

    def row_copy(r):
        return rc(x_ref.at[r * GW : (r + 1) * GW], grow, gr_s.at[r], gr_r.at[0], (r, t))

    far_first = (6, 7, 4, 8, 5, 9, 2, 10, 3, 11, 0, 12, 1, 13, 14)

    @pl.when(is_root)
    def _():
        for r in far_first:
            row_copy(r).start()
        grow[...] = x_ref[last * GW : (last + 1) * GW]

    def window_copy(d):
        r = (br + d) % ROWS
        odd = r % 2 == 1
        g, f = jnp.where(odd, yy, xx), jnp.where(odd, xx, yy)
        return rc(win.at[r], wall.at[g, f, br], zw_s.at[d], zw_r.at[br], (r, t))

    @pl.when(is_local)
    def _():
        for d in range(1, ROWS):
            window_copy(d).start()
        wall[g0, f0, slot] = win[br]

    diag = iota((WIN, GW), 1) - iota((WIN, GW), 0)

    def left_of(s, tile):
        return jnp.where(own_ref[s, 0, tile] == t, off_ref[s, 1, tile], -1024)

    def strip_step(i, carry):
        tile = tile_of(i // n, i % n)
        for s in range(SLOTS):
            at = pl.ds(pl.multiple_of((i * SLOTS + s) * WIN, WIN), WIN)
            smat[at] = jnp.where(diag == left_of(s, tile), 1.0, 0.0).astype(BF)
        return carry

    lax.fori_loop(0, tiles, strip_step, 0)

    piece = iota((1, GW), 1) // WIN
    place = iota((1, GW), 1) % WIN
    column = iota((GW, 1), 0)

    def place_step(i, carry):
        tile = tile_of(i % n, i // n)
        lefts = jnp.full((1, GW), -1024, jnp.int32)
        for s in range(SLOTS):
            lefts = jnp.where(piece == s, left_of(s, tile), lefts)
        pmat[i] = jnp.where(column == lefts + place, 1.0, 0.0).astype(BF)
        return carry

    def gather1(d):
        dev = (br, tile_of((f0 + d) % n, g0))
        own = wall.at[g0, f0, 0:SLOTS]
        return rc(own, own, a1_s.at[d], a1_r.at[f0], dev)

    def gather1_wait(d):
        f = (f0 + d) % n
        part = wall.at[g0, f, 0:SLOTS]
        rc(part, part, a1_s.at[d], a1_r.at[f], (br, t)).wait_recv()

    def gather2(d):
        dev = (br, tile_of(f0, (g0 + d) % n))
        own = wall.at[g0, :, 0:SLOTS]
        return rc(own, own, a2_s.at[d], a2_r.at[g0], dev)

    def gather2_wait(d):
        g = (g0 + d) % n
        part = wall.at[g, :, 0:SLOTS]
        rc(part, part, a2_s.at[d], a2_r.at[g], (br, t)).wait_recv()

    for s in range(SLOTS):

        @pl.when(br != s)
        def _(s=s):
            part = wall.at[g0, f0, s]
            rc(win.at[s], part, zw_s.at[s], zw_r.at[s], (br, t)).wait_recv()

    for d in range(1, n):
        gather1(d).start()

    @pl.when(is_local)
    def _():
        rc(grow, grow, gr_s.at[0], gr_r.at[0], (br, t)).wait_recv()

    def scatter1(d):
        f = (f0 + d) % n
        return rc(rs1.at[f], rs1_in.at[f0], r1_s.at[d], r1_r.at[f0], (br, tile_of(f, g0)))

    def scatter1_wait(d):
        f = (f0 + d) % n
        rc(rs1.at[f], rs1_in.at[f], r1_s.at[d], r1_r.at[f], (br, t)).wait_recv()

    block = n * SLOTS * WIN
    for d in [*range(1, n), 0]:
        f = (f0 + d) % n
        at = pl.ds(pl.multiple_of(f * block, WIN), block)
        strips = jnp.dot(smat[at], grow[...], preferred_element_type=F32).astype(BF)
        rs1[f] = strips.reshape(n, SLOTS, WIN, C)
        if d:
            scatter1(d).start()

    lax.fori_loop(0, tiles, place_step, 0)
    for i in range(n):
        for j in range(n):
            wall[i, j, SLOTS] = jnp.zeros((WIN, C), BF)

    for d in range(1, n):
        gather1_wait(d)
    for d in range(1, n):
        gather2(d).start()

    fetches[4].wait()
    fetches[5].wait()
    fetch(6, cl_hbm, conv_ref).wait()
    zero = jnp.zeros((C, C), BF)
    for sft in range(3):
        for r in range(2):
            at = slice((r * 3 + sft) * C, (r * 3 + sft + 1) * C)
            for o in range(2):
                to = slice(o * C, (o + 1) * C)
                tap = r - o
                wlo[at, to] = conv_ref[tap, sft] if tap >= 0 else zero
                tap = r + 2 - o
                whi[at, to] = conv_ref[tap, sft] if tap <= 2 else zero

    def scatter2(d):
        g = (g0 + d) % n
        return rc(rs2.at[g], rs2_in.at[g0], r2_s.at[d], r2_r.at[g0], (br, tile_of(f0, g)))

    def scatter2_wait(d):
        g = (g0 + d) % n
        rc(rs2.at[g], rs2_in.at[g], r2_s.at[d], r2_r.at[g], (br, t)).wait_recv()

    for d in range(1, n):
        scatter1_wait(d)
    for d in [*range(1, n), 0]:
        g = (g0 + d) % n
        total = rs1[f0, g]
        for e in range(1, n):
            total = total + rs1_in[(f0 + e) % n, g]
        rs2[g] = total
        if d:
            scatter2(d).start()

    def merged_copy():
        return rc(mine, rows.at[br + 1], m_s.at[0], m_r.at[br + 1], (last, t))

    def edge_up():
        return rc(mine, rows.at[ROWS + 1], m_s.at[1], m_r.at[ROWS + 1], (last, before))

    def edge_down():
        return rc(mine, rows.at[0], m_s.at[1], m_r.at[0], (last, after))

    for d in range(1, n):
        gather2_wait(d)
    pooled = jnp.zeros((GW, C), F32)
    for i in range(n):
        for j in range(n):
            w = wall[i, j].reshape(GW, C)
            pooled = pooled + jnp.dot(pmat[i * n + j], w, preferred_element_type=F32)
    both = jnp.concatenate([grow[...], pooled.astype(BF)], axis=1)
    merged = jnp.maximum(jnp.dot(both, mg_ref[...], preferred_element_type=F32), 0.0)
    mine[...] = merged.astype(BF)
    pl.when(is_local)(lambda: merged_copy().start())
    pl.when(first_up)(lambda: edge_up().start())
    pl.when(root_down)(lambda: edge_down().start())

    def crop_copy(d):
        b = (br + d) % ROWS
        return rc(rs3.at[b], crop.at[br], zc_s.at[d], zc_r.at[br], (b, t))

    for d in range(1, n):
        scatter2_wait(d)
    total = rs2[g0]
    for d in range(1, n):
        total = total + rs2_in[(g0 + d) % n]
    rs3[0:SLOTS] = total
    for d in range(1, ROWS):

        @pl.when((br + d) % ROWS != last)
        def _(d=d):
            crop_copy(d).start()

    def put(at, lanes, value, width):
        m = value.reshape(-1, width, C)
        col = iota((1, width, 1), 1)
        left = jnp.where(col == 0, 0.0, pltpu.roll(m, 1, 1))
        right = jnp.where(col == width - 1, 0.0, pltpu.roll(m, width - 1, 1))
        for sft, v in enumerate((left, m, right)):
            zbuf[at, lanes + sft * C : lanes + (sft + 1) * C] = v.reshape(-1, C).astype(BF)

    def conv_block(first, hi_first):
        lo = zbuf[pl.ds(first, 256)]
        hi = zbuf[pl.ds(hi_first, 256)]
        res = jnp.dot(lo, wlo[...], preferred_element_type=F32)
        res = res + jnp.dot(hi, whi[...], preferred_element_type=F32)
        return res.astype(BF)

    @pl.when(is_local)
    def _():
        zbuf[0:S, 0 : 3 * C] = jnp.zeros((S, 3 * C), BF)
        zbuf[S // 2 * S : (S // 2 + 1) * S, 3 * C :] = jnp.zeros((S, 3 * C), BF)
        s1024 = iota((1024, 1), 0)
        target = (s1024 // S) * WIN + (((s1024 % S) * ww) >> 6)
        lhs = jnp.where(iota((1, 256), 1) == target, 1.0, 0.0).astype(BF)
        weight = ml_ref[...]
        crop[br] = rs3[slot]
        for r in range(ROWS):

            @pl.when(br != r)
            def _(r=r):
                rc(rs3.at[0], crop.at[r], zc_s.at[r], zc_r.at[r], (br, t)).wait_recv()

        strips = crop[...].reshape(ROWS * WIN, C)
        cu[...] = jnp.dot(lhs, strips, preferred_element_type=F32).astype(BF).reshape(ROWS, S, C)

        def merge_block(b, carry):
            ups = []
            for i in range(8):
                r = (((b * 8 + i) * hh) >> 6) + top
                ups.append(cu[jnp.clip(r, 0, ROWS - 1)])
            first = pl.multiple_of(b * 8 * S, 8 * S)
            both = jnp.concatenate(
                [x_ref[pl.ds(first, 8 * S)], jnp.concatenate(ups, axis=0)], axis=1
            )
            m = jnp.maximum(jnp.dot(both, weight, preferred_element_type=F32), 0.0)
            for i in range(8):
                pair = b * 4 + (i + 1) // 2
                at = pl.ds(pl.multiple_of(pair * S, S), S)
                put(at, 3 * C * ((i + 1) % 2), m[i * S : (i + 1) * S], S)
            return carry

        lax.fori_loop(0, S // 8, merge_block, 0)

        def conv_step(b, carry):
            first = pl.multiple_of(b * 256, 256)
            res = conv_block(first, pl.multiple_of(b * 256 + S, S))
            for i in range(4):
                for o in range(2):
                    at = pl.ds(pl.multiple_of(b * 512 + (2 * i + o) * S, S), S)
                    out_ref[at] = res[i * S : (i + 1) * S, o * C : (o + 1) * C]
            return carry

        lax.fori_loop(0, S // 8, conv_step, 0)

    @pl.when(is_root)
    def _():
        rows[ROWS] = mine[...]

        @pl.when(jnp.logical_not(has_before))
        def _():
            rows[0] = jnp.zeros((GW, C), BF)

        @pl.when(jnp.logical_not(has_after))
        def _():
            rows[ROWS + 1] = jnp.zeros((GW, C), BF)

        def wait(i):
            rc(mine, rows.at[i], m_s.at[0], m_r.at[i], (br, t)).wait_recv()

        here = set()
        done = set()
        for i in (16, 15, 1, 2, 13, 14, 3, 4, 11, 12, 5, 6, 9, 10, 0, 17, 7, 8):
            if i == 0:
                pl.when(has_before)(functools.partial(wait, 0))
            elif i == ROWS + 1:
                pl.when(has_after)(functools.partial(wait, ROWS + 1))
            elif i != ROWS:
                wait(i)
            put(slice(i // 2 * GW, (i // 2 + 1) * GW), 3 * C * (i % 2), rows[i].astype(F32), GW)
            here.add(i)
            for q in range(8):
                if q not in done and here >= {2 * q, 2 * q + 1, 2 * q + 2, 2 * q + 3}:
                    done.add(q)
                    res = conv_block(q * GW, (q + 1) * GW)
                    for o in range(2):
                        at = slice((2 * q + o) * GW, (2 * q + o + 1) * GW)
                        out_ref[at] = res[:, o * C : (o + 1) * C]

    @pl.when(is_root)
    def _():
        for r in far_first:
            row_copy(r).wait_send()

    @pl.when(is_local)
    def _():
        for d in range(1, ROWS):
            window_copy(d).wait_send()
        merged_copy().wait_send()

    for d in range(1, n):
        gather1(d).wait_send()
        gather2(d).wait_send()
        scatter1(d).wait_send()
        scatter2(d).wait_send()
    for d in range(1, ROWS):

        @pl.when((br + d) % ROWS != last)
        def _(d=d):
            crop_copy(d).wait_send()

    pl.when(first_up)(lambda: edge_up().wait_send())
    pl.when(root_down)(lambda: edge_down().wait_send())


def run(n, features, merge_local, conv_local, merge_global, conv_global, offsets, sizes, owners):
    hbm = pl.BlockSpec(memory_space=pltpu.HBM)
    dma = pltpu.SemaphoreType.DMA

    def vm(*shape):
        return pltpu.VMEM(shape, BF)

    def sm(*shape):
        return pltpu.SMEM(shape, jnp.int32)

    tiles = n * n
    out = pl.pallas_call(
        functools.partial(kernel, n),
        out_shape=jax.ShapeDtypeStruct((CELLS, C), BF),
        in_specs=[hbm] * 8,
        out_specs=pl.BlockSpec(memory_space=pltpu.VMEM),
        scratch_shapes=[
            vm(CELLS, C),
            vm(2 * C, C),
            vm(2 * C, C),
            vm(3, 3, C, C),
            sm(SLOTS, 2, tiles),
            sm(SLOTS, 2, tiles),
            sm(SLOTS, 1, tiles),
            vm(ROWS, WIN, C),
            vm(n, n, ROWS, WIN, C),
            vm(GW, C),
            vm(tiles * SLOTS * WIN, GW),
            vm(tiles, GW, GW),
            vm(n, n, SLOTS, WIN, C),
            vm(n, n, SLOTS, WIN, C),
            vm(n, SLOTS, WIN, C),
            vm(n, SLOTS, WIN, C),
            vm(ROWS, WIN, C),
            vm(ROWS, WIN, C),
            vm(ROWS + 2, GW, C),
            vm(GW, C),
            vm(ROWS, S, C),
            vm(9 * GW, 6 * C),
            vm(6 * C, 2 * C),
            vm(6 * C, 2 * C),
            dma((7,)),
            dma((ROWS,)),
            dma((1,)),
            dma((ROWS,)),
            dma((ROWS,)),
            dma((n,)),
            dma((n,)),
            dma((n,)),
            dma((n,)),
            dma((n,)),
            dma((n,)),
            dma((n,)),
            dma((n,)),
            dma((ROWS,)),
            dma((ROWS,)),
            dma((2,)),
            dma((ROWS + 2,)),
        ],
        compiler_params=pltpu.CompilerParams(
            collective_id=0, has_side_effects=True, vmem_limit_bytes=58 * 1024 * 1024
        ),
        name="glue",
    )(
        features.reshape(CELLS, C), merge_local, conv_local, merge_global, conv_global,
        offsets.transpose(0, 2, 3, 1).reshape(SLOTS, 2, tiles),
        sizes.transpose(0, 2, 3, 1).reshape(SLOTS, 2, tiles),
        owners.transpose(0, 2, 1),
    )
    return out.reshape(features.shape)


def solution(mesh):
    n = 1
    while n * n < mesh.shape["tile"]:
        n += 1
    in_specs = (P("branch", "tile", None, None, None), P(), P(), P(), P(), P(), P(), P())
    out_specs = P("branch", "tile", None, None, None)
    return jax.shard_map(
        functools.partial(run, n),
        mesh=mesh,
        in_specs=in_specs,
        out_specs=out_specs,
        check_vma=False,
    )
```

```python
import functools

import jax
import jax.numpy as jnp
from jax import lax
from jax.experimental import pallas as pl
from jax.experimental.pallas import tpu as pltpu
from jax.sharding import PartitionSpec as P

MESH = pl.DeviceIdType.MESH
BF = jnp.bfloat16
F32 = jnp.float32
C = 128
S = 64
GW = 256
WIN = 16
CELLS = 4096
ROWS = 16
SLOTS = 15


def iota(shape, dim):
    return lax.broadcasted_iota(jnp.int32, shape, dim)


def kernel(
    n, x_hbm, ml_hbm, cl_hbm, mg_hbm, cg_hbm, off_hbm, size_hbm, own_hbm, out_ref,
    x_ref, ml_ref, mg_ref, conv_ref, off_ref, size_ref, own_ref,
    win, wall, bands, smat, pmat, strip, strip_in, canv, canv_in, total_strip, crop, rows, mine, cu, zbuf, wlo, whi,
    in_s, gr_s, gr_r, zw_s, zw_r, a1_s, a1_r, a2_s, a2_r, r1_s, r1_r, r2_s, r2_r, zc_s, zc_r, m_s, m_r,
):
    tiles = n * n
    br = lax.axis_index("branch")
    t = lax.axis_index("tile")
    up = br % 2 == 1
    xx, yy = t // n, t % n
    f0 = jnp.where(up, xx, yy)
    g0 = jnp.where(up, yy, xx)
    last = ROWS - 1
    is_root = br == last
    is_local = br < last

    def tile_of(f, g):
        return jnp.where(up, f * n + g, g * n + f)

    def rc(src, dst, ss, rs, dev):
        return pltpu.make_async_remote_copy(
            src_ref=src, dst_ref=dst, send_sem=ss, recv_sem=rs, device_id=dev, device_id_type=MESH
        )

    barrier = pltpu.get_barrier_semaphore()

    def greet(b, tile):
        pl.semaphore_signal(barrier, inc=1, device_id=(b, tile), device_id_type=MESH)

    for d in range(1, ROWS):
        greet((br + d) % ROWS, t)
    for d in range(1, n):
        greet(br, ((xx + d) % n) * n + yy)
        greet(br, xx * n + (yy + d) % n)
    before = jnp.maximum(t - 1, 0)
    after = jnp.minimum(t + 1, tiles - 1)
    has_before, has_after = t > 0, t < tiles - 1
    is_first = br == 0
    first_up = jnp.logical_and(is_first, has_before)
    root_up = jnp.logical_and(is_root, has_before)
    root_down = jnp.logical_and(is_root, has_after)

    @pl.when(first_up)
    def _():
        greet(last, before)

    @pl.when(root_up)
    def _():
        greet(last, before)

    @pl.when(root_down)
    def _():
        greet(0, after)
        greet(last, after)

    def fetch(i, src, dst):
        return pltpu.make_async_copy(src, dst, in_s.at[i])

    fetches = [
        fetch(0, size_hbm, size_ref),
        fetch(1, off_hbm, off_ref),
        fetch(2, own_hbm, own_ref),
        fetch(3, x_hbm, x_ref),
        fetch(4, mg_hbm, mg_ref),
        fetch(5, ml_hbm, ml_ref),
    ]
    for f in fetches:
        f.start()
    pl.when(is_root)(lambda: fetch(6, cg_hbm, conv_ref).start())
    pl.when(is_local)(lambda: fetch(6, cl_hbm, conv_ref).start())
    for f in fetches[:4]:
        f.wait()

    slot = jnp.minimum(br, last - 1)
    top = off_ref[slot, 0, t]
    hh = size_ref[slot, 0, t]
    ww = size_ref[slot, 1, t]

    @pl.when(is_local)
    def _():
        sub = iota((256, 1), 0)
        sub_row = sub // WIN - top
        sub_col = sub % WIN
        lane64 = iota((1, 128), 1)
        inside = lane64 < S
        row_hits = jnp.where(jnp.logical_and(inside, ((lane64 * hh) >> 6) == sub_row), 1.0, 0.0)
        col_hits = jnp.where(jnp.logical_and(inside, ((lane64 * ww) >> 6) == sub_col), 1.0, 0.0)
        counts = jnp.sum(row_hits, axis=1, keepdims=True) * jnp.sum(col_hits, axis=1, keepdims=True)
        wide = 1024
        lane = iota((1, wide), 1)
        cols = jnp.where((((lane % S) * ww) >> 6) == sub_col, 1.0, 0.0)

        def pool_step(step, acc):
            rows_at = ((step * (wide // S) + lane // S) * hh) >> 6
            lhs = jnp.where(rows_at == sub_row, cols, 0.0).astype(BF)
            rhs = x_ref[pl.ds(pl.multiple_of(step * wide, wide), wide)]
            return acc + jnp.dot(lhs, rhs, preferred_element_type=F32)

        total = lax.fori_loop(0, CELLS // wide, pool_step, jnp.zeros((256, C), F32))
        win[...] = (total / jnp.maximum(counts, 1.0)).astype(BF).reshape(ROWS, WIN, C)

    count = ROWS - 1 + 2 * (n - 1)
    extra = jnp.where(first_up, 1, 0) + jnp.where(root_up, 1, 0) + jnp.where(root_down, 2, 0)
    pl.semaphore_wait(barrier, count + extra)

    def row_copy(r):
        f = xx if r % 2 else yy
        return rc(x_ref.at[r * GW : (r + 1) * GW], bands.at[f], gr_s.at[r], gr_r.at[0], (r, t))

    far_first = (6, 7, 4, 8, 5, 9, 2, 10, 3, 11, 0, 12, 1, 13, 14)

    @pl.when(is_root)
    def _():
        for r in far_first:
            row_copy(r).start()
        bands[f0] = x_ref[last * GW : (last + 1) * GW]

    def window_copy(d):
        r = (br + d) % ROWS
        f = jnp.where(r % 2 == 1, xx, yy)
        return rc(win.at[r], wall.at[f, br], zw_s.at[d], zw_r.at[br], (r, t))

    @pl.when(is_local)
    def _():
        for d in range(1, ROWS):
            window_copy(d).start()
        wall[f0, slot] = win[br]

    def axes_of(tile):
        high, low = lax.div(tile, n), lax.rem(tile, n)
        return jnp.where(up, high, low), jnp.where(up, low, high)

    diag = iota((WIN, n * GW), 1) - iota((WIN, n * GW), 0)

    def strip_step(g, carry):
        tile = tile_of(f0, g)
        for s in range(SLOTS):
            f_own, g_own = axes_of(own_ref[s, 0, tile])
            target = jnp.where(g_own == g0, f_own * GW + off_ref[s, 1, tile], -(n + 1) * GW)
            at = pl.ds(pl.multiple_of((g * SLOTS + s) * WIN, WIN), WIN)
            smat[at] = jnp.where(diag == target, 1.0, 0.0).astype(BF)
        return carry

    piece = iota((1, GW), 1) // WIN
    place = iota((1, GW), 1) % WIN
    column = iota((GW, 1), 0)

    def place_step(f, carry):
        tile = tile_of(f, g0)
        target = jnp.full((1, GW), -(n + 1) * GW, jnp.int32)
        for s in range(SLOTS):
            f_own, g_own = axes_of(own_ref[s, 0, tile])
            here = jnp.where(f_own == f0, g_own * GW + off_ref[s, 1, tile], -(n + 1) * GW)
            target = jnp.where(piece == s, here, target)
        target = target + place
        for g in range(n):
            pmat[g, f] = jnp.where(column + g * GW == target, 1.0, 0.0).astype(BF)
        wall[f, SLOTS] = jnp.zeros((WIN, C), BF)
        return carry

    lax.fori_loop(0, n, place_step, 0)
    lax.fori_loop(0, n, strip_step, 0)

    def gather_windows(d):
        own = wall.at[f0, 0:SLOTS]
        return rc(own, own, a1_s.at[d], a1_r.at[f0], (br, tile_of((f0 + d) % n, g0)))

    def gather_windows_wait(d):
        f = (f0 + d) % n
        part = wall.at[f, 0:SLOTS]
        rc(part, part, a1_s.at[d], a1_r.at[f], (br, t)).wait_recv()

    def gather_bands(d):
        own = bands.at[f0]
        return rc(own, own, r1_s.at[d], r1_r.at[f0], (br, tile_of((f0 + d) % n, g0)))

    def gather_bands_wait(d):
        f = (f0 + d) % n
        rc(bands.at[f], bands.at[f], r1_s.at[d], r1_r.at[f], (br, t)).wait_recv()

    for s in range(SLOTS):

        @pl.when(br != s)
        def _(s=s):
            rc(win.at[s], wall.at[f0, s], zw_s.at[s], zw_r.at[s], (br, t)).wait_recv()

    for d in range(1, n):
        gather_windows(d).start()

    @pl.when(is_local)
    def _():
        rc(bands.at[0], bands.at[f0], gr_s.at[0], gr_r.at[0], (br, t)).wait_recv()

    for d in range(1, n):
        gather_bands(d).start()

    fetches[4].wait()
    fetches[5].wait()
    fetch(6, cl_hbm, conv_ref).wait()
    zero = jnp.zeros((C, C), BF)
    for sft in range(3):
        for r in range(2):
            at = slice((r * 3 + sft) * C, (r * 3 + sft + 1) * C)
            for o in range(2):
                to = slice(o * C, (o + 1) * C)
                tap = r - o
                wlo[at, to] = conv_ref[tap, sft] if tap >= 0 else zero
                tap = r + 2 - o
                whi[at, to] = conv_ref[tap, sft] if tap <= 2 else zero

    def scatter_canvas(d):
        g = (g0 + d) % n
        return rc(canv.at[g], canv_in.at[g0], a2_s.at[d], a2_r.at[g0], (br, tile_of(f0, g)))

    def scatter_canvas_wait(d):
        g = (g0 + d) % n
        rc(canv.at[g], canv_in.at[g], a2_s.at[d], a2_r.at[g], (br, t)).wait_recv()

    def scatter_strips(d):
        g = (g0 + d) % n
        return rc(strip.at[g], strip_in.at[g0], r2_s.at[d], r2_r.at[g0], (br, tile_of(f0, g)))

    def scatter_strips_wait(d):
        g = (g0 + d) % n
        rc(strip.at[g], strip_in.at[g], r2_s.at[d], r2_r.at[g], (br, t)).wait_recv()

    for d in range(1, n):
        gather_windows_wait(d)
    pooled = jnp.zeros((GW, C), F32)
    for d in [*range(1, n), 0]:
        g = (g0 + d) % n
        pooled = jnp.zeros((GW, C), F32)
        for f in range(n):
            w = wall[f].reshape(GW, C)
            pooled = pooled + jnp.dot(pmat[g, f], w, preferred_element_type=F32)
        if d:
            canv[g] = pooled.astype(BF)
            scatter_canvas(d).start()

    for d in range(1, n):
        gather_bands_wait(d)
    own_strips = None
    block = SLOTS * WIN
    for d in [*range(1, n), 0]:
        g = (g0 + d) % n
        at = pl.ds(pl.multiple_of(g * block, WIN), block)
        cut = jnp.dot(smat[at], bands[...].reshape(n * GW, C), preferred_element_type=F32)
        own_strips = cut.astype(BF).reshape(SLOTS, WIN, C)
        if d:
            strip[g] = own_strips
            scatter_strips(d).start()

    def merged_copy():
        return rc(mine, rows.at[br + 1], m_s.at[0], m_r.at[br + 1], (last, t))

    def edge_up():
        return rc(mine, rows.at[ROWS + 1], m_s.at[1], m_r.at[ROWS + 1], (last, before))

    def edge_down():
        return rc(mine, rows.at[0], m_s.at[1], m_r.at[0], (last, after))

    for d in range(1, n):
        scatter_canvas_wait(d)
        pooled = pooled + canv_in[(g0 + d) % n].astype(F32)
    both = jnp.concatenate([bands[f0], pooled.astype(BF)], axis=1)
    merged = jnp.maximum(jnp.dot(both, mg_ref[...], preferred_element_type=F32), 0.0)
    mine[...] = merged.astype(BF)
    pl.when(is_local)(lambda: merged_copy().start())
    pl.when(first_up)(lambda: edge_up().start())
    pl.when(root_down)(lambda: edge_down().start())

    def crop_copy(d):
        b = (br + d) % ROWS
        return rc(total_strip.at[b], crop.at[br], zc_s.at[d], zc_r.at[br], (b, t))

    for d in range(1, n):
        scatter_strips_wait(d)
        own_strips = own_strips + strip_in[(g0 + d) % n]
    total_strip[0:SLOTS] = own_strips
    for d in range(1, ROWS):

        @pl.when((br + d) % ROWS != last)
        def _(d=d):
            crop_copy(d).start()

    def put(at, lanes, value, width):
        m = value.reshape(-1, width, C)
        col = iota((1, width, 1), 1)
        left = jnp.where(col == 0, 0.0, pltpu.roll(m, 1, 1))
        right = jnp.where(col == width - 1, 0.0, pltpu.roll(m, width - 1, 1))
        for sft, v in enumerate((left, m, right)):
            zbuf[at, lanes + sft * C : lanes + (sft + 1) * C] = v.reshape(-1, C).astype(BF)

    def conv_block(first, hi_first):
        lo = zbuf[pl.ds(first, 256)]
        hi = zbuf[pl.ds(hi_first, 256)]
        res = jnp.dot(lo, wlo[...], preferred_element_type=F32)
        res = res + jnp.dot(hi, whi[...], preferred_element_type=F32)
        return res.astype(BF)

    @pl.when(is_local)
    def _():
        zbuf[0:S, 0 : 3 * C] = jnp.zeros((S, 3 * C), BF)
        zbuf[S // 2 * S : (S // 2 + 1) * S, 3 * C :] = jnp.zeros((S, 3 * C), BF)
        s1024 = iota((1024, 1), 0)
        target = (s1024 // S) * WIN + (((s1024 % S) * ww) >> 6)
        lhs = jnp.where(iota((1, 256), 1) == target, 1.0, 0.0).astype(BF)
        weight = ml_ref[...]
        crop[br] = total_strip[slot]
        for r in range(ROWS):

            @pl.when(br != r)
            def _(r=r):
                rc(total_strip.at[0], crop.at[r], zc_s.at[r], zc_r.at[r], (br, t)).wait_recv()

        strips = crop[...].reshape(ROWS * WIN, C)
        cu[...] = jnp.dot(lhs, strips, preferred_element_type=F32).astype(BF).reshape(ROWS, S, C)

        def merge_block(b, carry):
            ups = []
            for i in range(8):
                r = (((b * 8 + i) * hh) >> 6) + top
                ups.append(cu[jnp.clip(r, 0, ROWS - 1)])
            first = pl.multiple_of(b * 8 * S, 8 * S)
            both = jnp.concatenate(
                [x_ref[pl.ds(first, 8 * S)], jnp.concatenate(ups, axis=0)], axis=1
            )
            m = jnp.maximum(jnp.dot(both, weight, preferred_element_type=F32), 0.0)
            for i in range(8):
                pair = b * 4 + (i + 1) // 2
                at = pl.ds(pl.multiple_of(pair * S, S), S)
                put(at, 3 * C * ((i + 1) % 2), m[i * S : (i + 1) * S], S)
            return carry

        lax.fori_loop(0, S // 8, merge_block, 0)

        def conv_step(b, carry):
            first = pl.multiple_of(b * 256, 256)
            res = conv_block(first, pl.multiple_of(b * 256 + S, S))
            for i in range(4):
                for o in range(2):
                    at = pl.ds(pl.multiple_of(b * 512 + (2 * i + o) * S, S), S)
                    out_ref[at] = res[i * S : (i + 1) * S, o * C : (o + 1) * C]
            return carry

        lax.fori_loop(0, S // 8, conv_step, 0)

    @pl.when(is_root)
    def _():
        rows[ROWS] = mine[...]

        @pl.when(jnp.logical_not(has_before))
        def _():
            rows[0] = jnp.zeros((GW, C), BF)

        @pl.when(jnp.logical_not(has_after))
        def _():
            rows[ROWS + 1] = jnp.zeros((GW, C), BF)

        def wait(i):
            rc(mine, rows.at[i], m_s.at[0], m_r.at[i], (br, t)).wait_recv()

        here = set()
        done = set()
        for i in (16, 15, 1, 2, 13, 14, 3, 4, 11, 12, 5, 6, 9, 10, 0, 17, 7, 8):
            if i == 0:
                pl.when(has_before)(functools.partial(wait, 0))
            elif i == ROWS + 1:
                pl.when(has_after)(functools.partial(wait, ROWS + 1))
            elif i != ROWS:
                wait(i)
            put(slice(i // 2 * GW, (i // 2 + 1) * GW), 3 * C * (i % 2), rows[i].astype(F32), GW)
            here.add(i)
            for q in range(8):
                if q not in done and here >= {2 * q, 2 * q + 1, 2 * q + 2, 2 * q + 3}:
                    done.add(q)
                    res = conv_block(q * GW, (q + 1) * GW)
                    for o in range(2):
                        at = slice((2 * q + o) * GW, (2 * q + o + 1) * GW)
                        out_ref[at] = res[:, o * C : (o + 1) * C]

    @pl.when(is_root)
    def _():
        for r in far_first:
            row_copy(r).wait_send()

    @pl.when(is_local)
    def _():
        for d in range(1, ROWS):
            window_copy(d).wait_send()
        merged_copy().wait_send()

    for d in range(1, n):
        gather_windows(d).wait_send()
        gather_bands(d).wait_send()
        scatter_canvas(d).wait_send()
        scatter_strips(d).wait_send()
    for d in range(1, ROWS):

        @pl.when((br + d) % ROWS != last)
        def _(d=d):
            crop_copy(d).wait_send()

    pl.when(first_up)(lambda: edge_up().wait_send())
    pl.when(root_down)(lambda: edge_down().wait_send())


def run(n, features, merge_local, conv_local, merge_global, conv_global, offsets, sizes, owners):
    hbm = pl.BlockSpec(memory_space=pltpu.HBM)
    dma = pltpu.SemaphoreType.DMA

    def vm(*shape):
        return pltpu.VMEM(shape, BF)

    def sm(*shape):
        return pltpu.SMEM(shape, jnp.int32)

    tiles = n * n
    out = pl.pallas_call(
        functools.partial(kernel, n),
        out_shape=jax.ShapeDtypeStruct((CELLS, C), BF),
        in_specs=[hbm] * 8,
        out_specs=pl.BlockSpec(memory_space=pltpu.VMEM),
        scratch_shapes=[
            vm(CELLS, C),
            vm(2 * C, C),
            vm(2 * C, C),
            vm(3, 3, C, C),
            sm(SLOTS, 2, tiles),
            sm(SLOTS, 2, tiles),
            sm(SLOTS, 1, tiles),
            vm(ROWS, WIN, C),
            vm(n, ROWS, WIN, C),
            vm(n, GW, C),
            vm(n * SLOTS * WIN, n * GW),
            vm(n, n, GW, GW),
            vm(n, SLOTS, WIN, C),
            vm(n, SLOTS, WIN, C),
            vm(n, GW, C),
            vm(n, GW, C),
            vm(ROWS, WIN, C),
            vm(ROWS, WIN, C),
            vm(ROWS + 2, GW, C),
            vm(GW, C),
            vm(ROWS, S, C),
            vm(9 * GW, 6 * C),
            vm(6 * C, 2 * C),
            vm(6 * C, 2 * C),
            dma((7,)),
            dma((ROWS,)),
            dma((1,)),
            dma((ROWS,)),
            dma((ROWS,)),
            dma((n,)),
            dma((n,)),
            dma((n,)),
            dma((n,)),
            dma((n,)),
            dma((n,)),
            dma((n,)),
            dma((n,)),
            dma((ROWS,)),
            dma((ROWS,)),
            dma((2,)),
            dma((ROWS + 2,)),
        ],
        compiler_params=pltpu.CompilerParams(
            collective_id=0, has_side_effects=True, vmem_limit_bytes=58 * 1024 * 1024
        ),
        name="glue",
    )(
        features.reshape(CELLS, C), merge_local, conv_local, merge_global, conv_global,
        offsets.transpose(0, 2, 3, 1).reshape(SLOTS, 2, tiles),
        sizes.transpose(0, 2, 3, 1).reshape(SLOTS, 2, tiles),
        owners.transpose(0, 2, 1),
    )
    return out.reshape(features.shape)


def solution(mesh):
    n = 1
    while n * n < mesh.shape["tile"]:
        n += 1
    in_specs = (P("branch", "tile", None, None, None), P(), P(), P(), P(), P(), P(), P())
    out_specs = P("branch", "tile", None, None, None)
    return jax.shard_map(
        functools.partial(run, n),
        mesh=mesh,
        in_specs=in_specs,
        out_specs=out_specs,
        check_vma=False,
    )
```

```python
import functools

import jax
import jax.numpy as jnp
from jax import lax
from jax.experimental import pallas as pl
from jax.experimental.pallas import tpu as pltpu
from jax.sharding import PartitionSpec as P

MESH = pl.DeviceIdType.MESH
BF = jnp.bfloat16
F32 = jnp.float32
C = 128
S = 64
GW = 256
WIN = 16
CELLS = 4096
ROWS = 16
SLOTS = 15


def iota(shape, dim):
    return lax.broadcasted_iota(jnp.int32, shape, dim)


def kernel(
    n, x_hbm, ml_hbm, cl_hbm, mg_hbm, cg_hbm, off_hbm, size_hbm, own_hbm, out_hbm,
    x_ref, ml_ref, mg_ref, conv_ref, off_ref, size_ref, own_ref,
    win, wall, bands, smat, pmat, strip, strip_in, canv, canv_in, total_strip, crop, rows, mine, cu, zbuf, wlo, whi, out_ref,
    in_s, out_s, gr_s, gr_r, zw_s, zw_r, a1_s, a1_r, a2_s, a2_r, r1_s, r1_r, r2_s, r2_r, zc_s, zc_r, m_s, m_r,
):
    tiles = n * n
    br = lax.axis_index("branch")
    t = lax.axis_index("tile")
    up = br % 2 == 1
    xx, yy = t // n, t % n
    f0 = jnp.where(up, xx, yy)
    g0 = jnp.where(up, yy, xx)
    last = ROWS - 1
    is_root = br == last
    is_local = br < last

    def tile_of(f, g):
        return jnp.where(up, f * n + g, g * n + f)

    def rc(src, dst, ss, rs, dev):
        return pltpu.make_async_remote_copy(
            src_ref=src, dst_ref=dst, send_sem=ss, recv_sem=rs, device_id=dev, device_id_type=MESH
        )

    barrier = pltpu.get_barrier_semaphore()

    def greet(b, tile):
        pl.semaphore_signal(barrier, inc=1, device_id=(b, tile), device_id_type=MESH)

    for d in range(1, ROWS):
        greet((br + d) % ROWS, t)
    for d in range(1, n):
        greet(br, ((xx + d) % n) * n + yy)
        greet(br, xx * n + (yy + d) % n)
    before = jnp.maximum(t - 1, 0)
    after = jnp.minimum(t + 1, tiles - 1)
    has_before, has_after = t > 0, t < tiles - 1
    is_first = br == 0
    first_up = jnp.logical_and(is_first, has_before)
    root_up = jnp.logical_and(is_root, has_before)
    root_down = jnp.logical_and(is_root, has_after)

    @pl.when(first_up)
    def _():
        greet(last, before)

    @pl.when(root_up)
    def _():
        greet(last, before)

    @pl.when(root_down)
    def _():
        greet(0, after)
        greet(last, after)

    def fetch(i, src, dst):
        return pltpu.make_async_copy(src, dst, in_s.at[i])

    fetches = [
        fetch(0, size_hbm, size_ref),
        fetch(1, off_hbm, off_ref),
        fetch(2, own_hbm, own_ref),
        fetch(3, x_hbm, x_ref),
        fetch(4, mg_hbm, mg_ref),
        fetch(5, ml_hbm, ml_ref),
    ]
    for f in fetches:
        f.start()
    pl.when(is_root)(lambda: fetch(6, cg_hbm, conv_ref).start())
    pl.when(is_local)(lambda: fetch(6, cl_hbm, conv_ref).start())
    for f in fetches[:4]:
        f.wait()

    slot = jnp.minimum(br, last - 1)
    top = off_ref[slot, 0, t]
    hh = size_ref[slot, 0, t]
    ww = size_ref[slot, 1, t]

    @pl.when(is_local)
    def _():
        sub = iota((256, 1), 0)
        sub_row = sub // WIN - top
        sub_col = sub % WIN
        lane64 = iota((1, 128), 1)
        inside = lane64 < S
        row_hits = jnp.where(jnp.logical_and(inside, ((lane64 * hh) >> 6) == sub_row), 1.0, 0.0)
        col_hits = jnp.where(jnp.logical_and(inside, ((lane64 * ww) >> 6) == sub_col), 1.0, 0.0)
        counts = jnp.sum(row_hits, axis=1, keepdims=True) * jnp.sum(col_hits, axis=1, keepdims=True)
        wide = 1024
        lane = iota((1, wide), 1)
        cols = jnp.where((((lane % S) * ww) >> 6) == sub_col, 1.0, 0.0)

        def pool_step(step, acc):
            rows_at = ((step * (wide // S) + lane // S) * hh) >> 6
            lhs = jnp.where(rows_at == sub_row, cols, 0.0).astype(BF)
            rhs = x_ref[pl.ds(pl.multiple_of(step * wide, wide), wide)]
            return acc + jnp.dot(lhs, rhs, preferred_element_type=F32)

        total = lax.fori_loop(0, CELLS // wide, pool_step, jnp.zeros((256, C), F32))
        win[...] = (total / jnp.maximum(counts, 1.0)).astype(BF).reshape(ROWS, WIN, C)

    count = ROWS - 1 + 2 * (n - 1)
    extra = jnp.where(first_up, 1, 0) + jnp.where(root_up, 1, 0) + jnp.where(root_down, 2, 0)
    pl.semaphore_wait(barrier, count + extra)

    def row_copy(r):
        f = xx if r % 2 else yy
        return rc(x_ref.at[r * GW : (r + 1) * GW], bands.at[f], gr_s.at[r], gr_r.at[0], (r, t))

    far_first = (6, 7, 4, 8, 5, 9, 2, 10, 3, 11, 0, 12, 1, 13, 14)

    @pl.when(is_root)
    def _():
        for r in far_first:
            row_copy(r).start()
        bands[f0] = x_ref[last * GW : (last + 1) * GW]

    def window_copy(d):
        r = (br + d) % ROWS
        f = jnp.where(r % 2 == 1, xx, yy)
        return rc(win.at[r], wall.at[f, br], zw_s.at[d], zw_r.at[br], (r, t))

    @pl.when(is_local)
    def _():
        for d in range(1, ROWS):
            window_copy(d).start()
        wall[f0, slot] = win[br]

    def axes_of(tile):
        high, low = lax.div(tile, n), lax.rem(tile, n)
        return jnp.where(up, high, low), jnp.where(up, low, high)

    diag = iota((WIN, n * GW), 1) - iota((WIN, n * GW), 0)

    def strip_step(g, carry):
        tile = tile_of(f0, g)
        for s in range(SLOTS):
            f_own, g_own = axes_of(own_ref[s, 0, tile])
            target = jnp.where(g_own == g0, f_own * GW + off_ref[s, 1, tile], -(n + 1) * GW)
            at = pl.ds(pl.multiple_of((g * SLOTS + s) * WIN, WIN), WIN)
            smat[at] = jnp.where(diag == target, 1.0, 0.0).astype(BF)
        return carry

    piece = iota((1, GW), 1) // WIN
    place = iota((1, GW), 1) % WIN
    column = iota((GW, 1), 0)

    def place_step(f, carry):
        tile = tile_of(f, g0)
        target = jnp.full((1, GW), -(n + 1) * GW, jnp.int32)
        for s in range(SLOTS):
            f_own, g_own = axes_of(own_ref[s, 0, tile])
            here = jnp.where(f_own == f0, g_own * GW + off_ref[s, 1, tile], -(n + 1) * GW)
            target = jnp.where(piece == s, here, target)
        target = target + place
        for g in range(n):
            pmat[g, f] = jnp.where(column + g * GW == target, 1.0, 0.0).astype(BF)
        wall[f, SLOTS] = jnp.zeros((WIN, C), BF)
        return carry

    lax.fori_loop(0, n, place_step, 0)
    lax.fori_loop(0, n, strip_step, 0)

    def gather_windows(d):
        own = wall.at[f0, 0:SLOTS]
        return rc(own, own, a1_s.at[d], a1_r.at[f0], (br, tile_of((f0 + d) % n, g0)))

    def gather_windows_wait(d):
        f = (f0 + d) % n
        part = wall.at[f, 0:SLOTS]
        rc(part, part, a1_s.at[d], a1_r.at[f], (br, t)).wait_recv()

    def gather_bands(d):
        own = bands.at[f0]
        return rc(own, own, r1_s.at[d], r1_r.at[f0], (br, tile_of((f0 + d) % n, g0)))

    def gather_bands_wait(d):
        f = (f0 + d) % n
        rc(bands.at[f], bands.at[f], r1_s.at[d], r1_r.at[f], (br, t)).wait_recv()

    for s in range(SLOTS):

        @pl.when(br != s)
        def _(s=s):
            rc(win.at[s], wall.at[f0, s], zw_s.at[s], zw_r.at[s], (br, t)).wait_recv()

    for d in range(1, n):
        gather_windows(d).start()

    @pl.when(is_local)
    def _():
        rc(bands.at[0], bands.at[f0], gr_s.at[0], gr_r.at[0], (br, t)).wait_recv()

    for d in range(1, n):
        gather_bands(d).start()

    fetches[4].wait()
    fetches[5].wait()
    fetch(6, cl_hbm, conv_ref).wait()
    zero = jnp.zeros((C, C), BF)
    for sft in range(3):
        for r in range(2):
            at = slice((r * 3 + sft) * C, (r * 3 + sft + 1) * C)
            for o in range(2):
                to = slice(o * C, (o + 1) * C)
                tap = r - o
                wlo[at, to] = conv_ref[tap, sft] if tap >= 0 else zero
                tap = r + 2 - o
                whi[at, to] = conv_ref[tap, sft] if tap <= 2 else zero

    def scatter_canvas(d):
        g = (g0 + d) % n
        return rc(canv.at[g], canv_in.at[g0], a2_s.at[d], a2_r.at[g0], (br, tile_of(f0, g)))

    def scatter_canvas_wait(d):
        g = (g0 + d) % n
        rc(canv.at[g], canv_in.at[g], a2_s.at[d], a2_r.at[g], (br, t)).wait_recv()

    def scatter_strips(d):
        g = (g0 + d) % n
        return rc(strip.at[g], strip_in.at[g0], r2_s.at[d], r2_r.at[g0], (br, tile_of(f0, g)))

    def scatter_strips_wait(d):
        g = (g0 + d) % n
        rc(strip.at[g], strip_in.at[g], r2_s.at[d], r2_r.at[g], (br, t)).wait_recv()

    for d in range(1, n):
        gather_windows_wait(d)
    pooled = jnp.zeros((GW, C), F32)
    for d in [*range(1, n), 0]:
        g = (g0 + d) % n
        pooled = jnp.zeros((GW, C), F32)
        for f in range(n):
            w = wall[f].reshape(GW, C)
            pooled = pooled + jnp.dot(pmat[g, f], w, preferred_element_type=F32)
        if d:
            canv[g] = pooled.astype(BF)
            scatter_canvas(d).start()

    for d in range(1, n):
        gather_bands_wait(d)
    own_strips = None
    block = SLOTS * WIN
    for d in [*range(1, n), 0]:
        g = (g0 + d) % n
        at = pl.ds(pl.multiple_of(g * block, WIN), block)
        cut = jnp.dot(smat[at], bands[...].reshape(n * GW, C), preferred_element_type=F32)
        own_strips = cut.astype(BF).reshape(SLOTS, WIN, C)
        if d:
            strip[g] = own_strips
            scatter_strips(d).start()

    def merged_copy():
        return rc(mine, rows.at[br + 1], m_s.at[0], m_r.at[br + 1], (last, t))

    def edge_up():
        return rc(mine, rows.at[ROWS + 1], m_s.at[1], m_r.at[ROWS + 1], (last, before))

    def edge_down():
        return rc(mine, rows.at[0], m_s.at[1], m_r.at[0], (last, after))

    for d in range(1, n):
        scatter_canvas_wait(d)
        pooled = pooled + canv_in[(g0 + d) % n].astype(F32)
    both = jnp.concatenate([bands[f0], pooled.astype(BF)], axis=1)
    merged = jnp.maximum(jnp.dot(both, mg_ref[...], preferred_element_type=F32), 0.0)
    mine[...] = merged.astype(BF)
    pl.when(is_local)(lambda: merged_copy().start())
    pl.when(first_up)(lambda: edge_up().start())
    pl.when(root_down)(lambda: edge_down().start())

    def crop_copy(d):
        b = (br + d) % ROWS
        return rc(total_strip.at[b], crop.at[br], zc_s.at[d], zc_r.at[br], (b, t))

    for d in range(1, n):
        scatter_strips_wait(d)
        own_strips = own_strips + strip_in[(g0 + d) % n]
    total_strip[0:SLOTS] = own_strips
    for d in range(1, ROWS):

        @pl.when((br + d) % ROWS != last)
        def _(d=d):
            crop_copy(d).start()

    def put(at, lanes, value, width):
        m = value.reshape(-1, width, C)
        col = iota((1, width, 1), 1)
        left = jnp.where(col == 0, 0.0, pltpu.roll(m, 1, 1))
        right = jnp.where(col == width - 1, 0.0, pltpu.roll(m, width - 1, 1))
        for sft, v in enumerate((left, m, right)):
            zbuf[at, lanes + sft * C : lanes + (sft + 1) * C] = v.reshape(-1, C).astype(BF)

    def out_copy(b):
        at = pl.ds(b * 512, 512)
        return pltpu.make_async_copy(out_ref.at[at], out_hbm.at[at], out_s.at[b])

    def conv_block(first, hi_first):
        lo = zbuf[first : first + 256]
        hi = zbuf[hi_first : hi_first + 256]
        res = jnp.dot(lo, wlo[...], preferred_element_type=F32)
        res = res + jnp.dot(hi, whi[...], preferred_element_type=F32)
        return res.astype(BF)

    @pl.when(is_local)
    def _():
        zbuf[0:S, 0 : 3 * C] = jnp.zeros((S, 3 * C), BF)
        zbuf[S // 2 * S : (S // 2 + 1) * S, 3 * C :] = jnp.zeros((S, 3 * C), BF)
        s1024 = iota((1024, 1), 0)
        target = (s1024 // S) * WIN + (((s1024 % S) * ww) >> 6)
        lhs = jnp.where(iota((1, 256), 1) == target, 1.0, 0.0).astype(BF)
        weight = ml_ref[...]
        crop[br] = total_strip[slot]
        for r in range(ROWS):

            @pl.when(br != r)
            def _(r=r):
                rc(total_strip.at[0], crop.at[r], zc_s.at[r], zc_r.at[r], (br, t)).wait_recv()

        strips = crop[...].reshape(ROWS * WIN, C)
        cu[...] = jnp.dot(lhs, strips, preferred_element_type=F32).astype(BF).reshape(ROWS, S, C)

        for b in range(S // 8):
            ups = []
            for i in range(8):
                r = (((b * 8 + i) * hh) >> 6) + top
                ups.append(cu[jnp.clip(r, 0, ROWS - 1)])
            both = jnp.concatenate(
                [x_ref[b * 8 * S : (b + 1) * 8 * S], jnp.concatenate(ups, axis=0)], axis=1
            )
            m = jnp.maximum(jnp.dot(both, weight, preferred_element_type=F32), 0.0)
            for i in range(8):
                pair = b * 4 + (i + 1) // 2
                at = slice(pair * S, (pair + 1) * S)
                put(at, 3 * C * ((i + 1) % 2), m[i * S : (i + 1) * S], S)

        for b in range(S // 8):
            res = conv_block(b * 256, b * 256 + S)
            for i in range(4):
                for o in range(2):
                    at = b * 512 + (2 * i + o) * S
                    out_ref[at : at + S] = res[i * S : (i + 1) * S, o * C : (o + 1) * C]
            out_copy(b).start()

    @pl.when(is_root)
    def _():
        rows[ROWS] = mine[...]

        @pl.when(jnp.logical_not(has_before))
        def _():
            rows[0] = jnp.zeros((GW, C), BF)

        @pl.when(jnp.logical_not(has_after))
        def _():
            rows[ROWS + 1] = jnp.zeros((GW, C), BF)

        def wait(i):
            rc(mine, rows.at[i], m_s.at[0], m_r.at[i], (br, t)).wait_recv()

        here = set()
        done = set()
        for i in (16, 15, 1, 2, 13, 14, 3, 4, 11, 12, 5, 6, 9, 10, 0, 17, 7, 8):
            if i == 0:
                pl.when(has_before)(functools.partial(wait, 0))
            elif i == ROWS + 1:
                pl.when(has_after)(functools.partial(wait, ROWS + 1))
            elif i != ROWS:
                wait(i)
            put(slice(i // 2 * GW, (i // 2 + 1) * GW), 3 * C * (i % 2), rows[i].astype(F32), GW)
            here.add(i)
            for q in range(8):
                if q not in done and here >= {2 * q, 2 * q + 1, 2 * q + 2, 2 * q + 3}:
                    done.add(q)
                    res = conv_block(q * GW, (q + 1) * GW)
                    for o in range(2):
                        at = slice((2 * q + o) * GW, (2 * q + o + 1) * GW)
                        out_ref[at] = res[:, o * C : (o + 1) * C]
                    out_copy(q).start()

    for b in range(8):
        out_copy(b).wait()
    @pl.when(is_root)
    def _():
        for r in far_first:
            row_copy(r).wait_send()

    @pl.when(is_local)
    def _():
        for d in range(1, ROWS):
            window_copy(d).wait_send()
        merged_copy().wait_send()

    for d in range(1, n):
        gather_windows(d).wait_send()
        gather_bands(d).wait_send()
        scatter_canvas(d).wait_send()
        scatter_strips(d).wait_send()
    for d in range(1, ROWS):

        @pl.when((br + d) % ROWS != last)
        def _(d=d):
            crop_copy(d).wait_send()

    pl.when(first_up)(lambda: edge_up().wait_send())
    pl.when(root_down)(lambda: edge_down().wait_send())


def run(n, features, merge_local, conv_local, merge_global, conv_global, offsets, sizes, owners):
    hbm = pl.BlockSpec(memory_space=pltpu.HBM)
    dma = pltpu.SemaphoreType.DMA

    def vm(*shape):
        return pltpu.VMEM(shape, BF)

    def sm(*shape):
        return pltpu.SMEM(shape, jnp.int32)

    tiles = n * n
    out = pl.pallas_call(
        functools.partial(kernel, n),
        out_shape=jax.ShapeDtypeStruct((CELLS, C), BF),
        in_specs=[hbm] * 8,
        out_specs=hbm,
        scratch_shapes=[
            vm(CELLS, C),
            vm(2 * C, C),
            vm(2 * C, C),
            vm(3, 3, C, C),
            sm(SLOTS, 2, tiles),
            sm(SLOTS, 2, tiles),
            sm(SLOTS, 1, tiles),
            vm(ROWS, WIN, C),
            vm(n, ROWS, WIN, C),
            vm(n, GW, C),
            vm(n * SLOTS * WIN, n * GW),
            vm(n, n, GW, GW),
            vm(n, SLOTS, WIN, C),
            vm(n, SLOTS, WIN, C),
            vm(n, GW, C),
            vm(n, GW, C),
            vm(ROWS, WIN, C),
            vm(ROWS, WIN, C),
            vm(ROWS + 2, GW, C),
            vm(GW, C),
            vm(ROWS, S, C),
            vm(9 * GW, 6 * C),
            vm(6 * C, 2 * C),
            vm(6 * C, 2 * C),
            vm(CELLS, C),
            dma((7,)),
            dma((8,)),
            dma((ROWS,)),
            dma((1,)),
            dma((ROWS,)),
            dma((ROWS,)),
            dma((n,)),
            dma((n,)),
            dma((n,)),
            dma((n,)),
            dma((n,)),
            dma((n,)),
            dma((n,)),
            dma((n,)),
            dma((ROWS,)),
            dma((ROWS,)),
            dma((2,)),
            dma((ROWS + 2,)),
        ],
        compiler_params=pltpu.CompilerParams(
            collective_id=0, has_side_effects=True, vmem_limit_bytes=58 * 1024 * 1024
        ),
        name="glue",
    )(
        features.reshape(CELLS, C), merge_local, conv_local, merge_global, conv_global,
        offsets.transpose(0, 2, 3, 1).reshape(SLOTS, 2, tiles),
        sizes.transpose(0, 2, 3, 1).reshape(SLOTS, 2, tiles),
        owners.transpose(0, 2, 1),
    )
    return out.reshape(features.shape)


def solution(mesh):
    n = 1
    while n * n < mesh.shape["tile"]:
        n += 1
    in_specs = (P("branch", "tile", None, None, None), P(), P(), P(), P(), P(), P(), P())
    out_specs = P("branch", "tile", None, None, None)
    return jax.shard_map(
        functools.partial(run, n),
        mesh=mesh,
        in_specs=in_specs,
        out_specs=out_specs,
        check_vma=False,
    )
```

```python
import functools

import jax
import jax.numpy as jnp
from jax import lax
from jax.experimental import pallas as pl
from jax.experimental.pallas import tpu as pltpu
from jax.sharding import PartitionSpec as P

MESH = pl.DeviceIdType.MESH
BF = jnp.bfloat16
F32 = jnp.float32
C = 128
S = 64
GW = 256
WIN = 16
CELLS = 4096
ROWS = 16
SLOTS = 15


def iota(shape, dim):
    return lax.broadcasted_iota(jnp.int32, shape, dim)


def kernel(
    n, x_hbm, ml_hbm, cl_hbm, mg_hbm, cg_hbm, off_hbm, size_hbm, own_hbm, out_ref,
    x_ref, ml_ref, mg_ref, conv_ref, off_ref, size_ref, own_ref,
    win, wall, bands, smat, pmat, strip, strip_in, canv, canv_in, total_strip, crop, rows, mine, cu, zbuf, wlo, whi,
    in_s, gr_s, gr_r, zw_s, zw_r, a1_s, a1_r, a2_s, a2_r, r1_s, r1_r, r2_s, r2_r, zc_s, zc_r, m_s, m_r,
):
    tiles = n * n
    br = lax.axis_index("branch")
    t = lax.axis_index("tile")
    up = br % 2 == 1
    xx, yy = t // n, t % n
    f0 = jnp.where(up, xx, yy)
    g0 = jnp.where(up, yy, xx)
    last = ROWS - 1
    is_root = br == last
    is_local = br < last

    def tile_of(f, g):
        return jnp.where(up, f * n + g, g * n + f)

    def rc(src, dst, ss, rs, dev):
        return pltpu.make_async_remote_copy(
            src_ref=src, dst_ref=dst, send_sem=ss, recv_sem=rs, device_id=dev, device_id_type=MESH
        )

    barrier = pltpu.get_barrier_semaphore()

    def greet(b, tile):
        pl.semaphore_signal(barrier, inc=1, device_id=(b, tile), device_id_type=MESH)

    for d in range(1, ROWS):
        greet((br + d) % ROWS, t)
    for d in range(1, n):
        greet(br, ((xx + d) % n) * n + yy)
        greet(br, xx * n + (yy + d) % n)
    before = jnp.maximum(t - 1, 0)
    after = jnp.minimum(t + 1, tiles - 1)
    has_before, has_after = t > 0, t < tiles - 1
    is_first = br == 0
    first_up = jnp.logical_and(is_first, has_before)
    root_up = jnp.logical_and(is_root, has_before)
    root_down = jnp.logical_and(is_root, has_after)

    @pl.when(first_up)
    def _():
        greet(last, before)

    @pl.when(root_up)
    def _():
        greet(last, before)

    @pl.when(root_down)
    def _():
        greet(0, after)
        greet(last, after)

    def fetch(i, src, dst):
        return pltpu.make_async_copy(src, dst, in_s.at[i])

    fetches = [
        fetch(0, size_hbm, size_ref),
        fetch(1, off_hbm, off_ref),
        fetch(2, own_hbm, own_ref),
        fetch(3, x_hbm, x_ref),
        fetch(4, mg_hbm, mg_ref),
        fetch(5, ml_hbm, ml_ref),
    ]
    for f in fetches:
        f.start()
    pl.when(is_root)(lambda: fetch(6, cg_hbm, conv_ref).start())
    pl.when(is_local)(lambda: fetch(6, cl_hbm, conv_ref).start())
    for f in fetches[:4]:
        f.wait()

    slot = jnp.minimum(br, last - 1)
    top = off_ref[slot, 0, t]
    hh = size_ref[slot, 0, t]
    ww = size_ref[slot, 1, t]

    @pl.when(is_local)
    def _():
        sub = iota((256, 1), 0)
        sub_row = sub // WIN - top
        sub_col = sub % WIN
        lane64 = iota((1, 128), 1)
        inside = lane64 < S
        row_hits = jnp.where(jnp.logical_and(inside, ((lane64 * hh) >> 6) == sub_row), 1.0, 0.0)
        col_hits = jnp.where(jnp.logical_and(inside, ((lane64 * ww) >> 6) == sub_col), 1.0, 0.0)
        counts = jnp.sum(row_hits, axis=1, keepdims=True) * jnp.sum(col_hits, axis=1, keepdims=True)
        wide = 1024
        lane = iota((1, wide), 1)
        cols = jnp.where((((lane % S) * ww) >> 6) == sub_col, 1.0, 0.0)

        def pool_step(step, acc):
            rows_at = ((step * (wide // S) + lane // S) * hh) >> 6
            lhs = jnp.where(rows_at == sub_row, cols, 0.0).astype(BF)
            rhs = x_ref[pl.ds(pl.multiple_of(step * wide, wide), wide)]
            return acc + jnp.dot(lhs, rhs, preferred_element_type=F32)

        total = lax.fori_loop(0, CELLS // wide, pool_step, jnp.zeros((256, C), F32))
        win[...] = (total / jnp.maximum(counts, 1.0)).astype(BF).reshape(ROWS, WIN, C)

    count = ROWS - 1 + 2 * (n - 1)
    extra = jnp.where(first_up, 1, 0) + jnp.where(root_up, 1, 0) + jnp.where(root_down, 2, 0)
    pl.semaphore_wait(barrier, count + extra)

    def row_copy(r):
        f = xx if r % 2 else yy
        return rc(x_ref.at[r * GW : (r + 1) * GW], bands.at[f], gr_s.at[r], gr_r.at[0], (r, t))

    far_first = (6, 7, 4, 8, 5, 9, 2, 10, 3, 11, 0, 12, 1, 13, 14)

    @pl.when(is_root)
    def _():
        for r in far_first:
            row_copy(r).start()
        bands[f0] = x_ref[last * GW : (last + 1) * GW]

    def window_copy(d):
        r = (br + d) % ROWS
        f = jnp.where(r % 2 == 1, xx, yy)
        return rc(win.at[r], wall.at[f, br], zw_s.at[d], zw_r.at[br], (r, t))

    @pl.when(is_local)
    def _():
        for d in range(1, ROWS):
            window_copy(d).start()
        wall[f0, slot] = win[br]

    def axes_of(tile):
        high, low = lax.div(tile, n), lax.rem(tile, n)
        return jnp.where(up, high, low), jnp.where(up, low, high)

    diag = iota((WIN, n * GW), 1) - iota((WIN, n * GW), 0)

    def strip_step(g, carry):
        tile = tile_of(f0, g)
        for s in range(SLOTS):
            f_own, g_own = axes_of(own_ref[s, 0, tile])
            target = jnp.where(g_own == g0, f_own * GW + off_ref[s, 1, tile], -(n + 1) * GW)
            at = pl.ds(pl.multiple_of((g * SLOTS + s) * WIN, WIN), WIN)
            smat[at] = jnp.where(diag == target, 1.0, 0.0).astype(BF)
        return carry

    piece = iota((1, GW), 1) // WIN
    place = iota((1, GW), 1) % WIN
    column = iota((GW, 1), 0)

    def place_step(f, carry):
        tile = tile_of(f, g0)
        target = jnp.full((1, GW), -(n + 1) * GW, jnp.int32)
        for s in range(SLOTS):
            f_own, g_own = axes_of(own_ref[s, 0, tile])
            here = jnp.where(f_own == f0, g_own * GW + off_ref[s, 1, tile], -(n + 1) * GW)
            target = jnp.where(piece == s, here, target)
        target = target + place
        for g in range(n):
            pmat[g, f] = jnp.where(column + g * GW == target, 1.0, 0.0).astype(BF)
        wall[f, SLOTS] = jnp.zeros((WIN, C), BF)
        return carry

    lax.fori_loop(0, n, place_step, 0)
    lax.fori_loop(0, n, strip_step, 0)

    def gather_windows(d):
        own = wall.at[f0, 0:SLOTS]
        return rc(own, own, a1_s.at[d], a1_r.at[f0], (br, tile_of((f0 + d) % n, g0)))

    def gather_windows_wait(d):
        f = (f0 + d) % n
        part = wall.at[f, 0:SLOTS]
        rc(part, part, a1_s.at[d], a1_r.at[f], (br, t)).wait_recv()

    def gather_bands(d):
        own = bands.at[f0]
        return rc(own, own, r1_s.at[d], r1_r.at[f0], (br, tile_of((f0 + d) % n, g0)))

    def gather_bands_wait(d):
        f = (f0 + d) % n
        rc(bands.at[f], bands.at[f], r1_s.at[d], r1_r.at[f], (br, t)).wait_recv()

    for s in range(SLOTS):

        @pl.when(br != s)
        def _(s=s):
            rc(win.at[s], wall.at[f0, s], zw_s.at[s], zw_r.at[s], (br, t)).wait_recv()

    for d in range(1, n):
        gather_windows(d).start()

    @pl.when(is_local)
    def _():
        rc(bands.at[0], bands.at[f0], gr_s.at[0], gr_r.at[0], (br, t)).wait_recv()

    for d in range(1, n):
        gather_bands(d).start()

    fetches[4].wait()
    fetches[5].wait()
    fetch(6, cl_hbm, conv_ref).wait()
    zero = jnp.zeros((C, C), BF)
    for sft in range(3):
        for r in range(2):
            at = slice((r * 3 + sft) * C, (r * 3 + sft + 1) * C)
            for o in range(2):
                to = slice(o * C, (o + 1) * C)
                tap = r - o
                wlo[at, to] = conv_ref[tap, sft] if tap >= 0 else zero
                tap = r + 2 - o
                whi[at, to] = conv_ref[tap, sft] if tap <= 2 else zero

    def scatter_canvas(d):
        g = (g0 + d) % n
        return rc(canv.at[g], canv_in.at[g0], a2_s.at[d], a2_r.at[g0], (br, tile_of(f0, g)))

    def scatter_canvas_wait(d):
        g = (g0 + d) % n
        rc(canv.at[g], canv_in.at[g], a2_s.at[d], a2_r.at[g], (br, t)).wait_recv()

    def scatter_strips(d):
        g = (g0 + d) % n
        return rc(strip.at[g], strip_in.at[g0], r2_s.at[d], r2_r.at[g0], (br, tile_of(f0, g)))

    def scatter_strips_wait(d):
        g = (g0 + d) % n
        rc(strip.at[g], strip_in.at[g], r2_s.at[d], r2_r.at[g], (br, t)).wait_recv()

    for d in range(1, n):
        gather_windows_wait(d)
    pooled = jnp.zeros((GW, C), F32)
    for d in [*range(1, n), 0]:
        g = (g0 + d) % n
        pooled = jnp.zeros((GW, C), F32)
        for f in range(n):
            w = wall[f].reshape(GW, C)
            pooled = pooled + jnp.dot(pmat[g, f], w, preferred_element_type=F32)
        if d:
            canv[g] = pooled.astype(BF)
            scatter_canvas(d).start()

    for d in range(1, n):
        gather_bands_wait(d)
    own_strips = None
    block = SLOTS * WIN
    for d in [*range(1, n), 0]:
        g = (g0 + d) % n
        at = pl.ds(pl.multiple_of(g * block, WIN), block)
        cut = jnp.dot(smat[at], bands[...].reshape(n * GW, C), preferred_element_type=F32)
        own_strips = cut.astype(BF).reshape(SLOTS, WIN, C)
        if d:
            strip[g] = own_strips
            scatter_strips(d).start()

    def merged_copy():
        return rc(mine, rows.at[br + 1], m_s.at[0], m_r.at[br + 1], (last, t))

    def edge_up():
        return rc(mine, rows.at[ROWS + 1], m_s.at[1], m_r.at[ROWS + 1], (last, before))

    def edge_down():
        return rc(mine, rows.at[0], m_s.at[1], m_r.at[0], (last, after))

    for d in range(1, n):
        scatter_canvas_wait(d)
        pooled = pooled + canv_in[(g0 + d) % n].astype(F32)
    both = jnp.concatenate([bands[f0], pooled.astype(BF)], axis=1)
    merged = jnp.maximum(jnp.dot(both, mg_ref[...], preferred_element_type=F32), 0.0)
    mine[...] = merged.astype(BF)
    pl.when(is_local)(lambda: merged_copy().start())
    pl.when(first_up)(lambda: edge_up().start())
    pl.when(root_down)(lambda: edge_down().start())

    def crop_copy(d):
        b = (br + d) % ROWS
        return rc(total_strip.at[b], crop.at[br], zc_s.at[d], zc_r.at[br], (b, t))

    for d in range(1, n):
        scatter_strips_wait(d)
        own_strips = own_strips + strip_in[(g0 + d) % n]
    total_strip[0:SLOTS] = own_strips
    for d in range(1, ROWS):

        @pl.when((br + d) % ROWS != last)
        def _(d=d):
            crop_copy(d).start()

    def put(at, lanes, value, width):
        m = value.reshape(-1, width, C)
        col = iota((1, width, 1), 1)
        left = jnp.where(col == 0, 0.0, pltpu.roll(m, 1, 1))
        right = jnp.where(col == width - 1, 0.0, pltpu.roll(m, width - 1, 1))
        for sft, v in enumerate((left, m, right)):
            zbuf[at, lanes + sft * C : lanes + (sft + 1) * C] = v.reshape(-1, C).astype(BF)

    def conv_block(first, hi_first):
        lo = zbuf[first : first + 256]
        hi = zbuf[hi_first : hi_first + 256]
        res = jnp.dot(lo, wlo[...], preferred_element_type=F32)
        res = res + jnp.dot(hi, whi[...], preferred_element_type=F32)
        return res.astype(BF)

    @pl.when(is_local)
    def _():
        zbuf[0:S, 0 : 3 * C] = jnp.zeros((S, 3 * C), BF)
        zbuf[S // 2 * S : (S // 2 + 1) * S, 3 * C :] = jnp.zeros((S, 3 * C), BF)
        s1024 = iota((1024, 1), 0)
        target = (s1024 // S) * WIN + (((s1024 % S) * ww) >> 6)
        lhs = jnp.where(iota((1, 256), 1) == target, 1.0, 0.0).astype(BF)
        weight = ml_ref[...]
        crop[br] = total_strip[slot]
        for r in range(ROWS):

            @pl.when(br != r)
            def _(r=r):
                rc(total_strip.at[0], crop.at[r], zc_s.at[r], zc_r.at[r], (br, t)).wait_recv()

        strips = crop[...].reshape(ROWS * WIN, C)
        cu[...] = jnp.dot(lhs, strips, preferred_element_type=F32).astype(BF).reshape(ROWS, S, C)

        for b in range(S // 8):
            ups = []
            for i in range(8):
                r = (((b * 8 + i) * hh) >> 6) + top
                ups.append(cu[jnp.clip(r, 0, ROWS - 1)])
            both = jnp.concatenate(
                [x_ref[b * 8 * S : (b + 1) * 8 * S], jnp.concatenate(ups, axis=0)], axis=1
            )
            m = jnp.maximum(jnp.dot(both, weight, preferred_element_type=F32), 0.0)
            for i in range(8):
                pair = b * 4 + (i + 1) // 2
                at = slice(pair * S, (pair + 1) * S)
                put(at, 3 * C * ((i + 1) % 2), m[i * S : (i + 1) * S], S)

        for b in range(S // 8):
            res = conv_block(b * 256, b * 256 + S)
            for i in range(4):
                for o in range(2):
                    at = b * 512 + (2 * i + o) * S
                    out_ref[at : at + S] = res[i * S : (i + 1) * S, o * C : (o + 1) * C]

    @pl.when(is_root)
    def _():
        rows[ROWS] = mine[...]

        @pl.when(jnp.logical_not(has_before))
        def _():
            rows[0] = jnp.zeros((GW, C), BF)

        @pl.when(jnp.logical_not(has_after))
        def _():
            rows[ROWS + 1] = jnp.zeros((GW, C), BF)

        def wait(i):
            rc(mine, rows.at[i], m_s.at[0], m_r.at[i], (br, t)).wait_recv()

        here = set()
        done = set()
        for i in (16, 15, 1, 2, 13, 14, 3, 4, 11, 12, 5, 6, 9, 10, 0, 17, 7, 8):
            if i == 0:
                pl.when(has_before)(functools.partial(wait, 0))
            elif i == ROWS + 1:
                pl.when(has_after)(functools.partial(wait, ROWS + 1))
            elif i != ROWS:
                wait(i)
            put(slice(i // 2 * GW, (i // 2 + 1) * GW), 3 * C * (i % 2), rows[i].astype(F32), GW)
            here.add(i)
            for q in range(8):
                if q not in done and here >= {2 * q, 2 * q + 1, 2 * q + 2, 2 * q + 3}:
                    done.add(q)
                    res = conv_block(q * GW, (q + 1) * GW)
                    for o in range(2):
                        at = slice((2 * q + o) * GW, (2 * q + o + 1) * GW)
                        out_ref[at] = res[:, o * C : (o + 1) * C]

    @pl.when(is_root)
    def _():
        for r in far_first:
            row_copy(r).wait_send()

    @pl.when(is_local)
    def _():
        for d in range(1, ROWS):
            window_copy(d).wait_send()
        merged_copy().wait_send()

    for d in range(1, n):
        gather_windows(d).wait_send()
        gather_bands(d).wait_send()
        scatter_canvas(d).wait_send()
        scatter_strips(d).wait_send()
    for d in range(1, ROWS):

        @pl.when((br + d) % ROWS != last)
        def _(d=d):
            crop_copy(d).wait_send()

    pl.when(first_up)(lambda: edge_up().wait_send())
    pl.when(root_down)(lambda: edge_down().wait_send())


def run(n, features, merge_local, conv_local, merge_global, conv_global, offsets, sizes, owners):
    hbm = pl.BlockSpec(memory_space=pltpu.HBM)
    dma = pltpu.SemaphoreType.DMA

    def vm(*shape):
        return pltpu.VMEM(shape, BF)

    def sm(*shape):
        return pltpu.SMEM(shape, jnp.int32)

    tiles = n * n
    out = pl.pallas_call(
        functools.partial(kernel, n),
        out_shape=pltpu.VMEM((CELLS, C), BF),
        in_specs=[hbm] * 8,
        out_specs=pl.BlockSpec(memory_space=pltpu.VMEM),
        scratch_shapes=[
            vm(CELLS, C),
            vm(2 * C, C),
            vm(2 * C, C),
            vm(3, 3, C, C),
            sm(SLOTS, 2, tiles),
            sm(SLOTS, 2, tiles),
            sm(SLOTS, 1, tiles),
            vm(ROWS, WIN, C),
            vm(n, ROWS, WIN, C),
            vm(n, GW, C),
            vm(n * SLOTS * WIN, n * GW),
            vm(n, n, GW, GW),
            vm(n, SLOTS, WIN, C),
            vm(n, SLOTS, WIN, C),
            vm(n, GW, C),
            vm(n, GW, C),
            vm(ROWS, WIN, C),
            vm(ROWS, WIN, C),
            vm(ROWS + 2, GW, C),
            vm(GW, C),
            vm(ROWS, S, C),
            vm(9 * GW, 6 * C),
            vm(6 * C, 2 * C),
            vm(6 * C, 2 * C),
            dma((7,)),
            dma((ROWS,)),
            dma((1,)),
            dma((ROWS,)),
            dma((ROWS,)),
            dma((n,)),
            dma((n,)),
            dma((n,)),
            dma((n,)),
            dma((n,)),
            dma((n,)),
            dma((n,)),
            dma((n,)),
            dma((ROWS,)),
            dma((ROWS,)),
            dma((2,)),
            dma((ROWS + 2,)),
        ],
        compiler_params=pltpu.CompilerParams(
            collective_id=0, has_side_effects=True, vmem_limit_bytes=40 * 1024 * 1024
        ),
        name="glue",
    )(
        *(
            pltpu.with_memory_space_constraint(a, pltpu.HBM)
            for a in (
                features.reshape(CELLS, C),
                merge_local,
                conv_local,
                merge_global,
                conv_global,
                offsets.transpose(0, 2, 3, 1).reshape(SLOTS, 2, tiles),
                sizes.transpose(0, 2, 3, 1).reshape(SLOTS, 2, tiles),
                owners.transpose(0, 2, 1),
            )
        )
    )
    return out.reshape(features.shape)


def solution(mesh):
    n = 1
    while n * n < mesh.shape["tile"]:
        n += 1
    in_specs = (P("branch", "tile", None, None, None), P(), P(), P(), P(), P(), P(), P())
    out_specs = P("branch", "tile", None, None, None)
    return jax.shard_map(
        functools.partial(run, n),
        mesh=mesh,
        in_specs=in_specs,
        out_specs=out_specs,
        check_vma=False,
    )
```

```python
import functools

import jax
import jax.numpy as jnp
from jax import lax
from jax.experimental import pallas as pl
from jax.experimental.pallas import tpu as pltpu
from jax.sharding import PartitionSpec as P

MESH = pl.DeviceIdType.MESH
BF = jnp.bfloat16
F32 = jnp.float32
C = 128
S = 64
GW = 256
WIN = 16
CELLS = 4096
ROWS = 16
SLOTS = 15


def iota(shape, dim):
    return lax.broadcasted_iota(jnp.int32, shape, dim)


def kernel(
    n, x_hbm, ml_hbm, cl_hbm, mg_hbm, cg_hbm, off_hbm, size_hbm, own_hbm, out_ref,
    x_ref, ml_ref, mg_ref, conv_ref, off_ref, size_ref, own_ref,
    win, wall, bands, smat, pmat, strip, strip_in, canv, canv_in, total_strip, crop, rows, mine, cu, zbuf, wlo, whi,
    in_s, gr_s, gr_r, zw_s, zw_r, a1_s, a1_r, a2_s, a2_r, r1_s, r1_r, r2_s, r2_r, zc_s, zc_r, m_s, m_r,
):
    tiles = n * n
    peers = sorted(range(1, n), key=lambda d: -min(d, n - d))
    br = lax.axis_index("branch")
    t = lax.axis_index("tile")
    up = br % 2 == 1
    xx, yy = t // n, t % n
    f0 = jnp.where(up, xx, yy)
    g0 = jnp.where(up, yy, xx)
    last = ROWS - 1
    is_root = br == last
    is_local = br < last

    def tile_of(f, g):
        return jnp.where(up, f * n + g, g * n + f)

    def rc(src, dst, ss, rs, dev):
        return pltpu.make_async_remote_copy(
            src_ref=src, dst_ref=dst, send_sem=ss, recv_sem=rs, device_id=dev, device_id_type=MESH
        )

    barrier = pltpu.get_barrier_semaphore()

    def greet(b, tile):
        pl.semaphore_signal(barrier, inc=1, device_id=(b, tile), device_id_type=MESH)

    for b in (ROWS - 1, *range(ROWS - 1)):
        pl.when(br != b)(functools.partial(greet, b, t))
    for d in range(1, n):
        greet(br, ((xx + d) % n) * n + yy)
        greet(br, xx * n + (yy + d) % n)
    before = jnp.maximum(t - 1, 0)
    after = jnp.minimum(t + 1, tiles - 1)
    has_before, has_after = t > 0, t < tiles - 1
    is_first = br == 0
    first_up = jnp.logical_and(is_first, has_before)
    root_up = jnp.logical_and(is_root, has_before)
    root_down = jnp.logical_and(is_root, has_after)

    @pl.when(first_up)
    def _():
        greet(last, before)

    @pl.when(root_up)
    def _():
        greet(last, before)

    @pl.when(root_down)
    def _():
        greet(0, after)
        greet(last, after)

    def fetch(i, src, dst):
        return pltpu.make_async_copy(src, dst, in_s.at[i])

    fetches = [
        fetch(0, size_hbm, size_ref),
        fetch(1, off_hbm, off_ref),
        fetch(2, own_hbm, own_ref),
        fetch(3, x_hbm, x_ref),
        fetch(4, mg_hbm, mg_ref),
        fetch(5, ml_hbm, ml_ref),
    ]
    for f in fetches:
        f.start()
    pl.when(is_root)(lambda: fetch(6, cg_hbm, conv_ref).start())
    pl.when(is_local)(lambda: fetch(6, cl_hbm, conv_ref).start())
    for f in fetches[:4]:
        f.wait()

    slot = jnp.minimum(br, last - 1)
    top = off_ref[slot, 0, t]
    hh = size_ref[slot, 0, t]
    ww = size_ref[slot, 1, t]

    @pl.when(is_local)
    def _():
        sub = iota((256, 1), 0)
        sub_row = sub // WIN - top
        sub_col = sub % WIN
        lane64 = iota((1, 128), 1)
        inside = lane64 < S
        row_hits = jnp.where(jnp.logical_and(inside, ((lane64 * hh) >> 6) == sub_row), 1.0, 0.0)
        col_hits = jnp.where(jnp.logical_and(inside, ((lane64 * ww) >> 6) == sub_col), 1.0, 0.0)
        counts = jnp.sum(row_hits, axis=1, keepdims=True) * jnp.sum(col_hits, axis=1, keepdims=True)
        wide = 1024
        lane = iota((1, wide), 1)
        cols = jnp.where((((lane % S) * ww) >> 6) == sub_col, 1.0, 0.0)

        def pool_step(step, acc):
            rows_at = ((step * (wide // S) + lane // S) * hh) >> 6
            lhs = jnp.where(rows_at == sub_row, cols, 0.0).astype(BF)
            rhs = x_ref[pl.ds(pl.multiple_of(step * wide, wide), wide)]
            return acc + jnp.dot(lhs, rhs, preferred_element_type=F32)

        total = lax.fori_loop(0, CELLS // wide, pool_step, jnp.zeros((256, C), F32))
        win[...] = (total / jnp.maximum(counts, 1.0)).astype(BF).reshape(ROWS, WIN, C)

    count = ROWS - 1 + 2 * (n - 1)
    extra = jnp.where(first_up, 1, 0) + jnp.where(root_up, 1, 0) + jnp.where(root_down, 2, 0)
    pl.semaphore_wait(barrier, count + extra)

    def row_copy(r):
        f = xx if r % 2 else yy
        return rc(x_ref.at[r * GW : (r + 1) * GW], bands.at[f], gr_s.at[r], gr_r.at[0], (r, t))

    far_first = (8, 6, 9, 7, 10, 4, 11, 5, 12, 2, 13, 3, 0, 1, 14)

    @pl.when(is_root)
    def _():
        for r in far_first:
            row_copy(r).start()
        bands[f0] = x_ref[last * GW : (last + 1) * GW]

    def window_copy(d):
        r = (br + d) % ROWS
        f = jnp.where(r % 2 == 1, xx, yy)
        return rc(win.at[r], wall.at[f, br], zw_s.at[d], zw_r.at[br], (r, t))

    @pl.when(is_local)
    def _():
        for d in range(1, ROWS):
            window_copy(d).start()
        wall[f0, slot] = win[br]

    def axes_of(tile):
        high, low = lax.div(tile, n), lax.rem(tile, n)
        return jnp.where(up, high, low), jnp.where(up, low, high)

    diag = iota((WIN, n * GW), 1) - iota((WIN, n * GW), 0)

    def strip_step(g, carry):
        tile = tile_of(f0, g)
        for s in range(SLOTS):
            f_own, g_own = axes_of(own_ref[s, 0, tile])
            target = jnp.where(g_own == g0, f_own * GW + off_ref[s, 1, tile], -(n + 1) * GW)
            at = pl.ds(pl.multiple_of((g * SLOTS + s) * WIN, WIN), WIN)
            smat[at] = jnp.where(diag == target, 1.0, 0.0).astype(BF)
        return carry

    piece = iota((1, GW), 1) // WIN
    place = iota((1, GW), 1) % WIN
    column = iota((GW, 1), 0)

    def place_step(f, carry):
        tile = tile_of(f, g0)
        target = jnp.full((1, GW), -(n + 1) * GW, jnp.int32)
        for s in range(SLOTS):
            f_own, g_own = axes_of(own_ref[s, 0, tile])
            here = jnp.where(f_own == f0, g_own * GW + off_ref[s, 1, tile], -(n + 1) * GW)
            target = jnp.where(piece == s, here, target)
        target = target + place
        for g in range(n):
            pmat[g, f] = jnp.where(column + g * GW == target, 1.0, 0.0).astype(BF)
        wall[f, SLOTS] = jnp.zeros((WIN, C), BF)
        return carry

    lax.fori_loop(0, n, place_step, 0)
    lax.fori_loop(0, n, strip_step, 0)

    def gather_windows(d):
        own = wall.at[f0, 0:SLOTS]
        return rc(own, own, a1_s.at[d], a1_r.at[f0], (br, tile_of((f0 + d) % n, g0)))

    def gather_windows_wait(d):
        f = (f0 + d) % n
        part = wall.at[f, 0:SLOTS]
        rc(part, part, a1_s.at[d], a1_r.at[f], (br, t)).wait_recv()

    def gather_bands(d):
        own = bands.at[f0]
        return rc(own, own, r1_s.at[d], r1_r.at[f0], (br, tile_of((f0 + d) % n, g0)))

    def gather_bands_wait(d):
        f = (f0 + d) % n
        rc(bands.at[f], bands.at[f], r1_s.at[d], r1_r.at[f], (br, t)).wait_recv()

    @pl.when(is_local)
    def _():
        rc(bands.at[0], bands.at[f0], gr_s.at[0], gr_r.at[0], (br, t)).wait_recv()

    for d in peers:
        gather_bands(d).start()

    for s in range(SLOTS):

        @pl.when(br != s)
        def _(s=s):
            rc(win.at[s], wall.at[f0, s], zw_s.at[s], zw_r.at[s], (br, t)).wait_recv()

    for d in peers:
        gather_windows(d).start()

    fetches[4].wait()
    fetches[5].wait()
    fetch(6, cl_hbm, conv_ref).wait()
    zero = jnp.zeros((C, C), BF)
    for sft in range(3):
        for r in range(2):
            at = slice((r * 3 + sft) * C, (r * 3 + sft + 1) * C)
            for o in range(2):
                to = slice(o * C, (o + 1) * C)
                tap = r - o
                wlo[at, to] = conv_ref[tap, sft] if tap >= 0 else zero
                tap = r + 2 - o
                whi[at, to] = conv_ref[tap, sft] if tap <= 2 else zero

    def scatter_canvas(d):
        g = (g0 + d) % n
        return rc(canv.at[g], canv_in.at[g0], a2_s.at[d], a2_r.at[g0], (br, tile_of(f0, g)))

    def scatter_canvas_wait(d):
        g = (g0 + d) % n
        rc(canv.at[g], canv_in.at[g], a2_s.at[d], a2_r.at[g], (br, t)).wait_recv()

    def scatter_strips(d):
        g = (g0 + d) % n
        return rc(strip.at[g], strip_in.at[g0], r2_s.at[d], r2_r.at[g0], (br, tile_of(f0, g)))

    def scatter_strips_wait(d):
        g = (g0 + d) % n
        rc(strip.at[g], strip_in.at[g], r2_s.at[d], r2_r.at[g], (br, t)).wait_recv()

    for d in range(1, n):
        gather_bands_wait(d)
    own_strips = None
    block = SLOTS * WIN
    for d in [*peers, 0]:
        g = (g0 + d) % n
        at = pl.ds(pl.multiple_of(g * block, WIN), block)
        cut = jnp.dot(smat[at], bands[...].reshape(n * GW, C), preferred_element_type=F32)
        own_strips = cut.astype(BF).reshape(SLOTS, WIN, C)
        if d:
            strip[g] = own_strips
            scatter_strips(d).start()

    for d in range(1, n):
        gather_windows_wait(d)
    pooled = jnp.zeros((GW, C), F32)
    for d in [*peers, 0]:
        g = (g0 + d) % n
        pooled = jnp.zeros((GW, C), F32)
        for f in range(n):
            w = wall[f].reshape(GW, C)
            pooled = pooled + jnp.dot(pmat[g, f], w, preferred_element_type=F32)
        if d:
            canv[g] = pooled.astype(BF)
            scatter_canvas(d).start()

    def crop_copy(b):
        return rc(total_strip.at[b], crop.at[br], zc_s.at[b], zc_r.at[br], (b, t))

    for d in range(1, n):
        scatter_strips_wait(d)
        own_strips = own_strips + strip_in[(g0 + d) % n]
    total_strip[0:SLOTS] = own_strips
    for b in (1, 3, 0, 2, 5, 4, 7, 6, *range(8, SLOTS)):

        @pl.when(br != b)
        def _(b=b):
            crop_copy(b).start()

    def merged_copy():
        return rc(mine, rows.at[br + 1], m_s.at[0], m_r.at[br + 1], (last, t))

    def edge_up():
        return rc(mine, rows.at[ROWS + 1], m_s.at[1], m_r.at[ROWS + 1], (last, before))

    def edge_down():
        return rc(mine, rows.at[0], m_s.at[1], m_r.at[0], (last, after))

    for d in range(1, n):
        scatter_canvas_wait(d)
        pooled = pooled + canv_in[(g0 + d) % n].astype(F32)
    both = jnp.concatenate([bands[f0], pooled.astype(BF)], axis=1)
    merged = jnp.maximum(jnp.dot(both, mg_ref[...], preferred_element_type=F32), 0.0)
    mine[...] = merged.astype(BF)
    pl.when(is_local)(lambda: merged_copy().start())
    pl.when(first_up)(lambda: edge_up().start())
    pl.when(root_down)(lambda: edge_down().start())

    def put(at, lanes, value, width):
        m = value.reshape(-1, width, C)
        col = iota((1, width, 1), 1)
        left = jnp.where(col == 0, 0.0, pltpu.roll(m, 1, 1))
        right = jnp.where(col == width - 1, 0.0, pltpu.roll(m, width - 1, 1))
        for sft, v in enumerate((left, m, right)):
            zbuf[at, lanes + sft * C : lanes + (sft + 1) * C] = v.reshape(-1, C).astype(BF)

    def conv_block(first, hi_first):
        lo = zbuf[first : first + 256]
        hi = zbuf[hi_first : hi_first + 256]
        res = jnp.dot(lo, wlo[...], preferred_element_type=F32)
        res = res + jnp.dot(hi, whi[...], preferred_element_type=F32)
        return res.astype(BF)

    @pl.when(is_local)
    def _():
        zbuf[0:S, 0 : 3 * C] = jnp.zeros((S, 3 * C), BF)
        zbuf[S // 2 * S : (S // 2 + 1) * S, 3 * C :] = jnp.zeros((S, 3 * C), BF)
        s256 = iota((4 * S, 1), 0)
        target = (s256 // S) * WIN + (((s256 % S) * ww) >> 6)
        lhs = jnp.where(iota((1, 4 * WIN), 1) == target, 1.0, 0.0).astype(BF)
        weight = ml_ref[...]
        crop[br] = total_strip[slot]
        order = sorted(range(ROWS), key=lambda d: min(d, ROWS - d))
        for i in range(0, ROWS, 4):
            part = [(br + d) % ROWS for d in order[i : i + 4]]
            for d, r in zip(order[i : i + 4], part):
                if d:
                    rc(
                        total_strip.at[0], crop.at[r], zc_s.at[d], zc_r.at[r], (br, t)
                    ).wait_recv()
            strips = jnp.concatenate([crop[r] for r in part], axis=0)
            wide_rows = jnp.dot(lhs, strips, preferred_element_type=F32).astype(BF)
            for j, r in enumerate(part):
                cu[r] = wide_rows[j * S : (j + 1) * S]

        for b in range(S // 8):
            ups = []
            for i in range(8):
                r = (((b * 8 + i) * hh) >> 6) + top
                ups.append(cu[jnp.clip(r, 0, ROWS - 1)])
            both = jnp.concatenate(
                [x_ref[b * 8 * S : (b + 1) * 8 * S], jnp.concatenate(ups, axis=0)], axis=1
            )
            m = jnp.maximum(jnp.dot(both, weight, preferred_element_type=F32), 0.0)
            for i in range(8):
                pair = b * 4 + (i + 1) // 2
                at = slice(pair * S, (pair + 1) * S)
                put(at, 3 * C * ((i + 1) % 2), m[i * S : (i + 1) * S], S)

        for b in range(S // 8):
            res = conv_block(b * 256, b * 256 + S)
            for i in range(4):
                for o in range(2):
                    at = b * 512 + (2 * i + o) * S
                    out_ref[at : at + S] = res[i * S : (i + 1) * S, o * C : (o + 1) * C]

    @pl.when(is_root)
    def _():
        rows[ROWS] = mine[...]

        @pl.when(jnp.logical_not(has_before))
        def _():
            rows[0] = jnp.zeros((GW, C), BF)

        @pl.when(jnp.logical_not(has_after))
        def _():
            rows[ROWS + 1] = jnp.zeros((GW, C), BF)

        def wait(i):
            rc(mine, rows.at[i], m_s.at[0], m_r.at[i], (br, t)).wait_recv()

        here = set()
        done = set()
        for i in (16, 15, 1, 2, 13, 14, 3, 4, 11, 12, 5, 6, 9, 10, 0, 17, 7, 8):
            if i == 0:
                pl.when(has_before)(functools.partial(wait, 0))
            elif i == ROWS + 1:
                pl.when(has_after)(functools.partial(wait, ROWS + 1))
            elif i != ROWS:
                wait(i)
            put(slice(i // 2 * GW, (i // 2 + 1) * GW), 3 * C * (i % 2), rows[i].astype(F32), GW)
            here.add(i)
            for q in range(8):
                if q not in done and here >= {2 * q, 2 * q + 1, 2 * q + 2, 2 * q + 3}:
                    done.add(q)
                    res = conv_block(q * GW, (q + 1) * GW)
                    for o in range(2):
                        at = slice((2 * q + o) * GW, (2 * q + o + 1) * GW)
                        out_ref[at] = res[:, o * C : (o + 1) * C]

    @pl.when(is_root)
    def _():
        for r in far_first:
            row_copy(r).wait_send()

    @pl.when(is_local)
    def _():
        for d in range(1, ROWS):
            window_copy(d).wait_send()
        merged_copy().wait_send()

    for d in range(1, n):
        gather_windows(d).wait_send()
        gather_bands(d).wait_send()
        scatter_canvas(d).wait_send()
        scatter_strips(d).wait_send()
    for b in range(SLOTS):

        @pl.when(br != b)
        def _(b=b):
            crop_copy(b).wait_send()

    pl.when(first_up)(lambda: edge_up().wait_send())
    pl.when(root_down)(lambda: edge_down().wait_send())


def run(n, features, merge_local, conv_local, merge_global, conv_global, offsets, sizes, owners):
    hbm = pl.BlockSpec(memory_space=pltpu.HBM)
    dma = pltpu.SemaphoreType.DMA

    def vm(*shape):
        return pltpu.VMEM(shape, BF)

    def sm(*shape):
        return pltpu.SMEM(shape, jnp.int32)

    tiles = n * n
    out = pl.pallas_call(
        functools.partial(kernel, n),
        out_shape=pltpu.VMEM((CELLS, C), BF),
        in_specs=[hbm] * 8,
        out_specs=pl.BlockSpec(memory_space=pltpu.VMEM),
        scratch_shapes=[
            vm(CELLS, C),
            vm(2 * C, C),
            vm(2 * C, C),
            vm(3, 3, C, C),
            sm(SLOTS, 2, tiles),
            sm(SLOTS, 2, tiles),
            sm(SLOTS, 1, tiles),
            vm(ROWS, WIN, C),
            vm(n, ROWS, WIN, C),
            vm(n, GW, C),
            vm(n * SLOTS * WIN, n * GW),
            vm(n, n, GW, GW),
            vm(n, SLOTS, WIN, C),
            vm(n, SLOTS, WIN, C),
            vm(n, GW, C),
            vm(n, GW, C),
            vm(ROWS, WIN, C),
            vm(ROWS, WIN, C),
            vm(ROWS + 2, GW, C),
            vm(GW, C),
            vm(ROWS, S, C),
            vm(9 * GW, 6 * C),
            vm(6 * C, 2 * C),
            vm(6 * C, 2 * C),
            dma((7,)),
            dma((ROWS,)),
            dma((1,)),
            dma((ROWS,)),
            dma((ROWS,)),
            dma((n,)),
            dma((n,)),
            dma((n,)),
            dma((n,)),
            dma((n,)),
            dma((n,)),
            dma((n,)),
            dma((n,)),
            dma((ROWS,)),
            dma((ROWS,)),
            dma((2,)),
            dma((ROWS + 2,)),
        ],
        compiler_params=pltpu.CompilerParams(
            collective_id=0, has_side_effects=True, vmem_limit_bytes=40 * 1024 * 1024
        ),
        name="glue",
    )(
        *(
            pltpu.with_memory_space_constraint(a, pltpu.HBM)
            for a in (
                features.reshape(CELLS, C),
                merge_local,
                conv_local,
                merge_global,
                conv_global,
                offsets.transpose(0, 2, 3, 1).reshape(SLOTS, 2, tiles),
                sizes.transpose(0, 2, 3, 1).reshape(SLOTS, 2, tiles),
                owners.transpose(0, 2, 1),
            )
        )
    )
    return out.reshape(features.shape)


def solution(mesh):
    n = 1
    while n * n < mesh.shape["tile"]:
        n += 1
    in_specs = (P("branch", "tile", None, None, None), P(), P(), P(), P(), P(), P(), P())
    out_specs = P("branch", "tile", None, None, None)
    return jax.shard_map(
        functools.partial(run, n),
        mesh=mesh,
        in_specs=in_specs,
        out_specs=out_specs,
        check_vma=False,
    )
```

```python
import functools

import jax
import jax.numpy as jnp
from jax import lax
from jax.experimental import pallas as pl
from jax.experimental.pallas import tpu as pltpu
from jax.sharding import PartitionSpec as P

MESH = pl.DeviceIdType.MESH
BF = jnp.bfloat16
F32 = jnp.float32
C = 128
S = 64
GW = 256
WIN = 16
CELLS = 4096
ROWS = 16
SLOTS = 15


def iota(shape, dim):
    return lax.broadcasted_iota(jnp.int32, shape, dim)


def kernel(
    n, x_hbm, ml_hbm, cl_hbm, mg_hbm, cg_hbm, off_hbm, size_hbm, own_hbm, out_ref,
    x_ref, ml_ref, mg_ref, conv_ref, off_ref, size_ref, own_ref,
    win, wall, bands, smat, pmat, strip, strip_in, canv, canv_in, total_strip, crop, rows, mine, cu, zbuf, wlo, whi,
    in_s, gr_s, gr_r, zw_s, zw_r, a1_s, a1_r, a2_s, a2_r, r1_s, r1_r, r2_s, r2_r, zc_s, zc_r, m_s, m_r,
):
    tiles = n * n
    peers = sorted(range(1, n), key=lambda d: -min(d, n - d))
    br = lax.axis_index("branch")
    t = lax.axis_index("tile")
    up = br % 2 == 1
    xx, yy = t // n, t % n
    f0 = jnp.where(up, xx, yy)
    g0 = jnp.where(up, yy, xx)
    last = ROWS - 1
    is_root = br == last
    is_local = br < last

    def tile_of(f, g):
        return jnp.where(up, f * n + g, g * n + f)

    def rc(src, dst, ss, rs, dev):
        return pltpu.make_async_remote_copy(
            src_ref=src, dst_ref=dst, send_sem=ss, recv_sem=rs, device_id=dev, device_id_type=MESH
        )

    barrier = pltpu.get_barrier_semaphore()

    def greet(b, tile):
        pl.semaphore_signal(barrier, inc=1, device_id=(b, tile), device_id_type=MESH)

    for b in (ROWS - 1, *range(ROWS - 1)):
        pl.when(br != b)(functools.partial(greet, b, t))
    for d in range(1, n):
        greet(br, ((xx + d) % n) * n + yy)
        greet(br, xx * n + (yy + d) % n)
    before = jnp.maximum(t - 1, 0)
    after = jnp.minimum(t + 1, tiles - 1)
    has_before, has_after = t > 0, t < tiles - 1
    is_first = br == 0
    first_up = jnp.logical_and(is_first, has_before)
    root_up = jnp.logical_and(is_root, has_before)
    root_down = jnp.logical_and(is_root, has_after)

    @pl.when(first_up)
    def _():
        greet(last, before)

    @pl.when(root_up)
    def _():
        greet(last, before)

    @pl.when(root_down)
    def _():
        greet(0, after)
        greet(last, after)

    def fetch(i, src, dst):
        return pltpu.make_async_copy(src, dst, in_s.at[i])

    fetches = [
        fetch(0, size_hbm, size_ref),
        fetch(1, off_hbm, off_ref),
        fetch(2, own_hbm, own_ref),
        fetch(3, x_hbm, x_ref),
        fetch(4, mg_hbm, mg_ref),
        fetch(5, ml_hbm, ml_ref),
    ]
    for f in fetches:
        f.start()
    pl.when(is_root)(lambda: fetch(6, cg_hbm, conv_ref).start())
    pl.when(is_local)(lambda: fetch(6, cl_hbm, conv_ref).start())
    for f in fetches[:4]:
        f.wait()

    slot = jnp.minimum(br, last - 1)
    top = off_ref[slot, 0, t]
    hh = size_ref[slot, 0, t]
    ww = size_ref[slot, 1, t]

    @pl.when(is_local)
    def _():
        sub = iota((256, 1), 0)
        sub_row = sub // WIN - top
        sub_col = sub % WIN
        lane64 = iota((1, 128), 1)
        inside = lane64 < S
        row_hits = jnp.where(jnp.logical_and(inside, ((lane64 * hh) >> 6) == sub_row), 1.0, 0.0)
        col_hits = jnp.where(jnp.logical_and(inside, ((lane64 * ww) >> 6) == sub_col), 1.0, 0.0)
        counts = jnp.sum(row_hits, axis=1, keepdims=True) * jnp.sum(col_hits, axis=1, keepdims=True)
        wide = 1024
        lane = iota((1, wide), 1)
        cols = jnp.where((((lane % S) * ww) >> 6) == sub_col, 1.0, 0.0)

        def pool_step(step, acc):
            rows_at = ((step * (wide // S) + lane // S) * hh) >> 6
            lhs = jnp.where(rows_at == sub_row, cols, 0.0).astype(BF)
            rhs = x_ref[pl.ds(pl.multiple_of(step * wide, wide), wide)]
            return acc + jnp.dot(lhs, rhs, preferred_element_type=F32)

        total = lax.fori_loop(0, CELLS // wide, pool_step, jnp.zeros((256, C), F32))
        win[...] = (total / jnp.maximum(counts, 1.0)).astype(BF).reshape(ROWS, WIN, C)

    count = ROWS - 1 + 2 * (n - 1)
    extra = jnp.where(first_up, 1, 0) + jnp.where(root_up, 1, 0) + jnp.where(root_down, 2, 0)
    pl.semaphore_wait(barrier, count + extra)

    def row_copy(r):
        f = xx if r % 2 else yy
        return rc(x_ref.at[r * GW : (r + 1) * GW], bands.at[f], gr_s.at[r], gr_r.at[0], (r, t))

    far_first = (8, 6, 9, 7, 10, 4, 11, 5, 12, 2, 13, 3, 0, 1, 14)

    @pl.when(is_root)
    def _():
        for r in far_first:
            row_copy(r).start()
        bands[f0] = x_ref[last * GW : (last + 1) * GW]

    def window_copy(d):
        r = (br + d) % ROWS
        f = jnp.where(r % 2 == 1, xx, yy)
        return rc(win.at[r], wall.at[f, br], zw_s.at[d], zw_r.at[br], (r, t))

    @pl.when(is_local)
    def _():
        for d in range(1, ROWS):
            window_copy(d).start()
        wall[f0, slot] = win[br]

    def axes_of(tile):
        high, low = lax.div(tile, n), lax.rem(tile, n)
        return jnp.where(up, high, low), jnp.where(up, low, high)

    diag = iota((WIN, n * GW), 1) - iota((WIN, n * GW), 0)

    def strip_step(g, carry):
        tile = tile_of(f0, g)
        for s in range(SLOTS):
            f_own, g_own = axes_of(own_ref[s, 0, tile])
            target = jnp.where(g_own == g0, f_own * GW + off_ref[s, 1, tile], -(n + 1) * GW)
            at = pl.ds(pl.multiple_of((g * SLOTS + s) * WIN, WIN), WIN)
            smat[at] = jnp.where(diag == target, 1.0, 0.0).astype(BF)
        return carry

    piece = iota((1, GW), 1) // WIN
    place = iota((1, GW), 1) % WIN
    column = iota((GW, 1), 0)

    def place_step(f, carry):
        tile = tile_of(f, g0)
        target = jnp.full((1, GW), -(n + 1) * GW, jnp.int32)
        for s in range(SLOTS):
            f_own, g_own = axes_of(own_ref[s, 0, tile])
            here = jnp.where(f_own == f0, g_own * GW + off_ref[s, 1, tile], -(n + 1) * GW)
            target = jnp.where(piece == s, here, target)
        target = target + place
        for g in range(n):
            pmat[g, f] = jnp.where(column + g * GW == target, 1.0, 0.0).astype(BF)
        wall[f, SLOTS] = jnp.zeros((WIN, C), BF)
        return carry


    def gather_windows(d):
        own = wall.at[f0, 0:SLOTS]
        return rc(own, own, a1_s.at[d], a1_r.at[f0], (br, tile_of((f0 + d) % n, g0)))

    def gather_windows_wait(d):
        f = (f0 + d) % n
        part = wall.at[f, 0:SLOTS]
        rc(part, part, a1_s.at[d], a1_r.at[f], (br, t)).wait_recv()

    def gather_bands(d):
        own = bands.at[f0]
        return rc(own, own, r1_s.at[d], r1_r.at[f0], (br, tile_of((f0 + d) % n, g0)))

    def gather_bands_wait(d):
        f = (f0 + d) % n
        rc(bands.at[f], bands.at[f], r1_s.at[d], r1_r.at[f], (br, t)).wait_recv()

    @pl.when(is_local)
    def _():
        rc(bands.at[0], bands.at[f0], gr_s.at[0], gr_r.at[0], (br, t)).wait_recv()

    for d in peers:
        gather_bands(d).start()

    lax.fori_loop(0, n, place_step, 0)
    lax.fori_loop(0, n, strip_step, 0)

    for s in range(SLOTS):

        @pl.when(br != s)
        def _(s=s):
            rc(win.at[s], wall.at[f0, s], zw_s.at[s], zw_r.at[s], (br, t)).wait_recv()

    for d in peers:
        gather_windows(d).start()

    fetches[4].wait()
    fetches[5].wait()
    fetch(6, cl_hbm, conv_ref).wait()
    zero = jnp.zeros((C, C), BF)
    for sft in range(3):
        for r in range(2):
            at = slice((r * 3 + sft) * C, (r * 3 + sft + 1) * C)
            for o in range(2):
                to = slice(o * C, (o + 1) * C)
                tap = r - o
                wlo[at, to] = conv_ref[tap, sft] if tap >= 0 else zero
                tap = r + 2 - o
                whi[at, to] = conv_ref[tap, sft] if tap <= 2 else zero

    def scatter_canvas(d):
        g = (g0 + d) % n
        return rc(canv.at[g], canv_in.at[g0], a2_s.at[d], a2_r.at[g0], (br, tile_of(f0, g)))

    def scatter_canvas_wait(d):
        g = (g0 + d) % n
        rc(canv.at[g], canv_in.at[g], a2_s.at[d], a2_r.at[g], (br, t)).wait_recv()

    def scatter_strips(d):
        g = (g0 + d) % n
        return rc(strip.at[g], strip_in.at[g0], r2_s.at[d], r2_r.at[g0], (br, tile_of(f0, g)))

    def scatter_strips_wait(d):
        g = (g0 + d) % n
        rc(strip.at[g], strip_in.at[g], r2_s.at[d], r2_r.at[g], (br, t)).wait_recv()

    for d in range(1, n):
        gather_bands_wait(d)
    own_strips = None
    block = SLOTS * WIN
    for d in [*peers, 0]:
        g = (g0 + d) % n
        at = pl.ds(pl.multiple_of(g * block, WIN), block)
        cut = jnp.dot(smat[at], bands[...].reshape(n * GW, C), preferred_element_type=F32)
        own_strips = cut.astype(BF).reshape(SLOTS, WIN, C)
        if d:
            strip[g] = own_strips
            scatter_strips(d).start()

    for d in range(1, n):
        gather_windows_wait(d)
    pooled = jnp.zeros((GW, C), F32)
    for d in [*peers, 0]:
        g = (g0 + d) % n
        pooled = jnp.zeros((GW, C), F32)
        for f in range(n):
            w = wall[f].reshape(GW, C)
            pooled = pooled + jnp.dot(pmat[g, f], w, preferred_element_type=F32)
        if d:
            canv[g] = pooled.astype(BF)
            scatter_canvas(d).start()

    def crop_copy(b):
        return rc(total_strip.at[b], crop.at[br], zc_s.at[b], zc_r.at[br], (b, t))

    for d in range(1, n):
        scatter_strips_wait(d)
        own_strips = own_strips + strip_in[(g0 + d) % n]
    total_strip[0:SLOTS] = own_strips
    for b in (1, 3, 0, 2, 5, 4, 7, 6, *range(8, SLOTS)):

        @pl.when(br != b)
        def _(b=b):
            crop_copy(b).start()

    def merged_copy():
        return rc(mine, rows.at[br + 1], m_s.at[0], m_r.at[br + 1], (last, t))

    def edge_up():
        return rc(mine, rows.at[ROWS + 1], m_s.at[1], m_r.at[ROWS + 1], (last, before))

    def edge_down():
        return rc(mine, rows.at[0], m_s.at[1], m_r.at[0], (last, after))

    for d in range(1, n):
        scatter_canvas_wait(d)
        pooled = pooled + canv_in[(g0 + d) % n].astype(F32)
    both = jnp.concatenate([bands[f0], pooled.astype(BF)], axis=1)
    merged = jnp.maximum(jnp.dot(both, mg_ref[...], preferred_element_type=F32), 0.0)
    mine[...] = merged.astype(BF)
    pl.when(is_local)(lambda: merged_copy().start())
    pl.when(first_up)(lambda: edge_up().start())
    pl.when(root_down)(lambda: edge_down().start())

    def put(at, lanes, value, width):
        m = value.reshape(-1, width, C)
        col = iota((1, width, 1), 1)
        left = jnp.where(col == 0, 0.0, pltpu.roll(m, 1, 1))
        right = jnp.where(col == width - 1, 0.0, pltpu.roll(m, width - 1, 1))
        for sft, v in enumerate((left, m, right)):
            zbuf[at, lanes + sft * C : lanes + (sft + 1) * C] = v.reshape(-1, C).astype(BF)

    def conv_block(first, hi_first):
        lo = zbuf[first : first + 256]
        hi = zbuf[hi_first : hi_first + 256]
        res = jnp.dot(lo, wlo[...], preferred_element_type=F32)
        res = res + jnp.dot(hi, whi[...], preferred_element_type=F32)
        return res.astype(BF)

    @pl.when(is_local)
    def _():
        zbuf[0:S, 0 : 3 * C] = jnp.zeros((S, 3 * C), BF)
        zbuf[S // 2 * S : (S // 2 + 1) * S, 3 * C :] = jnp.zeros((S, 3 * C), BF)
        s256 = iota((4 * S, 1), 0)
        target = (s256 // S) * WIN + (((s256 % S) * ww) >> 6)
        lhs = jnp.where(iota((1, 4 * WIN), 1) == target, 1.0, 0.0).astype(BF)
        weight = ml_ref[...]
        crop[br] = total_strip[slot]
        order = sorted(range(ROWS), key=lambda d: min(d, ROWS - d))
        for i in range(0, ROWS, 4):
            part = [(br + d) % ROWS for d in order[i : i + 4]]
            for d, r in zip(order[i : i + 4], part):
                if d:
                    rc(
                        total_strip.at[0], crop.at[r], zc_s.at[d], zc_r.at[r], (br, t)
                    ).wait_recv()
            strips = jnp.concatenate([crop[r] for r in part], axis=0)
            wide_rows = jnp.dot(lhs, strips, preferred_element_type=F32).astype(BF)
            for j, r in enumerate(part):
                cu[r] = wide_rows[j * S : (j + 1) * S]

        for b in range(S // 8):
            ups = []
            for i in range(8):
                r = (((b * 8 + i) * hh) >> 6) + top
                ups.append(cu[jnp.clip(r, 0, ROWS - 1)])
            both = jnp.concatenate(
                [x_ref[b * 8 * S : (b + 1) * 8 * S], jnp.concatenate(ups, axis=0)], axis=1
            )
            m = jnp.maximum(jnp.dot(both, weight, preferred_element_type=F32), 0.0)
            for i in range(8):
                pair = b * 4 + (i + 1) // 2
                at = slice(pair * S, (pair + 1) * S)
                put(at, 3 * C * ((i + 1) % 2), m[i * S : (i + 1) * S], S)

        for b in range(S // 8):
            res = conv_block(b * 256, b * 256 + S)
            for i in range(4):
                for o in range(2):
                    at = b * 512 + (2 * i + o) * S
                    out_ref[at : at + S] = res[i * S : (i + 1) * S, o * C : (o + 1) * C]

    @pl.when(is_root)
    def _():
        rows[ROWS] = mine[...]

        @pl.when(jnp.logical_not(has_before))
        def _():
            rows[0] = jnp.zeros((GW, C), BF)

        @pl.when(jnp.logical_not(has_after))
        def _():
            rows[ROWS + 1] = jnp.zeros((GW, C), BF)

        def wait(i):
            rc(mine, rows.at[i], m_s.at[0], m_r.at[i], (br, t)).wait_recv()

        here = set()
        done = set()
        for i in (16, 15, 1, 2, 13, 14, 3, 4, 11, 12, 5, 6, 9, 10, 0, 17, 7, 8):
            if i == 0:
                pl.when(has_before)(functools.partial(wait, 0))
            elif i == ROWS + 1:
                pl.when(has_after)(functools.partial(wait, ROWS + 1))
            elif i != ROWS:
                wait(i)
            put(slice(i // 2 * GW, (i // 2 + 1) * GW), 3 * C * (i % 2), rows[i].astype(F32), GW)
            here.add(i)
            for q in range(8):
                if q not in done and here >= {2 * q, 2 * q + 1, 2 * q + 2, 2 * q + 3}:
                    done.add(q)
                    res = conv_block(q * GW, (q + 1) * GW)
                    for o in range(2):
                        at = slice((2 * q + o) * GW, (2 * q + o + 1) * GW)
                        out_ref[at] = res[:, o * C : (o + 1) * C]

    @pl.when(is_root)
    def _():
        for r in far_first:
            row_copy(r).wait_send()

    @pl.when(is_local)
    def _():
        for d in range(1, ROWS):
            window_copy(d).wait_send()
        merged_copy().wait_send()

    for d in range(1, n):
        gather_windows(d).wait_send()
        gather_bands(d).wait_send()
        scatter_canvas(d).wait_send()
        scatter_strips(d).wait_send()
    for b in range(SLOTS):

        @pl.when(br != b)
        def _(b=b):
            crop_copy(b).wait_send()

    pl.when(first_up)(lambda: edge_up().wait_send())
    pl.when(root_down)(lambda: edge_down().wait_send())


def run(n, features, merge_local, conv_local, merge_global, conv_global, offsets, sizes, owners):
    hbm = pl.BlockSpec(memory_space=pltpu.HBM)
    dma = pltpu.SemaphoreType.DMA

    def vm(*shape):
        return pltpu.VMEM(shape, BF)

    def sm(*shape):
        return pltpu.SMEM(shape, jnp.int32)

    tiles = n * n
    out = pl.pallas_call(
        functools.partial(kernel, n),
        out_shape=pltpu.VMEM((CELLS, C), BF),
        in_specs=[hbm] * 8,
        out_specs=pl.BlockSpec(memory_space=pltpu.VMEM),
        scratch_shapes=[
            vm(CELLS, C),
            vm(2 * C, C),
            vm(2 * C, C),
            vm(3, 3, C, C),
            sm(SLOTS, 2, tiles),
            sm(SLOTS, 2, tiles),
            sm(SLOTS, 1, tiles),
            vm(ROWS, WIN, C),
            vm(n, ROWS, WIN, C),
            vm(n, GW, C),
            vm(n * SLOTS * WIN, n * GW),
            vm(n, n, GW, GW),
            vm(n, SLOTS, WIN, C),
            vm(n, SLOTS, WIN, C),
            vm(n, GW, C),
            vm(n, GW, C),
            vm(ROWS, WIN, C),
            vm(ROWS, WIN, C),
            vm(ROWS + 2, GW, C),
            vm(GW, C),
            vm(ROWS, S, C),
            vm(9 * GW, 6 * C),
            vm(6 * C, 2 * C),
            vm(6 * C, 2 * C),
            dma((7,)),
            dma((ROWS,)),
            dma((1,)),
            dma((ROWS,)),
            dma((ROWS,)),
            dma((n,)),
            dma((n,)),
            dma((n,)),
            dma((n,)),
            dma((n,)),
            dma((n,)),
            dma((n,)),
            dma((n,)),
            dma((ROWS,)),
            dma((ROWS,)),
            dma((2,)),
            dma((ROWS + 2,)),
        ],
        compiler_params=pltpu.CompilerParams(
            collective_id=0, has_side_effects=True, vmem_limit_bytes=40 * 1024 * 1024
        ),
        name="glue",
    )(
        *(
            pltpu.with_memory_space_constraint(a, pltpu.HBM)
            for a in (
                features.reshape(CELLS, C),
                merge_local,
                conv_local,
                merge_global,
                conv_global,
                offsets.transpose(0, 2, 3, 1).reshape(SLOTS, 2, tiles),
                sizes.transpose(0, 2, 3, 1).reshape(SLOTS, 2, tiles),
                owners.transpose(0, 2, 1),
            )
        )
    )
    return out.reshape(features.shape)


def solution(mesh):
    n = 1
    while n * n < mesh.shape["tile"]:
        n += 1
    in_specs = (P("branch", "tile", None, None, None), P(), P(), P(), P(), P(), P(), P())
    out_specs = P("branch", "tile", None, None, None)
    return jax.shard_map(
        functools.partial(run, n),
        mesh=mesh,
        in_specs=in_specs,
        out_specs=out_specs,
        check_vma=False,
    )
```

```python
import functools

import jax
import jax.numpy as jnp
from jax import lax
from jax.experimental import pallas as pl
from jax.experimental.pallas import tpu as pltpu
from jax.sharding import PartitionSpec as P

MESH = pl.DeviceIdType.MESH
BF = jnp.bfloat16
F32 = jnp.float32
C = 128
S = 64
GW = 256
WIN = 16
CELLS = 4096
ROWS = 16
SLOTS = 15


def iota(shape, dim):
    return lax.broadcasted_iota(jnp.int32, shape, dim)


def kernel(
    n, x_hbm, ml_hbm, cl_hbm, mg_hbm, cg_hbm, off_hbm, size_hbm, own_hbm, out_ref,
    x_ref, ml_ref, mg_ref, conv_ref, off_ref, size_ref, own_ref,
    win, wall, bands, smat, pmat, strip, strip_in, canv, canv_in, total_strip, crop, rows, mine, cu, zbuf, wlo, whi,
    in_s, gr_s, gr_r, zw_s, zw_r, a1_s, a1_r, a2_s, a2_r, r1_s, r1_r, r2_s, r2_r, zc_s, zc_r, m_s, m_r,
):
    tiles = n * n
    peers = sorted(range(1, n), key=lambda d: -min(d, n - d))
    br = lax.axis_index("branch")
    t = lax.axis_index("tile")
    up = br % 2 == 1
    xx, yy = t // n, t % n
    f0 = jnp.where(up, xx, yy)
    g0 = jnp.where(up, yy, xx)
    last = ROWS - 1
    is_root = br == last
    is_local = br < last

    def tile_of(f, g):
        return jnp.where(up, f * n + g, g * n + f)

    def rc(src, dst, ss, rs, dev):
        return pltpu.make_async_remote_copy(
            src_ref=src, dst_ref=dst, send_sem=ss, recv_sem=rs, device_id=dev, device_id_type=MESH
        )

    def fetch(i, src, dst):
        return pltpu.make_async_copy(src, dst, in_s.at[i])

    fetches = [
        fetch(0, size_hbm, size_ref),
        fetch(1, off_hbm, off_ref),
        fetch(2, own_hbm, own_ref),
        fetch(3, x_hbm, x_ref),
        fetch(4, mg_hbm, mg_ref),
        fetch(5, ml_hbm, ml_ref),
    ]
    for f in fetches:
        f.start()
    pl.when(is_root)(lambda: fetch(6, cg_hbm, conv_ref).start())
    pl.when(is_local)(lambda: fetch(6, cl_hbm, conv_ref).start())

    barrier = pltpu.get_barrier_semaphore()

    def greet(b, tile):
        pl.semaphore_signal(barrier, inc=1, device_id=(b, tile), device_id_type=MESH)

    for b in (ROWS - 1, *range(ROWS - 1)):
        pl.when(br != b)(functools.partial(greet, b, t))
    for d in range(1, n):
        greet(br, ((xx + d) % n) * n + yy)
        greet(br, xx * n + (yy + d) % n)
    before = jnp.maximum(t - 1, 0)
    after = jnp.minimum(t + 1, tiles - 1)
    has_before, has_after = t > 0, t < tiles - 1
    is_first = br == 0
    first_up = jnp.logical_and(is_first, has_before)
    root_up = jnp.logical_and(is_root, has_before)
    root_down = jnp.logical_and(is_root, has_after)

    @pl.when(first_up)
    def _():
        greet(last, before)

    @pl.when(root_up)
    def _():
        greet(last, before)

    @pl.when(root_down)
    def _():
        greet(0, after)
        greet(last, after)

    for f in fetches[:4]:
        f.wait()

    slot = jnp.minimum(br, last - 1)
    top = off_ref[slot, 0, t]
    hh = size_ref[slot, 0, t]
    ww = size_ref[slot, 1, t]

    @pl.when(is_local)
    def _():
        sub = iota((256, 1), 0)
        sub_row = sub // WIN - top
        sub_col = sub % WIN
        lane64 = iota((1, 128), 1)
        inside = lane64 < S
        row_hits = jnp.where(jnp.logical_and(inside, ((lane64 * hh) >> 6) == sub_row), 1.0, 0.0)
        col_hits = jnp.where(jnp.logical_and(inside, ((lane64 * ww) >> 6) == sub_col), 1.0, 0.0)
        counts = jnp.sum(row_hits, axis=1, keepdims=True) * jnp.sum(col_hits, axis=1, keepdims=True)
        wide = 1024
        lane = iota((1, wide), 1)
        cols = jnp.where((((lane % S) * ww) >> 6) == sub_col, 1.0, 0.0)

        def pool_step(step, acc):
            rows_at = ((step * (wide // S) + lane // S) * hh) >> 6
            lhs = jnp.where(rows_at == sub_row, cols, 0.0).astype(BF)
            rhs = x_ref[pl.ds(pl.multiple_of(step * wide, wide), wide)]
            return acc + jnp.dot(lhs, rhs, preferred_element_type=F32)

        total = lax.fori_loop(0, CELLS // wide, pool_step, jnp.zeros((256, C), F32))
        win[...] = (total / jnp.maximum(counts, 1.0)).astype(BF).reshape(ROWS, WIN, C)

    count = ROWS - 1 + 2 * (n - 1)
    extra = jnp.where(first_up, 1, 0) + jnp.where(root_up, 1, 0) + jnp.where(root_down, 2, 0)
    pl.semaphore_wait(barrier, count + extra)

    def row_copy(r):
        f = xx if r % 2 else yy
        return rc(x_ref.at[r * GW : (r + 1) * GW], bands.at[f], gr_s.at[r], gr_r.at[0], (r, t))

    far_first = (8, 6, 9, 7, 10, 4, 11, 5, 12, 2, 13, 3, 0, 1, 14)

    @pl.when(is_root)
    def _():
        for r in far_first:
            row_copy(r).start()
        bands[f0] = x_ref[last * GW : (last + 1) * GW]

    def window_copy(d):
        r = (br + d) % ROWS
        f = jnp.where(r % 2 == 1, xx, yy)
        return rc(win.at[r], wall.at[f, br], zw_s.at[d], zw_r.at[br], (r, t))

    @pl.when(is_local)
    def _():
        for d in sorted(range(1, ROWS), key=lambda d: -min(d, ROWS - d)):
            window_copy(d).start()
        wall[f0, slot] = win[br]

    def axes_of(tile):
        high, low = lax.div(tile, n), lax.rem(tile, n)
        return jnp.where(up, high, low), jnp.where(up, low, high)

    diag = iota((WIN, n * GW), 1) - iota((WIN, n * GW), 0)

    def strip_step(g, carry):
        tile = tile_of(f0, g)
        for s in range(SLOTS):
            f_own, g_own = axes_of(own_ref[s, 0, tile])
            target = jnp.where(g_own == g0, f_own * GW + off_ref[s, 1, tile], -(n + 1) * GW)
            at = pl.ds(pl.multiple_of((g * SLOTS + s) * WIN, WIN), WIN)
            smat[at] = jnp.where(diag == target, 1.0, 0.0).astype(BF)
        return carry

    piece = iota((1, GW), 1) // WIN
    place = iota((1, GW), 1) % WIN
    column = iota((GW, 1), 0)

    def place_step(f, carry):
        tile = tile_of(f, g0)
        target = jnp.full((1, GW), -(n + 1) * GW, jnp.int32)
        for s in range(SLOTS):
            f_own, g_own = axes_of(own_ref[s, 0, tile])
            here = jnp.where(f_own == f0, g_own * GW + off_ref[s, 1, tile], -(n + 1) * GW)
            target = jnp.where(piece == s, here, target)
        target = target + place
        for g in range(n):
            pmat[g, f] = jnp.where(column + g * GW == target, 1.0, 0.0).astype(BF)
        wall[f, SLOTS] = jnp.zeros((WIN, C), BF)
        return carry


    def gather_windows(d):
        own = wall.at[f0, 0:SLOTS]
        return rc(own, own, a1_s.at[d], a1_r.at[f0], (br, tile_of((f0 + d) % n, g0)))

    def gather_windows_wait(d):
        f = (f0 + d) % n
        part = wall.at[f, 0:SLOTS]
        rc(part, part, a1_s.at[d], a1_r.at[f], (br, t)).wait_recv()

    def gather_bands(d):
        own = bands.at[f0]
        return rc(own, own, r1_s.at[d], r1_r.at[f0], (br, tile_of((f0 + d) % n, g0)))

    def gather_bands_wait(d):
        f = (f0 + d) % n
        rc(bands.at[f], bands.at[f], r1_s.at[d], r1_r.at[f], (br, t)).wait_recv()

    lax.fori_loop(0, n, strip_step, 0)

    @pl.when(is_local)
    def _():
        rc(bands.at[0], bands.at[f0], gr_s.at[0], gr_r.at[0], (br, t)).wait_recv()

    for d in peers:
        gather_bands(d).start()

    lax.fori_loop(0, n, place_step, 0)

    for s in range(SLOTS):

        @pl.when(br != s)
        def _(s=s):
            rc(win.at[s], wall.at[f0, s], zw_s.at[s], zw_r.at[s], (br, t)).wait_recv()

    for d in peers:
        gather_windows(d).start()

    fetches[4].wait()
    fetches[5].wait()
    fetch(6, cl_hbm, conv_ref).wait()
    zero = jnp.zeros((C, C), BF)
    for sft in range(3):
        for r in range(2):
            at = slice((r * 3 + sft) * C, (r * 3 + sft + 1) * C)
            for o in range(2):
                to = slice(o * C, (o + 1) * C)
                tap = r - o
                wlo[at, to] = conv_ref[tap, sft] if tap >= 0 else zero
                tap = r + 2 - o
                whi[at, to] = conv_ref[tap, sft] if tap <= 2 else zero

    def scatter_canvas(d):
        g = (g0 + d) % n
        return rc(canv.at[g], canv_in.at[g0], a2_s.at[d], a2_r.at[g0], (br, tile_of(f0, g)))

    def scatter_canvas_wait(d):
        g = (g0 + d) % n
        rc(canv.at[g], canv_in.at[g], a2_s.at[d], a2_r.at[g], (br, t)).wait_recv()

    def scatter_strips(d):
        g = (g0 + d) % n
        return rc(strip.at[g], strip_in.at[g0], r2_s.at[d], r2_r.at[g0], (br, tile_of(f0, g)))

    def scatter_strips_wait(d):
        g = (g0 + d) % n
        rc(strip.at[g], strip_in.at[g], r2_s.at[d], r2_r.at[g], (br, t)).wait_recv()

    for d in range(1, n):
        gather_bands_wait(d)
    own_strips = None
    block = SLOTS * WIN
    for d in [*peers, 0]:
        g = (g0 + d) % n
        at = pl.ds(pl.multiple_of(g * block, WIN), block)
        cut = jnp.dot(smat[at], bands[...].reshape(n * GW, C), preferred_element_type=F32)
        own_strips = cut.astype(BF).reshape(SLOTS, WIN, C)
        if d:
            strip[g] = own_strips
            scatter_strips(d).start()

    for d in range(1, n):
        gather_windows_wait(d)
    pooled = jnp.zeros((GW, C), F32)
    for d in [*peers, 0]:
        g = (g0 + d) % n
        pooled = jnp.zeros((GW, C), F32)
        for f in range(n):
            w = wall[f].reshape(GW, C)
            pooled = pooled + jnp.dot(pmat[g, f], w, preferred_element_type=F32)
        if d:
            canv[g] = pooled.astype(BF)
            scatter_canvas(d).start()

    def crop_copy(b):
        return rc(total_strip.at[b], crop.at[br], zc_s.at[b], zc_r.at[br], (b, t))

    for d in range(1, n):
        scatter_strips_wait(d)
        own_strips = own_strips + strip_in[(g0 + d) % n]
    total_strip[0:SLOTS] = own_strips
    for b in (1, 3, 0, 2, 5, 4, 7, 6, *range(8, SLOTS)):

        @pl.when(br != b)
        def _(b=b):
            crop_copy(b).start()

    def merged_copy():
        return rc(mine, rows.at[br + 1], m_s.at[0], m_r.at[br + 1], (last, t))

    def edge_up():
        return rc(mine, rows.at[ROWS + 1], m_s.at[1], m_r.at[ROWS + 1], (last, before))

    def edge_down():
        return rc(mine, rows.at[0], m_s.at[1], m_r.at[0], (last, after))

    for d in range(1, n):
        scatter_canvas_wait(d)
        pooled = pooled + canv_in[(g0 + d) % n].astype(F32)
    both = jnp.concatenate([bands[f0], pooled.astype(BF)], axis=1)
    merged = jnp.maximum(jnp.dot(both, mg_ref[...], preferred_element_type=F32), 0.0)
    mine[...] = merged.astype(BF)
    pl.when(is_local)(lambda: merged_copy().start())
    pl.when(first_up)(lambda: edge_up().start())
    pl.when(root_down)(lambda: edge_down().start())

    @pl.when(is_root)
    def _():
        for r in far_first:
            row_copy(r).wait_send()

    @pl.when(is_local)
    def _():
        for d in range(1, ROWS):
            window_copy(d).wait_send()

    for d in range(1, n):
        gather_windows(d).wait_send()
        gather_bands(d).wait_send()
        scatter_canvas(d).wait_send()
        scatter_strips(d).wait_send()

    def put(at, lanes, value, width):
        m = value.reshape(-1, width, C)
        col = iota((1, width, 1), 1)
        left = jnp.where(col == 0, 0.0, pltpu.roll(m, 1, 1))
        right = jnp.where(col == width - 1, 0.0, pltpu.roll(m, width - 1, 1))
        for sft, v in enumerate((left, m, right)):
            zbuf[at, lanes + sft * C : lanes + (sft + 1) * C] = v.reshape(-1, C).astype(BF)

    def conv_block(first, hi_first):
        lo = zbuf[first : first + 256]
        hi = zbuf[hi_first : hi_first + 256]
        res = jnp.dot(lo, wlo[...], preferred_element_type=F32)
        res = res + jnp.dot(hi, whi[...], preferred_element_type=F32)
        return res.astype(BF)

    @pl.when(is_local)
    def _():
        zbuf[0:S, 0 : 3 * C] = jnp.zeros((S, 3 * C), BF)
        zbuf[S // 2 * S : (S // 2 + 1) * S, 3 * C :] = jnp.zeros((S, 3 * C), BF)
        s256 = iota((4 * S, 1), 0)
        target = (s256 // S) * WIN + (((s256 % S) * ww) >> 6)
        lhs = jnp.where(iota((1, 4 * WIN), 1) == target, 1.0, 0.0).astype(BF)
        weight = ml_ref[...]
        crop[br] = total_strip[slot]
        order = sorted(range(ROWS), key=lambda d: min(d, ROWS - d))
        for i in range(0, ROWS, 4):
            part = [(br + d) % ROWS for d in order[i : i + 4]]
            for d, r in zip(order[i : i + 4], part):
                if d:
                    rc(
                        total_strip.at[0], crop.at[r], zc_s.at[d], zc_r.at[r], (br, t)
                    ).wait_recv()
            strips = jnp.concatenate([crop[r] for r in part], axis=0)
            wide_rows = jnp.dot(lhs, strips, preferred_element_type=F32).astype(BF)
            for j, r in enumerate(part):
                cu[r] = wide_rows[j * S : (j + 1) * S]

        for b in range(S // 8):
            ups = []
            for i in range(8):
                r = (((b * 8 + i) * hh) >> 6) + top
                ups.append(cu[jnp.clip(r, 0, ROWS - 1)])
            both = jnp.concatenate(
                [x_ref[b * 8 * S : (b + 1) * 8 * S], jnp.concatenate(ups, axis=0)], axis=1
            )
            m = jnp.maximum(jnp.dot(both, weight, preferred_element_type=F32), 0.0)
            for i in range(8):
                pair = b * 4 + (i + 1) // 2
                at = slice(pair * S, (pair + 1) * S)
                put(at, 3 * C * ((i + 1) % 2), m[i * S : (i + 1) * S], S)

        for b in range(S // 8):
            res = conv_block(b * 256, b * 256 + S)
            for i in range(4):
                for o in range(2):
                    at = b * 512 + (2 * i + o) * S
                    out_ref[at : at + S] = res[i * S : (i + 1) * S, o * C : (o + 1) * C]

    @pl.when(is_root)
    def _():
        rows[ROWS] = mine[...]

        @pl.when(jnp.logical_not(has_before))
        def _():
            rows[0] = jnp.zeros((GW, C), BF)

        @pl.when(jnp.logical_not(has_after))
        def _():
            rows[ROWS + 1] = jnp.zeros((GW, C), BF)

        def wait(i):
            rc(mine, rows.at[i], m_s.at[0], m_r.at[i], (br, t)).wait_recv()

        here = set()
        done = set()
        for i in (16, 15, 1, 2, 13, 14, 3, 4, 11, 12, 5, 6, 9, 10, 0, 17, 7, 8):
            if i == 0:
                pl.when(has_before)(functools.partial(wait, 0))
            elif i == ROWS + 1:
                pl.when(has_after)(functools.partial(wait, ROWS + 1))
            elif i != ROWS:
                wait(i)
            put(slice(i // 2 * GW, (i // 2 + 1) * GW), 3 * C * (i % 2), rows[i].astype(F32), GW)
            here.add(i)
            for q in range(8):
                if q not in done and here >= {2 * q, 2 * q + 1, 2 * q + 2, 2 * q + 3}:
                    done.add(q)
                    res = conv_block(q * GW, (q + 1) * GW)
                    for o in range(2):
                        at = slice((2 * q + o) * GW, (2 * q + o + 1) * GW)
                        out_ref[at] = res[:, o * C : (o + 1) * C]

    pl.when(is_local)(lambda: merged_copy().wait_send())
    for b in range(SLOTS):

        @pl.when(br != b)
        def _(b=b):
            crop_copy(b).wait_send()

    pl.when(first_up)(lambda: edge_up().wait_send())
    pl.when(root_down)(lambda: edge_down().wait_send())


def run(n, features, merge_local, conv_local, merge_global, conv_global, offsets, sizes, owners):
    hbm = pl.BlockSpec(memory_space=pltpu.HBM)
    dma = pltpu.SemaphoreType.DMA

    def vm(*shape):
        return pltpu.VMEM(shape, BF)

    def sm(*shape):
        return pltpu.SMEM(shape, jnp.int32)

    tiles = n * n
    out = pl.pallas_call(
        functools.partial(kernel, n),
        out_shape=pltpu.VMEM((CELLS, C), BF),
        in_specs=[hbm] * 8,
        out_specs=pl.BlockSpec(memory_space=pltpu.VMEM),
        scratch_shapes=[
            vm(CELLS, C),
            vm(2 * C, C),
            vm(2 * C, C),
            vm(3, 3, C, C),
            sm(SLOTS, 2, tiles),
            sm(SLOTS, 2, tiles),
            sm(SLOTS, 1, tiles),
            vm(ROWS, WIN, C),
            vm(n, ROWS, WIN, C),
            vm(n, GW, C),
            vm(n * SLOTS * WIN, n * GW),
            vm(n, n, GW, GW),
            vm(n, SLOTS, WIN, C),
            vm(n, SLOTS, WIN, C),
            vm(n, GW, C),
            vm(n, GW, C),
            vm(ROWS, WIN, C),
            vm(ROWS, WIN, C),
            vm(ROWS + 2, GW, C),
            vm(GW, C),
            vm(ROWS, S, C),
            vm(9 * GW, 6 * C),
            vm(6 * C, 2 * C),
            vm(6 * C, 2 * C),
            dma((7,)),
            dma((ROWS,)),
            dma((1,)),
            dma((ROWS,)),
            dma((ROWS,)),
            dma((n,)),
            dma((n,)),
            dma((n,)),
            dma((n,)),
            dma((n,)),
            dma((n,)),
            dma((n,)),
            dma((n,)),
            dma((ROWS,)),
            dma((ROWS,)),
            dma((2,)),
            dma((ROWS + 2,)),
        ],
        compiler_params=pltpu.CompilerParams(
            collective_id=0, has_side_effects=True, vmem_limit_bytes=40 * 1024 * 1024
        ),
        name="glue",
    )(
        *(
            pltpu.with_memory_space_constraint(a, pltpu.HBM)
            for a in (
                features.reshape(CELLS, C),
                merge_local,
                conv_local,
                merge_global,
                conv_global,
                offsets.transpose(0, 2, 3, 1).reshape(SLOTS, 2, tiles),
                sizes.transpose(0, 2, 3, 1).reshape(SLOTS, 2, tiles),
                owners.transpose(0, 2, 1),
            )
        )
    )
    return out.reshape(features.shape)


def solution(mesh):
    n = 1
    while n * n < mesh.shape["tile"]:
        n += 1
    in_specs = (P("branch", "tile", None, None, None), P(), P(), P(), P(), P(), P(), P())
    out_specs = P("branch", "tile", None, None, None)
    return jax.shard_map(
        functools.partial(run, n),
        mesh=mesh,
        in_specs=in_specs,
        out_specs=out_specs,
        check_vma=False,
    )
```

```python
import functools

import jax
import jax.numpy as jnp
from jax import lax
from jax.experimental import pallas as pl
from jax.experimental.pallas import tpu as pltpu
from jax.sharding import PartitionSpec as P

MESH = pl.DeviceIdType.MESH
BF = jnp.bfloat16
F32 = jnp.float32
C = 128
S = 64
GW = 256
WIN = 16
CELLS = 4096
ROWS = 16
SLOTS = 15


def iota(shape, dim):
    return lax.broadcasted_iota(jnp.int32, shape, dim)


def kernel(
    n, x_hbm, ml_hbm, cl_hbm, mg_hbm, cg_hbm, off_hbm, size_hbm, own_hbm, out_ref,
    x_ref, ml_ref, mg_ref, conv_ref, off_ref, size_ref, own_ref,
    win, wall, bands, smat, pmat, strip, strip_in, canv, canv_in, total_strip, crop, rows, mine, cu, zbuf, wlo, whi,
    in_s, gr_s, gr_r, zw_s, zw_r, a1_s, a1_r, a2_s, a2_r, r1_s, r1_r, r2_s, r2_r, zc_s, zc_r, m_s, m_r,
):
    tiles = n * n
    peers = sorted(range(1, n), key=lambda d: -min(d, n - d))
    br = lax.axis_index("branch")
    t = lax.axis_index("tile")
    up = br % 2 == 1
    xx, yy = t // n, t % n
    f0 = jnp.where(up, xx, yy)
    g0 = jnp.where(up, yy, xx)
    last = ROWS - 1
    is_root = br == last
    is_local = br < last

    def tile_of(f, g):
        return jnp.where(up, f * n + g, g * n + f)

    def rc(src, dst, ss, rs, dev):
        return pltpu.make_async_remote_copy(
            src_ref=src, dst_ref=dst, send_sem=ss, recv_sem=rs, device_id=dev, device_id_type=MESH
        )

    def fetch(i, src, dst):
        return pltpu.make_async_copy(src, dst, in_s.at[i])

    fetches = [
        fetch(0, size_hbm, size_ref),
        fetch(1, off_hbm, off_ref),
        fetch(2, own_hbm, own_ref),
        fetch(3, x_hbm, x_ref),
        fetch(4, mg_hbm, mg_ref),
        fetch(5, ml_hbm, ml_ref),
    ]
    for f in fetches:
        f.start()
    pl.when(is_root)(lambda: fetch(6, cg_hbm, conv_ref).start())
    pl.when(is_local)(lambda: fetch(6, cl_hbm, conv_ref).start())

    barrier = pltpu.get_barrier_semaphore()

    def greet(b, tile):
        pl.semaphore_signal(barrier, inc=1, device_id=(b, tile), device_id_type=MESH)

    for b in (ROWS - 1, *range(ROWS - 1)):
        pl.when(br != b)(functools.partial(greet, b, t))
    for d in range(1, n):
        greet(br, ((xx + d) % n) * n + yy)
        greet(br, xx * n + (yy + d) % n)
    before = jnp.maximum(t - 1, 0)
    after = jnp.minimum(t + 1, tiles - 1)
    has_before, has_after = t > 0, t < tiles - 1
    is_first = br == 0
    first_up = jnp.logical_and(is_first, has_before)
    root_up = jnp.logical_and(is_root, has_before)
    root_down = jnp.logical_and(is_root, has_after)

    @pl.when(first_up)
    def _():
        greet(last, before)

    @pl.when(root_up)
    def _():
        greet(last, before)

    @pl.when(root_down)
    def _():
        greet(0, after)
        greet(last, after)

    for f in fetches[:4]:
        f.wait()

    slot = jnp.minimum(br, last - 1)
    top = off_ref[slot, 0, t]
    hh = size_ref[slot, 0, t]
    ww = size_ref[slot, 1, t]

    @pl.when(is_local)
    def _():
        sub = iota((256, 1), 0)
        sub_row = sub // WIN - top
        sub_col = sub % WIN
        lane64 = iota((1, 128), 1)
        inside = lane64 < S
        row_hits = jnp.where(jnp.logical_and(inside, ((lane64 * hh) >> 6) == sub_row), 1.0, 0.0)
        col_hits = jnp.where(jnp.logical_and(inside, ((lane64 * ww) >> 6) == sub_col), 1.0, 0.0)
        counts = jnp.sum(row_hits, axis=1, keepdims=True) * jnp.sum(col_hits, axis=1, keepdims=True)
        wide = 1024
        lane = iota((1, wide), 1)
        cols = jnp.where((((lane % S) * ww) >> 6) == sub_col, 1.0, 0.0)

        def pool_step(step, acc):
            rows_at = ((step * (wide // S) + lane // S) * hh) >> 6
            lhs = jnp.where(rows_at == sub_row, cols, 0.0).astype(BF)
            rhs = x_ref[pl.ds(pl.multiple_of(step * wide, wide), wide)]
            return acc + jnp.dot(lhs, rhs, preferred_element_type=F32)

        total = lax.fori_loop(0, CELLS // wide, pool_step, jnp.zeros((256, C), F32))
        win[...] = (total / jnp.maximum(counts, 1.0)).astype(BF).reshape(ROWS, WIN, C)

    count = ROWS - 1 + 2 * (n - 1)
    extra = jnp.where(first_up, 1, 0) + jnp.where(root_up, 1, 0) + jnp.where(root_down, 2, 0)
    pl.semaphore_wait(barrier, count + extra)

    def row_copy(r):
        f = xx if r % 2 else yy
        return rc(x_ref.at[r * GW : (r + 1) * GW], bands.at[f], gr_s.at[r], gr_r.at[0], (r, t))

    far_first = (8, 6, 9, 7, 10, 4, 11, 5, 12, 2, 13, 3, 0, 1, 14)

    @pl.when(is_root)
    def _():
        for r in far_first:
            row_copy(r).start()
        bands[f0] = x_ref[last * GW : (last + 1) * GW]

    def window_copy(d):
        r = (br + d) % ROWS
        f = jnp.where(r % 2 == 1, xx, yy)
        return rc(win.at[r], wall.at[f, br], zw_s.at[d], zw_r.at[br], (r, t))

    @pl.when(is_local)
    def _():
        for d in sorted(range(1, ROWS), key=lambda d: -min(d, ROWS - d)):
            window_copy(d).start()
        wall[f0, slot] = win[br]

    def axes_of(tile):
        high, low = lax.div(tile, n), lax.rem(tile, n)
        return jnp.where(up, high, low), jnp.where(up, low, high)

    diag = iota((WIN, n * GW), 1) - iota((WIN, n * GW), 0)

    def strip_step(g, carry):
        tile = tile_of(f0, g)
        for s in range(SLOTS):
            f_own, g_own = axes_of(own_ref[s, 0, tile])
            target = jnp.where(g_own == g0, f_own * GW + off_ref[s, 1, tile], -(n + 1) * GW)
            at = pl.ds(pl.multiple_of((g * SLOTS + s) * WIN, WIN), WIN)
            smat[at] = jnp.where(diag == target, 1.0, 0.0).astype(BF)
        return carry

    piece = iota((1, GW), 1) // WIN
    place = iota((1, GW), 1) % WIN
    column = iota((GW, 1), 0)

    def place_step(f, carry):
        tile = tile_of(f, g0)
        target = jnp.full((1, GW), -(n + 1) * GW, jnp.int32)
        for s in range(SLOTS):
            f_own, g_own = axes_of(own_ref[s, 0, tile])
            here = jnp.where(f_own == f0, g_own * GW + off_ref[s, 1, tile], -(n + 1) * GW)
            target = jnp.where(piece == s, here, target)
        target = target + place
        for g in range(n):
            pmat[g, f] = jnp.where(column + g * GW == target, 1.0, 0.0).astype(BF)
        wall[f, SLOTS] = jnp.zeros((WIN, C), BF)
        return carry


    def gather_windows(d):
        own = wall.at[f0, 0:SLOTS]
        return rc(own, own, a1_s.at[d], a1_r.at[f0], (br, tile_of((f0 + d) % n, g0)))

    def gather_windows_wait(d):
        f = (f0 + d) % n
        part = wall.at[f, 0:SLOTS]
        rc(part, part, a1_s.at[d], a1_r.at[f], (br, t)).wait_recv()

    def gather_bands(d):
        own = bands.at[f0]
        return rc(own, own, r1_s.at[d], r1_r.at[f0], (br, tile_of((f0 + d) % n, g0)))

    def gather_bands_wait(d):
        f = (f0 + d) % n
        rc(bands.at[f], bands.at[f], r1_s.at[d], r1_r.at[f], (br, t)).wait_recv()

    lax.fori_loop(0, n, strip_step, 0)

    @pl.when(is_local)
    def _():
        rc(bands.at[0], bands.at[f0], gr_s.at[0], gr_r.at[0], (br, t)).wait_recv()

    for d in peers:
        gather_bands(d).start()


    for s in range(SLOTS):

        @pl.when(br != s)
        def _(s=s):
            rc(win.at[s], wall.at[f0, s], zw_s.at[s], zw_r.at[s], (br, t)).wait_recv()

    for d in peers:
        gather_windows(d).start()

    fetches[4].wait()
    fetches[5].wait()
    fetch(6, cl_hbm, conv_ref).wait()
    zero = jnp.zeros((C, C), BF)
    for sft in range(3):
        for r in range(2):
            at = slice((r * 3 + sft) * C, (r * 3 + sft + 1) * C)
            for o in range(2):
                to = slice(o * C, (o + 1) * C)
                tap = r - o
                wlo[at, to] = conv_ref[tap, sft] if tap >= 0 else zero
                tap = r + 2 - o
                whi[at, to] = conv_ref[tap, sft] if tap <= 2 else zero

    def scatter_canvas(d):
        g = (g0 + d) % n
        return rc(canv.at[g], canv_in.at[g0], a2_s.at[d], a2_r.at[g0], (br, tile_of(f0, g)))

    def scatter_canvas_wait(d):
        g = (g0 + d) % n
        rc(canv.at[g], canv_in.at[g], a2_s.at[d], a2_r.at[g], (br, t)).wait_recv()

    def scatter_strips(d):
        g = (g0 + d) % n
        return rc(strip.at[g], strip_in.at[g0], r2_s.at[d], r2_r.at[g0], (br, tile_of(f0, g)))

    def scatter_strips_wait(d):
        g = (g0 + d) % n
        rc(strip.at[g], strip_in.at[g], r2_s.at[d], r2_r.at[g], (br, t)).wait_recv()

    for d in range(1, n):
        gather_bands_wait(d)
    own_strips = None
    block = SLOTS * WIN
    for d in [*peers, 0]:
        g = (g0 + d) % n
        at = pl.ds(pl.multiple_of(g * block, WIN), block)
        cut = jnp.dot(smat[at], bands[...].reshape(n * GW, C), preferred_element_type=F32)
        own_strips = cut.astype(BF).reshape(SLOTS, WIN, C)
        if d:
            strip[g] = own_strips
            scatter_strips(d).start()

    lax.fori_loop(0, n, place_step, 0)
    for d in range(1, n):
        gather_windows_wait(d)
    pooled = jnp.zeros((GW, C), F32)
    for d in [*peers, 0]:
        g = (g0 + d) % n
        pooled = jnp.zeros((GW, C), F32)
        for f in range(n):
            w = wall[f].reshape(GW, C)
            pooled = pooled + jnp.dot(pmat[g, f], w, preferred_element_type=F32)
        if d:
            canv[g] = pooled.astype(BF)
            scatter_canvas(d).start()

    def crop_copy(b):
        return rc(total_strip.at[b], crop.at[br], zc_s.at[b], zc_r.at[br], (b, t))

    for d in range(1, n):
        scatter_strips_wait(d)
        own_strips = own_strips + strip_in[(g0 + d) % n]
    total_strip[0:SLOTS] = own_strips
    for b in (1, 3, 0, 2, 5, 4, 7, 6, *range(8, SLOTS)):

        @pl.when(br != b)
        def _(b=b):
            crop_copy(b).start()

    def merged_copy():
        return rc(mine, rows.at[br + 1], m_s.at[0], m_r.at[br + 1], (last, t))

    def edge_up():
        return rc(mine, rows.at[ROWS + 1], m_s.at[1], m_r.at[ROWS + 1], (last, before))

    def edge_down():
        return rc(mine, rows.at[0], m_s.at[1], m_r.at[0], (last, after))

    for d in range(1, n):
        scatter_canvas_wait(d)
        pooled = pooled + canv_in[(g0 + d) % n].astype(F32)
    both = jnp.concatenate([bands[f0], pooled.astype(BF)], axis=1)
    merged = jnp.maximum(jnp.dot(both, mg_ref[...], preferred_element_type=F32), 0.0)
    mine[...] = merged.astype(BF)
    pl.when(is_local)(lambda: merged_copy().start())
    pl.when(first_up)(lambda: edge_up().start())
    pl.when(root_down)(lambda: edge_down().start())

    @pl.when(is_root)
    def _():
        for r in far_first:
            row_copy(r).wait_send()

    @pl.when(is_local)
    def _():
        for d in range(1, ROWS):
            window_copy(d).wait_send()

    for d in range(1, n):
        gather_windows(d).wait_send()
        gather_bands(d).wait_send()
        scatter_canvas(d).wait_send()
        scatter_strips(d).wait_send()

    def put(at, lanes, value, width):
        m = value.reshape(-1, width, C)
        col = iota((1, width, 1), 1)
        left = jnp.where(col == 0, 0.0, pltpu.roll(m, 1, 1))
        right = jnp.where(col == width - 1, 0.0, pltpu.roll(m, width - 1, 1))
        for sft, v in enumerate((left, m, right)):
            zbuf[at, lanes + sft * C : lanes + (sft + 1) * C] = v.reshape(-1, C).astype(BF)

    def conv_block(first, hi_first):
        lo = zbuf[first : first + 256]
        hi = zbuf[hi_first : hi_first + 256]
        res = jnp.dot(lo, wlo[...], preferred_element_type=F32)
        res = res + jnp.dot(hi, whi[...], preferred_element_type=F32)
        return res.astype(BF)

    @pl.when(is_local)
    def _():
        zbuf[0:S, 0 : 3 * C] = jnp.zeros((S, 3 * C), BF)
        zbuf[S // 2 * S : (S // 2 + 1) * S, 3 * C :] = jnp.zeros((S, 3 * C), BF)
        s256 = iota((4 * S, 1), 0)
        target = (s256 // S) * WIN + (((s256 % S) * ww) >> 6)
        lhs = jnp.where(iota((1, 4 * WIN), 1) == target, 1.0, 0.0).astype(BF)
        weight = ml_ref[...]
        crop[br] = total_strip[slot]
        order = sorted(range(ROWS), key=lambda d: min(d, ROWS - d))
        for i in range(0, ROWS, 4):
            part = [(br + d) % ROWS for d in order[i : i + 4]]
            for d, r in zip(order[i : i + 4], part):
                if d:
                    rc(
                        total_strip.at[0], crop.at[r], zc_s.at[d], zc_r.at[r], (br, t)
                    ).wait_recv()
            strips = jnp.concatenate([crop[r] for r in part], axis=0)
            wide_rows = jnp.dot(lhs, strips, preferred_element_type=F32).astype(BF)
            for j, r in enumerate(part):
                cu[r] = wide_rows[j * S : (j + 1) * S]

        for b in range(S // 8):
            ups = []
            for i in range(8):
                r = (((b * 8 + i) * hh) >> 6) + top
                ups.append(cu[jnp.clip(r, 0, ROWS - 1)])
            both = jnp.concatenate(
                [x_ref[b * 8 * S : (b + 1) * 8 * S], jnp.concatenate(ups, axis=0)], axis=1
            )
            m = jnp.maximum(jnp.dot(both, weight, preferred_element_type=F32), 0.0)
            for i in range(8):
                pair = b * 4 + (i + 1) // 2
                at = slice(pair * S, (pair + 1) * S)
                put(at, 3 * C * ((i + 1) % 2), m[i * S : (i + 1) * S], S)

        for b in range(S // 8):
            res = conv_block(b * 256, b * 256 + S)
            for i in range(4):
                for o in range(2):
                    at = b * 512 + (2 * i + o) * S
                    out_ref[at : at + S] = res[i * S : (i + 1) * S, o * C : (o + 1) * C]

    @pl.when(is_root)
    def _():
        rows[ROWS] = mine[...]

        @pl.when(jnp.logical_not(has_before))
        def _():
            rows[0] = jnp.zeros((GW, C), BF)

        @pl.when(jnp.logical_not(has_after))
        def _():
            rows[ROWS + 1] = jnp.zeros((GW, C), BF)

        def wait(i):
            rc(mine, rows.at[i], m_s.at[0], m_r.at[i], (br, t)).wait_recv()

        here = set()
        done = set()
        for i in (16, 15, 7, 8, 9, 10, 5, 6, 11, 12, 3, 4, 13, 14, 0, 17, 1, 2):
            if i == 0:
                pl.when(has_before)(functools.partial(wait, 0))
            elif i == ROWS + 1:
                pl.when(has_after)(functools.partial(wait, ROWS + 1))
            elif i != ROWS:
                wait(i)
            put(slice(i // 2 * GW, (i // 2 + 1) * GW), 3 * C * (i % 2), rows[i].astype(F32), GW)
            here.add(i)
            for q in range(8):
                if q not in done and here >= {2 * q, 2 * q + 1, 2 * q + 2, 2 * q + 3}:
                    done.add(q)
                    res = conv_block(q * GW, (q + 1) * GW)
                    for o in range(2):
                        at = slice((2 * q + o) * GW, (2 * q + o + 1) * GW)
                        out_ref[at] = res[:, o * C : (o + 1) * C]

    pl.when(is_local)(lambda: merged_copy().wait_send())
    for b in range(SLOTS):

        @pl.when(br != b)
        def _(b=b):
            crop_copy(b).wait_send()

    pl.when(first_up)(lambda: edge_up().wait_send())
    pl.when(root_down)(lambda: edge_down().wait_send())


def run(n, features, merge_local, conv_local, merge_global, conv_global, offsets, sizes, owners):
    hbm = pl.BlockSpec(memory_space=pltpu.HBM)
    dma = pltpu.SemaphoreType.DMA

    def vm(*shape):
        return pltpu.VMEM(shape, BF)

    def sm(*shape):
        return pltpu.SMEM(shape, jnp.int32)

    tiles = n * n
    out = pl.pallas_call(
        functools.partial(kernel, n),
        out_shape=pltpu.VMEM((CELLS, C), BF),
        in_specs=[hbm] * 8,
        out_specs=pl.BlockSpec(memory_space=pltpu.VMEM),
        scratch_shapes=[
            vm(CELLS, C),
            vm(2 * C, C),
            vm(2 * C, C),
            vm(3, 3, C, C),
            sm(SLOTS, 2, tiles),
            sm(SLOTS, 2, tiles),
            sm(SLOTS, 1, tiles),
            vm(ROWS, WIN, C),
            vm(n, ROWS, WIN, C),
            vm(n, GW, C),
            vm(n * SLOTS * WIN, n * GW),
            vm(n, n, GW, GW),
            vm(n, SLOTS, WIN, C),
            vm(n, SLOTS, WIN, C),
            vm(n, GW, C),
            vm(n, GW, C),
            vm(ROWS, WIN, C),
            vm(ROWS, WIN, C),
            vm(ROWS + 2, GW, C),
            vm(GW, C),
            vm(ROWS, S, C),
            vm(9 * GW, 6 * C),
            vm(6 * C, 2 * C),
            vm(6 * C, 2 * C),
            dma((7,)),
            dma((ROWS,)),
            dma((1,)),
            dma((ROWS,)),
            dma((ROWS,)),
            dma((n,)),
            dma((n,)),
            dma((n,)),
            dma((n,)),
            dma((n,)),
            dma((n,)),
            dma((n,)),
            dma((n,)),
            dma((ROWS,)),
            dma((ROWS,)),
            dma((2,)),
            dma((ROWS + 2,)),
        ],
        compiler_params=pltpu.CompilerParams(
            collective_id=0, has_side_effects=True, vmem_limit_bytes=40 * 1024 * 1024
        ),
        name="glue",
    )(
        *(
            pltpu.with_memory_space_constraint(a, pltpu.HBM)
            for a in (
                features.reshape(CELLS, C),
                merge_local,
                conv_local,
                merge_global,
                conv_global,
                offsets.transpose(0, 2, 3, 1).reshape(SLOTS, 2, tiles),
                sizes.transpose(0, 2, 3, 1).reshape(SLOTS, 2, tiles),
                owners.transpose(0, 2, 1),
            )
        )
    )
    return out.reshape(features.shape)


def solution(mesh):
    n = 1
    while n * n < mesh.shape["tile"]:
        n += 1
    in_specs = (P("branch", "tile", None, None, None), P(), P(), P(), P(), P(), P(), P())
    out_specs = P("branch", "tile", None, None, None)
    return jax.shard_map(
        functools.partial(run, n),
        mesh=mesh,
        in_specs=in_specs,
        out_specs=out_specs,
        check_vma=False,
    )
```

```python
import functools

import jax
import jax.numpy as jnp
from jax import lax
from jax.experimental import pallas as pl
from jax.experimental.pallas import tpu as pltpu
from jax.sharding import PartitionSpec as P

MESH = pl.DeviceIdType.MESH
BF = jnp.bfloat16
F32 = jnp.float32
C = 128
S = 64
GW = 256
WIN = 16
CELLS = 4096
ROWS = 16
SLOTS = 15


def iota(shape, dim):
    return lax.broadcasted_iota(jnp.int32, shape, dim)


def kernel(
    n, x_hbm, ml_hbm, cl_hbm, mg_hbm, cg_hbm, off_hbm, size_hbm, own_hbm, out_ref,
    x_ref, ml_ref, mg_ref, conv_ref, off_ref, size_ref, own_ref,
    win, wall, bands, smat, pmat, strip, strip_in, canv, canv_in, total_strip, crop, rows, mine, cu, zbuf, wlo, whi,
    in_s, gr_s, gr_r, zw_s, zw_r, a1_s, a1_r, a2_s, a2_r, r1_s, r1_r, r2_s, r2_r, zc_s, zc_r, m_s, m_r,
):
    tiles = n * n
    peers = sorted(range(1, n), key=lambda d: -min(d, n - d))
    br = lax.axis_index("branch")
    t = lax.axis_index("tile")
    up = br % 2 == 1
    xx, yy = t // n, t % n
    f0 = jnp.where(up, xx, yy)
    g0 = jnp.where(up, yy, xx)
    last = ROWS - 1
    is_root = br == last
    is_local = br < last

    def tile_of(f, g):
        return jnp.where(up, f * n + g, g * n + f)

    def rc(src, dst, ss, rs, dev):
        return pltpu.make_async_remote_copy(
            src_ref=src, dst_ref=dst, send_sem=ss, recv_sem=rs, device_id=dev, device_id_type=MESH
        )

    def fetch(i, src, dst):
        return pltpu.make_async_copy(src, dst, in_s.at[i])

    fetches = [
        fetch(0, size_hbm, size_ref),
        fetch(1, off_hbm, off_ref),
        fetch(2, own_hbm, own_ref),
        fetch(3, x_hbm, x_ref),
        fetch(4, mg_hbm, mg_ref),
        fetch(5, ml_hbm, ml_ref),
    ]
    for f in fetches:
        f.start()
    pl.when(is_root)(lambda: fetch(6, cg_hbm, conv_ref).start())
    pl.when(is_local)(lambda: fetch(6, cl_hbm, conv_ref).start())

    barrier = pltpu.get_barrier_semaphore()

    def greet(b, tile):
        pl.semaphore_signal(barrier, inc=1, device_id=(b, tile), device_id_type=MESH)

    for b in (ROWS - 1, *range(ROWS - 1)):
        pl.when(br != b)(functools.partial(greet, b, t))
    for d in range(1, n):
        greet(br, ((xx + d) % n) * n + yy)
        greet(br, xx * n + (yy + d) % n)
    before = jnp.maximum(t - 1, 0)
    after = jnp.minimum(t + 1, tiles - 1)
    has_before, has_after = t > 0, t < tiles - 1
    is_first = br == 0
    first_up = jnp.logical_and(is_first, has_before)
    root_up = jnp.logical_and(is_root, has_before)
    root_down = jnp.logical_and(is_root, has_after)

    @pl.when(first_up)
    def _():
        greet(last, before)

    @pl.when(root_up)
    def _():
        greet(last, before)

    @pl.when(root_down)
    def _():
        greet(0, after)
        greet(last, after)

    for f in fetches[:4]:
        f.wait()

    slot = jnp.minimum(br, last - 1)
    top = off_ref[slot, 0, t]
    hh = size_ref[slot, 0, t]
    ww = size_ref[slot, 1, t]

    @pl.when(is_local)
    def _():
        sub = iota((256, 1), 0)
        sub_row = sub // WIN - top
        sub_col = sub % WIN
        lane64 = iota((1, 128), 1)
        inside = lane64 < S
        row_hits = jnp.where(jnp.logical_and(inside, ((lane64 * hh) >> 6) == sub_row), 1.0, 0.0)
        col_hits = jnp.where(jnp.logical_and(inside, ((lane64 * ww) >> 6) == sub_col), 1.0, 0.0)
        counts = jnp.sum(row_hits, axis=1, keepdims=True) * jnp.sum(col_hits, axis=1, keepdims=True)
        wide = 1024
        lane = iota((1, wide), 1)
        cols = jnp.where((((lane % S) * ww) >> 6) == sub_col, 1.0, 0.0)

        def pool_step(step, acc):
            rows_at = ((step * (wide // S) + lane // S) * hh) >> 6
            lhs = jnp.where(rows_at == sub_row, cols, 0.0).astype(BF)
            rhs = x_ref[pl.ds(pl.multiple_of(step * wide, wide), wide)]
            return acc + jnp.dot(lhs, rhs, preferred_element_type=F32)

        total = lax.fori_loop(0, CELLS // wide, pool_step, jnp.zeros((256, C), F32))
        win[...] = (total / jnp.maximum(counts, 1.0)).astype(BF).reshape(ROWS, WIN, C)

    count = ROWS - 1 + 2 * (n - 1)
    extra = jnp.where(first_up, 1, 0) + jnp.where(root_up, 1, 0) + jnp.where(root_down, 2, 0)
    pl.semaphore_wait(barrier, count + extra)

    def row_copy(r):
        f = xx if r % 2 else yy
        return rc(x_ref.at[r * GW : (r + 1) * GW], bands.at[f], gr_s.at[r], gr_r.at[0], (r, t))

    far_first = (8, 6, 9, 7, 10, 4, 11, 5, 12, 2, 13, 3, 0, 1, 14)

    @pl.when(is_root)
    def _():
        for r in far_first:
            row_copy(r).start()
        bands[f0] = x_ref[last * GW : (last + 1) * GW]

    def window_copy(d):
        r = (br + d) % ROWS
        f = jnp.where(r % 2 == 1, xx, yy)
        return rc(win.at[r], wall.at[f, br], zw_s.at[d], zw_r.at[br], (r, t))

    @pl.when(is_local)
    def _():
        for d in sorted(range(1, ROWS), key=lambda d: -min(d, ROWS - d)):
            window_copy(d).start()
        wall[f0, slot] = win[br]

    def axes_of(tile):
        high, low = lax.div(tile, n), lax.rem(tile, n)
        return jnp.where(up, high, low), jnp.where(up, low, high)

    diag = iota((WIN, n * GW), 1) - iota((WIN, n * GW), 0)

    def strip_step(g, carry):
        tile = tile_of(f0, g)
        for s in range(SLOTS):
            f_own, g_own = axes_of(own_ref[s, 0, tile])
            target = jnp.where(g_own == g0, f_own * GW + off_ref[s, 1, tile], -(n + 1) * GW)
            at = pl.ds(pl.multiple_of((g * SLOTS + s) * WIN, WIN), WIN)
            smat[at] = jnp.where(diag == target, 1.0, 0.0).astype(BF)
        return carry

    piece = iota((1, GW), 1) // WIN
    place = iota((1, GW), 1) % WIN
    column = iota((GW, 1), 0)

    def place_step(f, carry):
        tile = tile_of(f, g0)
        target = jnp.full((1, GW), -(n + 1) * GW, jnp.int32)
        for s in range(SLOTS):
            f_own, g_own = axes_of(own_ref[s, 0, tile])
            here = jnp.where(f_own == f0, g_own * GW + off_ref[s, 1, tile], -(n + 1) * GW)
            target = jnp.where(piece == s, here, target)
        target = target + place
        for g in range(n):
            pmat[g, f] = jnp.where(column + g * GW == target, 1.0, 0.0).astype(BF)
        wall[f, SLOTS] = jnp.zeros((WIN, C), BF)
        return carry


    def gather_windows(d):
        own = wall.at[f0, 0:SLOTS]
        return rc(own, own, a1_s.at[d], a1_r.at[f0], (br, tile_of((f0 + d) % n, g0)))

    def gather_windows_wait(d):
        f = (f0 + d) % n
        part = wall.at[f, 0:SLOTS]
        rc(part, part, a1_s.at[d], a1_r.at[f], (br, t)).wait_recv()

    def gather_bands(d):
        own = bands.at[f0]
        return rc(own, own, r1_s.at[d], r1_r.at[f0], (br, tile_of((f0 + d) % n, g0)))

    def gather_bands_wait(d):
        f = (f0 + d) % n
        rc(bands.at[f], bands.at[f], r1_s.at[d], r1_r.at[f], (br, t)).wait_recv()

    @pl.when(is_local)
    def _():
        rc(bands.at[0], bands.at[f0], gr_s.at[0], gr_r.at[0], (br, t)).wait_recv()

    for d in peers:
        gather_bands(d).start()

    lax.fori_loop(0, n, strip_step, 0)

    for s in range(SLOTS):

        @pl.when(br != s)
        def _(s=s):
            rc(win.at[s], wall.at[f0, s], zw_s.at[s], zw_r.at[s], (br, t)).wait_recv()

    for d in peers:
        gather_windows(d).start()

    fetches[4].wait()
    fetches[5].wait()
    fetch(6, cl_hbm, conv_ref).wait()
    zero = jnp.zeros((C, C), BF)
    for sft in range(3):
        for r in range(2):
            at = slice((r * 3 + sft) * C, (r * 3 + sft + 1) * C)
            for o in range(2):
                to = slice(o * C, (o + 1) * C)
                tap = r - o
                wlo[at, to] = conv_ref[tap, sft] if tap >= 0 else zero
                tap = r + 2 - o
                whi[at, to] = conv_ref[tap, sft] if tap <= 2 else zero

    def scatter_canvas(d):
        g = (g0 + d) % n
        return rc(canv.at[g], canv_in.at[g0], a2_s.at[d], a2_r.at[g0], (br, tile_of(f0, g)))

    def scatter_canvas_wait(d):
        g = (g0 + d) % n
        rc(canv.at[g], canv_in.at[g], a2_s.at[d], a2_r.at[g], (br, t)).wait_recv()

    def scatter_strips(d):
        g = (g0 + d) % n
        return rc(strip.at[g], strip_in.at[g0], r2_s.at[d], r2_r.at[g0], (br, tile_of(f0, g)))

    def scatter_strips_wait(d):
        g = (g0 + d) % n
        rc(strip.at[g], strip_in.at[g], r2_s.at[d], r2_r.at[g], (br, t)).wait_recv()

    for d in range(1, n):
        gather_bands_wait(d)
    own_strips = None
    block = SLOTS * WIN
    for d in [*peers, 0]:
        g = (g0 + d) % n
        at = pl.ds(pl.multiple_of(g * block, WIN), block)
        cut = jnp.dot(smat[at], bands[...].reshape(n * GW, C), preferred_element_type=F32)
        own_strips = cut.astype(BF).reshape(SLOTS, WIN, C)
        if d:
            strip[g] = own_strips
            scatter_strips(d).start()

    lax.fori_loop(0, n, place_step, 0)
    for d in range(1, n):
        gather_windows_wait(d)
    pooled = jnp.zeros((GW, C), F32)
    for d in [*peers, 0]:
        g = (g0 + d) % n
        pooled = jnp.zeros((GW, C), F32)
        for f in range(n):
            w = wall[f].reshape(GW, C)
            pooled = pooled + jnp.dot(pmat[g, f], w, preferred_element_type=F32)
        if d:
            canv[g] = pooled.astype(BF)
            scatter_canvas(d).start()

    def crop_copy(b):
        return rc(total_strip.at[b], crop.at[br], zc_s.at[b], zc_r.at[br], (b, t))

    for d in range(1, n):
        scatter_strips_wait(d)
        own_strips = own_strips + strip_in[(g0 + d) % n]
    total_strip[0:SLOTS] = own_strips
    for b in (1, 3, 0, 2, 5, 4, 7, 6, *range(8, SLOTS)):

        @pl.when(br != b)
        def _(b=b):
            crop_copy(b).start()

    def merged_copy():
        return rc(mine, rows.at[br + 1], m_s.at[0], m_r.at[br + 1], (last, t))

    def edge_up():
        return rc(mine, rows.at[ROWS + 1], m_s.at[1], m_r.at[ROWS + 1], (last, before))

    def edge_down():
        return rc(mine, rows.at[0], m_s.at[1], m_r.at[0], (last, after))

    for d in range(1, n):
        scatter_canvas_wait(d)
        pooled = pooled + canv_in[(g0 + d) % n].astype(F32)
    both = jnp.concatenate([bands[f0], pooled.astype(BF)], axis=1)
    merged = jnp.maximum(jnp.dot(both, mg_ref[...], preferred_element_type=F32), 0.0)
    mine[...] = merged.astype(BF)
    pl.when(is_local)(lambda: merged_copy().start())
    pl.when(first_up)(lambda: edge_up().start())
    pl.when(root_down)(lambda: edge_down().start())

    @pl.when(is_root)
    def _():
        for r in far_first:
            row_copy(r).wait_send()

    @pl.when(is_local)
    def _():
        for d in range(1, ROWS):
            window_copy(d).wait_send()

    for d in range(1, n):
        gather_windows(d).wait_send()
        gather_bands(d).wait_send()
        scatter_canvas(d).wait_send()
        scatter_strips(d).wait_send()

    def put(at, lanes, value, width):
        m = value.reshape(-1, width, C)
        col = iota((1, width, 1), 1)
        left = jnp.where(col == 0, 0.0, pltpu.roll(m, 1, 1))
        right = jnp.where(col == width - 1, 0.0, pltpu.roll(m, width - 1, 1))
        for sft, v in enumerate((left, m, right)):
            zbuf[at, lanes + sft * C : lanes + (sft + 1) * C] = v.reshape(-1, C).astype(BF)

    def conv_block(first, hi_first):
        lo = zbuf[first : first + 256]
        hi = zbuf[hi_first : hi_first + 256]
        res = jnp.dot(lo, wlo[...], preferred_element_type=F32)
        res = res + jnp.dot(hi, whi[...], preferred_element_type=F32)
        return res.astype(BF)

    @pl.when(is_local)
    def _():
        zbuf[0:S, 0 : 3 * C] = jnp.zeros((S, 3 * C), BF)
        zbuf[S // 2 * S : (S // 2 + 1) * S, 3 * C :] = jnp.zeros((S, 3 * C), BF)
        s256 = iota((4 * S, 1), 0)
        target = (s256 // S) * WIN + (((s256 % S) * ww) >> 6)
        lhs = jnp.where(iota((1, 4 * WIN), 1) == target, 1.0, 0.0).astype(BF)
        weight = ml_ref[...]
        crop[br] = total_strip[slot]
        order = sorted(range(ROWS), key=lambda d: min(d, ROWS - d))
        for i in range(0, ROWS, 4):
            part = [(br + d) % ROWS for d in order[i : i + 4]]
            for d, r in zip(order[i : i + 4], part):
                if d:
                    rc(
                        total_strip.at[0], crop.at[r], zc_s.at[d], zc_r.at[r], (br, t)
                    ).wait_recv()
            strips = jnp.concatenate([crop[r] for r in part], axis=0)
            wide_rows = jnp.dot(lhs, strips, preferred_element_type=F32).astype(BF)
            for j, r in enumerate(part):
                cu[r] = wide_rows[j * S : (j + 1) * S]

        for b in range(S // 8):
            ups = []
            for i in range(8):
                r = (((b * 8 + i) * hh) >> 6) + top
                ups.append(cu[jnp.clip(r, 0, ROWS - 1)])
            both = jnp.concatenate(
                [x_ref[b * 8 * S : (b + 1) * 8 * S], jnp.concatenate(ups, axis=0)], axis=1
            )
            m = jnp.maximum(jnp.dot(both, weight, preferred_element_type=F32), 0.0)
            for i in range(8):
                pair = b * 4 + (i + 1) // 2
                at = slice(pair * S, (pair + 1) * S)
                put(at, 3 * C * ((i + 1) % 2), m[i * S : (i + 1) * S], S)

        for b in range(S // 8):
            res = conv_block(b * 256, b * 256 + S)
            for i in range(4):
                for o in range(2):
                    at = b * 512 + (2 * i + o) * S
                    out_ref[at : at + S] = res[i * S : (i + 1) * S, o * C : (o + 1) * C]

    @pl.when(is_root)
    def _():
        rows[ROWS] = mine[...]

        @pl.when(jnp.logical_not(has_before))
        def _():
            rows[0] = jnp.zeros((GW, C), BF)

        @pl.when(jnp.logical_not(has_after))
        def _():
            rows[ROWS + 1] = jnp.zeros((GW, C), BF)

        def wait(i):
            rc(mine, rows.at[i], m_s.at[0], m_r.at[i], (br, t)).wait_recv()

        here = set()
        done = set()
        for i in (16, 15, 7, 8, 9, 10, 5, 6, 11, 12, 3, 4, 13, 14, 0, 17, 1, 2):
            if i == 0:
                pl.when(has_before)(functools.partial(wait, 0))
            elif i == ROWS + 1:
                pl.when(has_after)(functools.partial(wait, ROWS + 1))
            elif i != ROWS:
                wait(i)
            put(slice(i // 2 * GW, (i // 2 + 1) * GW), 3 * C * (i % 2), rows[i].astype(F32), GW)
            here.add(i)
            for q in range(8):
                if q not in done and here >= {2 * q, 2 * q + 1, 2 * q + 2, 2 * q + 3}:
                    done.add(q)
                    res = conv_block(q * GW, (q + 1) * GW)
                    for o in range(2):
                        at = slice((2 * q + o) * GW, (2 * q + o + 1) * GW)
                        out_ref[at] = res[:, o * C : (o + 1) * C]

    pl.when(is_local)(lambda: merged_copy().wait_send())
    for b in range(SLOTS):

        @pl.when(br != b)
        def _(b=b):
            crop_copy(b).wait_send()

    pl.when(first_up)(lambda: edge_up().wait_send())
    pl.when(root_down)(lambda: edge_down().wait_send())


def run(n, features, merge_local, conv_local, merge_global, conv_global, offsets, sizes, owners):
    hbm = pl.BlockSpec(memory_space=pltpu.HBM)
    dma = pltpu.SemaphoreType.DMA

    def vm(*shape):
        return pltpu.VMEM(shape, BF)

    def sm(*shape):
        return pltpu.SMEM(shape, jnp.int32)

    tiles = n * n
    out = pl.pallas_call(
        functools.partial(kernel, n),
        out_shape=pltpu.VMEM((CELLS, C), BF),
        in_specs=[hbm] * 8,
        out_specs=pl.BlockSpec(memory_space=pltpu.VMEM),
        scratch_shapes=[
            vm(CELLS, C),
            vm(2 * C, C),
            vm(2 * C, C),
            vm(3, 3, C, C),
            sm(SLOTS, 2, tiles),
            sm(SLOTS, 2, tiles),
            sm(SLOTS, 1, tiles),
            vm(ROWS, WIN, C),
            vm(n, ROWS, WIN, C),
            vm(n, GW, C),
            vm(n * SLOTS * WIN, n * GW),
            vm(n, n, GW, GW),
            vm(n, SLOTS, WIN, C),
            vm(n, SLOTS, WIN, C),
            vm(n, GW, C),
            vm(n, GW, C),
            vm(ROWS, WIN, C),
            vm(ROWS, WIN, C),
            vm(ROWS + 2, GW, C),
            vm(GW, C),
            vm(ROWS, S, C),
            vm(9 * GW, 6 * C),
            vm(6 * C, 2 * C),
            vm(6 * C, 2 * C),
            dma((7,)),
            dma((ROWS,)),
            dma((1,)),
            dma((ROWS,)),
            dma((ROWS,)),
            dma((n,)),
            dma((n,)),
            dma((n,)),
            dma((n,)),
            dma((n,)),
            dma((n,)),
            dma((n,)),
            dma((n,)),
            dma((ROWS,)),
            dma((ROWS,)),
            dma((2,)),
            dma((ROWS + 2,)),
        ],
        compiler_params=pltpu.CompilerParams(
            collective_id=0, has_side_effects=True, vmem_limit_bytes=40 * 1024 * 1024
        ),
        name="glue",
    )(
        *(
            pltpu.with_memory_space_constraint(a, pltpu.HBM)
            for a in (
                features.reshape(CELLS, C),
                merge_local,
                conv_local,
                merge_global,
                conv_global,
                offsets.transpose(0, 2, 3, 1).reshape(SLOTS, 2, tiles),
                sizes.transpose(0, 2, 3, 1).reshape(SLOTS, 2, tiles),
                owners.transpose(0, 2, 1),
            )
        )
    )
    return out.reshape(features.shape)


def solution(mesh):
    n = 1
    while n * n < mesh.shape["tile"]:
        n += 1
    in_specs = (P("branch", "tile", None, None, None), P(), P(), P(), P(), P(), P(), P())
    out_specs = P("branch", "tile", None, None, None)
    return jax.shard_map(
        functools.partial(run, n),
        mesh=mesh,
        in_specs=in_specs,
        out_specs=out_specs,
        check_vma=False,
    )
```
